512 devices in a mesh: gx: 4 (over x), gy: 4 (over y), gz: 32 (over z, core).
Axes of the slice: x: 4, y: 4, z: 16, core: 2. Of those that a mesh axis runs over, the one named last changes fastest.
Arguments:
- populations: float32 [19, 8, 64, 4096], P(None, 'gx', 'gy', 'gz'), may hold values from 0.005 to 0.8, as said below
- porosity: float32 [8, 64, 4096], P('gx', 'gy', 'gz'), may hold values from 0.05 to 0.45
- solid: int32 [8, 64, 4096], P('gx', 'gy', 'gz'), may hold values 0 or 1
- seed_adjoint: float32 [19, 8, 64, 4096], P(None, 'gx', 'gy', 'gz'), may hold values from -60 to 60
Outputs:
- porosity_grad: float32 [8, 64, 4096], P('gx', 'gy', 'gz')
- initial_adjoint: float32 [19, 8, 64, 4096], P(None, 'gx', 'gy', 'gz')
The draws below stay inside these ranges and needn't reach their ends.
Inputs may be any that keep to these rules, and one draw needn't show every extreme that they name: `populations`: every population is positive.
All inputs are finite; a program needn't handle non-finite values. No bound on the sum of `solid` on one device may be relied on, other than what follows from the above.
Results may differ from the reference program's by a relative error of at most 0.0003.
Values sent between devices are 32-bit elements; how exact they have to be, the bound alone decides.
No kernel may reach another device: no remote copies, remote signals or barrier semaphores. Data moves between devices by JAX's collectives and lax.ppermute only.
A program may use at most 64 MiB of HBM per device.

```python
import jax
import jax.numpy as jnp
from jax import lax

Q = 19
STEPS = 3
NX = 8
NY = 64
NZ = 4096


LATTICE_WEIGHTS = [1.0 / 3.0] + [1.0 / 18.0] * 6 + [1.0 / 36.0] * 12


def draw_populations(key, part):
    key_density = jax.random.fold_in(key, 11)
    key_jitter = jax.random.fold_in(key, 12)
    weight_table = jnp.asarray(LATTICE_WEIGHTS, jnp.float32).reshape(19, 1, 1, 1)
    density = jax.random.uniform(key_density, (NX, NY, NZ), jnp.float32, 0.7, 1.4)
    jitter = jax.random.uniform(key_jitter, (19, NX, NY, NZ), jnp.float32, -0.35, 0.35)
    factor = 1.0 + jitter
    return weight_table * density * factor


def with_ends(entries, rng, least, high):
    longest = entries.shape.index(max(entries.shape))
    spots = []
    for shift in (0, 1):
        where = [jax.random.randint(jax.random.fold_in(rng, axis), (), 0, length) for axis, length in enumerate(entries.shape)]
        where[longest] = (where[longest] + shift) % entries.shape[longest]
        spots.append(tuple(where))
    return entries.at[spots[0]].set(least).at[spots[1]].set(high)


def block_scale(own_key, dims, cuts, low, largest):
    loudness = 1.0
    for axis_at, blocks in cuts:
        heights = jax.random.uniform(jax.random.fold_in(jax.random.fold_in(own_key, 6), axis_at), (blocks,), jnp.float32, low / len(cuts), largest / len(cuts))
        loudness = loudness * jnp.repeat(jnp.exp(heights), dims[axis_at] // blocks).reshape((-1,) + (1,) * (len(dims) - 1 - axis_at))
    return loudness


def normal_values(own_key, dims, deviation, limit, split=(), kind=jnp.bfloat16):
    array = jax.random.normal(own_key, dims, jnp.float32) * deviation
    if len(split) > 0:
        array = block_scale(own_key, dims, split, -0.22, 0.18) * array
    return jnp.clip(array, min=-limit, max=limit).astype(kind)


def setup_inputs(seed: int = 0) -> dict:
    seeds = jax.random.split(jax.random.key(seed), 5)
    populations = draw_populations(jax.random.fold_in(seeds[4], 71), 0)
    porosity = jnp.clip(0.05 + 0.39999999 * jax.random.uniform(seeds[1], (NX, NY, NZ), jnp.float32) ** block_scale(seeds[1], (NX, NY, NZ), ((0, 4), (1, 4), (2, 32)), -0.2, 0.2), 0.05, 0.45)
    solid = with_ends((jax.random.randint(seeds[2], (NX, NY, NZ), 0, 8) < 1).astype(jnp.int32), jax.random.fold_in(seeds[2], 1), 0, 1)
    seed_adjoint = normal_values(seeds[3], (Q, NX, NY, NZ), 10.0, 60.0, ((1, 4), (2, 4), (3, 32)), jnp.float32)
    return {"populations": populations, "porosity": porosity, "solid": solid, "seed_adjoint": seed_adjoint}


VELOCITIES = [[0, 0, 0], [1, 0, 0], [-1, 0, 0], [0, 1, 0], [0, -1, 0], [0, 0, 1], [0, 0, -1], [1, 1, 0], [-1, -1, 0], [1, -1, 0], [-1, 1, 0], [1, 0, 1], [-1, 0, -1], [1, 0, -1], [-1, 0, 1], [0, 1, 1], [0, -1, -1], [0, 1, -1], [0, -1, 1]]
OPPOSITE = [0, 2, 1, 4, 3, 6, 5, 8, 7, 10, 9, 12, 11, 14, 13, 16, 15, 18, 17]
LATTICE_WEIGHTS = [1.0 / 3.0] + [1.0 / 18.0] * 6 + [1.0 / 36.0] * 12
OMEGA = 1.25

def relax_collision(field, porosity, solid):
    dtype = field.dtype
    vel_table = jnp.asarray(VELOCITIES, dtype=dtype)
    weight_table = jnp.asarray(LATTICE_WEIGHTS, dtype=dtype).reshape(19, 1, 1, 1)
    density = lax.optimization_barrier(jnp.sum(field, axis=0))
    momentum = jnp.tensordot(vel_table.T, field, axes=1, precision=lax.Precision.HIGHEST)
    velocity = momentum / density
    projected = jnp.tensordot(vel_table, velocity, axes=1, precision=lax.Precision.HIGHEST)
    speed_sq = lax.optimization_barrier(jnp.sum(velocity * velocity, axis=0))
    equilibrium = weight_table * density * (1.0 + 3.0 * projected + 4.5 * projected * projected - 1.5 * speed_sq)
    relaxed = field - OMEGA * (field - equilibrium)
    bounced = jnp.stack([field[index] for index in OPPOSITE])
    blocking = jnp.where(solid == 1, jnp.ones_like(porosity), porosity)
    return (1.0 - blocking) * relaxed + blocking * bounced

def translate(field, sign):
    return jnp.stack([jnp.roll(field[index], (sign * vel[0], sign * vel[1], sign * vel[2]), axis=(0, 1, 2)) for index, vel in enumerate(VELOCITIES)])

def reference(populations, porosity, solid, seed_adjoint):
    state_history = [populations]
    current = populations
    for lattice_update in range(STEPS):
        current = translate(relax_collision(current, porosity, solid), 1)
        state_history.append(current)
    adjoint = seed_adjoint
    gradient = jnp.zeros_like(porosity)
    for lattice_update in range(STEPS - 1, -1, -1):
        pulled = translate(adjoint, -1)
        unused_value, backward_pullback = jax.vjp(lambda flow_field, porosity_field: relax_collision(flow_field, porosity_field, solid), state_history[lattice_update], porosity)
        adjoint, grad_part = backward_pullback(pulled)
        gradient = gradient + grad_part
    return (gradient, adjoint)
```

```python
import jax
import jax.numpy as jnp
from jax import lax
from jax.experimental import pallas as pl
from jax.experimental.pallas import tpu as pltpu
from jax.sharding import PartitionSpec as P

INTERPRET = False

VEL = [
    (0, 0, 0),
    (1, 0, 0), (-1, 0, 0), (0, 1, 0), (0, -1, 0), (0, 0, 1), (0, 0, -1),
    (1, 1, 0), (-1, -1, 0), (1, -1, 0), (-1, 1, 0),
    (1, 0, 1), (-1, 0, -1), (1, 0, -1), (-1, 0, 1),
    (0, 1, 1), (0, -1, -1), (0, 1, -1), (0, -1, 1),
]
OPP = [0, 2, 1, 4, 3, 6, 5, 8, 7, 10, 9, 12, 11, 14, 13, 16, 15, 18, 17]
WEIGHT = [1.0 / 3.0] + [1.0 / 18.0] * 6 + [1.0 / 36.0] * 12
OMEGA = 1.25
Q = 19
XP = [i for i in range(Q) if VEL[i][0] == 1]
X0 = [i for i in range(Q) if VEL[i][0] == 0]
XM = [i for i in range(Q) if VEL[i][0] == -1]
PAIRS = [i for i in range(1, Q, 2)]

ROWS, OWN, LANES, RIM = 24, 16, 128, 4
FIELDS = 2 * Q + 1
ZTILES = -(-2 * FIELDS // 32)


def total(terms):
    terms = list(terms)
    while len(terms) > 1:
        terms = [a + b for a, b in zip(terms[::2], terms[1::2])] + (terms[-1:] if len(terms) % 2 else [])
    return terms[0]


def signed(values, axis):
    plus = total(values[i] for i in range(Q) if VEL[i][axis] == 1)
    minus = total(values[i] for i in range(Q) if VEL[i][axis] == -1)
    return plus - minus


def project(vector, i):
    out = None
    for axis in range(3):
        c = VEL[i][axis]
        if c == 0:
            continue
        if out is None:
            out = vector[axis] if c == 1 else -vector[axis]
        else:
            out = out + vector[axis] if c == 1 else out - vector[axis]
    return out


def moments(f):
    rho = total(f)
    inv = 1.0 / rho
    return rho, [signed(f, axis) * inv for axis in range(3)]


def collide(f, rho, u, blocking, want):
    keep = 1.0 - blocking
    own = (1.0 - OMEGA) * keep
    scale = OMEGA * keep * rho
    base = 1.0 - 1.5 * (u[0] * u[0] + u[1] * u[1] + u[2] * u[2])
    out = {}
    if 0 in want:
        out[0] = (own + blocking) * f[0] + (WEIGHT[0] * scale) * base
    for i in PAIRS:
        j = i + 1
        if i not in want and j not in want:
            continue
        s = WEIGHT[i] * scale
        p = project(u, i)
        even = s * (base + 4.5 * (p * p))
        odd = s * (3.0 * p)
        if i in want:
            out[i] = own * f[i] + blocking * f[j] + (even + odd)
        if j in want:
            out[j] = own * f[j] + blocking * f[i] + (even - odd)
    return out


def adjoint(b, u, blocking, want, f=None, rho=None):
    keep = 1.0 - blocking
    own = (1.0 - OMEGA) * keep
    mix = OMEGA * keep
    base = 1.0 - 1.5 * (u[0] * u[0] + u[1] * u[1] + u[2] * u[2])
    sums = {i: b[i] + b[i + 1] for i in PAIRS}
    diffs = {i: b[i] - b[i + 1] for i in PAIRS}
    weighted = total(
        [WEIGHT[0] * b[0], WEIGHT[1] * total(sums[i] for i in PAIRS[:3]), WEIGHT[7] * total(sums[i] for i in PAIRS[3:])]
    )
    value = []
    slope = [[], [], []]
    for i in PAIRS:
        p = project(u, i)
        ps = p * sums[i]
        d3 = 3.0 * diffs[i]
        value.append((WEIGHT[i] * p) * (d3 + 4.5 * ps))
        g = WEIGHT[i] * (d3 + 9.0 * ps)
        for axis in range(3):
            if VEL[i][axis]:
                slope[axis].append(g if VEL[i][axis] == 1 else -g)
    energy = base * weighted + total(value)
    v = [total(slope[axis]) - 3.0 * (u[axis] * weighted) for axis in range(3)]
    common = mix * (energy - (v[0] * u[0] + v[1] * u[1] + v[2] * u[2]))
    mv = [mix * v[axis] for axis in range(3)]
    out = {}
    if 0 in want:
        out[0] = (own + blocking) * b[0] + common
    for i in PAIRS:
        j = i + 1
        if i not in want and j not in want:
            continue
        p = project(mv, i)
        if i in want:
            out[i] = own * b[i] + blocking * b[j] + (common + p)
        if j in want:
            out[j] = own * b[j] + blocking * b[i] + (common - p)
    if f is None:
        return out
    part = total(b[i] * (f[OPP[i]] - (1.0 - OMEGA) * f[i]) for i in range(Q))
    return out, part - (OMEGA * rho) * energy


def column(shape):
    return lax.broadcasted_iota(jnp.int32, shape, len(shape) - 1)


def turn(tile, shift, axis):
    shift = shift % tile.shape[axis]
    return tile if shift == 0 else pltpu.roll(tile, shift, axis)


def moved(main, rim, i, sign):
    y, z = sign * VEL[i][1], sign * VEL[i][2]
    if y:
        main, rim = turn(main, y, 0), turn(rim, y, 0)
    if z:
        at = column(main.shape)
        edge = at == (0 if z == 1 else LANES - 1)
        main, rim = turn(main, z, 1), turn(rim, z, 1)
        main, rim = jnp.where(edge, rim, main), jnp.where(edge, main, rim)
    return main, rim


def pack(ref, tiles):
    n = len(tiles)
    at = column((ROWS, LANES)) // 8
    for k, (main, _) in enumerate(tiles):
        ref[k] = main()
    for first in range(0, n, 16):
        joined = None
        for k in range(first, min(first + 16, n)):
            piece = turn(tiles[k][1](), 8 * (k - first) + 4, 1)
            joined = piece if joined is None else jnp.where(at == k - first, piece, joined)
        ref[n + first // 16] = joined


def unpack(ref, n, k):
    return ref[k], turn(ref[n + k // 16], -(8 * (k % 16) + 4), 1)


def packed(n):
    return n + -(-n // 16)


UP1 = [("g", 0, i) for i in XP] + [("g", 1, i) for i in XP] + [("g", 1, i) for i in X0] + [("s", 1, i) for i in XM] + [("b", 1, 0)]
DOWN1 = [("g", 1, i) for i in XM] + [("g", 0, i) for i in XM] + [("g", 0, i) for i in X0] + [("s", 0, i) for i in XP] + [("b", 0, 0)]
UP2 = [("a", 0, i) for i in XM] + [("a", 1, i) for i in X0] + [("a", 1, i) for i in XM]
DOWN2 = [("a", 1, i) for i in XP] + [("a", 0, i) for i in X0] + [("a", 0, i) for i in XP]
FROM1 = {(kind, layer - 2, i): ("l", k) for k, (kind, layer, i) in enumerate(UP1)}
FROM1.update({(kind, layer + 2, i): ("r", k) for k, (kind, layer, i) in enumerate(DOWN1)})
FROM2 = {(kind, layer - 2, i): ("l", k) for k, (kind, layer, i) in enumerate(UP2)}
FROM2.update({(kind, layer + 2, i): ("r", k) for k, (kind, layer, i) in enumerate(DOWN2)})


def call(kernel, outs, scratch=()):
    return pl.pallas_call(
        kernel,
        out_shape=[jax.ShapeDtypeStruct(shape, jnp.float32) for shape in outs],
        scratch_shapes=[pltpu.VMEM(shape, jnp.float32) for shape in scratch],
        compiler_params=None if INTERPRET else pltpu.CompilerParams(vmem_limit_bytes=40 * 2**20),
        interpret=INTERPRET,
    )


def rows_kernel(f_ref, por_ref, solid_ref, seed_ref, up_ref, down_ref):
    for k in range(FIELDS):
        for layer in range(2):
            if k < Q:
                low, high = f_ref[k, layer, 0:4, :], f_ref[k, layer, 12:16, :]
            elif k < 2 * Q:
                low, high = seed_ref[k - Q, layer, 0:4, :], seed_ref[k - Q, layer, 12:16, :]
            else:
                blocking = jnp.where(solid_ref[layer] == 1, 1.0, por_ref[layer])
                low, high = blocking[0:4], blocking[12:16]
            up_ref[k, 4 * layer : 4 * layer + 4, :] = high
            down_ref[k, 4 * layer : 4 * layer + 4, :] = low


def columns_kernel(f_ref, por_ref, solid_ref, seed_ref, below_ref, above_ref, main_ref, up_ref, down_ref):
    at = column((ROWS, LANES)) // 4
    high = low = None
    for k in range(FIELDS):
        for layer in range(2):
            if k < Q:
                own = f_ref[k, layer]
            elif k < 2 * Q:
                own = seed_ref[k - Q, layer]
            else:
                own = jnp.where(solid_ref[layer] == 1, 1.0, por_ref[layer])
            rows = slice(4 * layer, 4 * layer + 4)
            tile = jnp.concatenate([own, above_ref[k, rows, :], below_ref[k, rows, :]], axis=0)
            main_ref[k, layer] = tile
            slot = (2 * k + layer) % 32
            piece_up, piece_down = turn(tile, 4 * slot + 4, 1), turn(tile, 4 * slot, 1)
            high = piece_up if slot == 0 else jnp.where(at == slot, piece_up, high)
            low = piece_down if slot == 0 else jnp.where(at == slot, piece_down, low)
            if slot == 31 or 2 * k + layer == 2 * FIELDS - 1:
                up_ref[(2 * k + layer) // 32] = high
                down_ref[(2 * k + layer) // 32] = low


def tiles_loop(count, body):
    def step(n, carry):
        body(n // 3, pl.multiple_of((n % 3) * 8, 8))
        return carry

    lax.fori_loop(0, count, step, 0)


def first_kernel(main_ref, before_ref, beyond_ref, g_ref, s_ref, b_ref, up_ref, down_ref, f_scr):
    at = column((ROWS, LANES))
    for k in range(FIELDS):
        for layer in range(2):
            n = 2 * k + layer
            slot, tile = n % 32, n // 32
            before = turn(before_ref[tile], -(4 * slot + 4), 1)
            beyond = turn(beyond_ref[tile], -4 * slot, 1)
            rim = jnp.where(at < RIM, beyond, before)
            if k < Q:
                f_scr[k, layer, 0] = main_ref[k, layer]
                f_scr[k, layer, 1] = rim
            elif k < 2 * Q:
                s_ref[k - Q, layer, 0] = main_ref[k, layer]
                s_ref[k - Q, layer, 1] = rim
            else:
                b_ref[layer, 0] = main_ref[k, layer]
                b_ref[layer, 1] = rim

    for layer in range(2):

        def body(lane, row, layer=layer):
            f = [f_scr[i, layer, lane, pl.ds(row, 8), :] for i in range(Q)]
            rho, u = moments(f)
            g = collide(f, rho, u, b_ref[layer, lane, pl.ds(row, 8), :], range(Q))
            for i in range(Q):
                g_ref[i, layer, lane, pl.ds(row, 8), :] = g[i]

        tiles_loop(6, body)

    def tile(field):
        kind, layer, i = field
        if kind == "g":
            return (lambda: g_ref[i, layer, 0]), (lambda: g_ref[i, layer, 1])
        if kind == "s":
            return (lambda: s_ref[i, layer, 0]), (lambda: s_ref[i, layer, 1])
        return (lambda: b_ref[layer, 0]), (lambda: b_ref[layer, 1])

    pack(up_ref, [tile(field) for field in UP1])
    pack(down_ref, [tile(field) for field in DOWN1])


def middle_kernel(
    g_ref, s_ref, b_ref, left_ref, right_ref,
    a_ref, u_ref, b4_ref, f1_ref, grad_ref, up_ref, down_ref,
    f_scr, g_scr, adj_scr,
):
    def got(kind, x, i):
        if x in (0, 1):
            ref = {"g": g_ref, "s": s_ref}[kind]
            return ref[i, x, 0], ref[i, x, 1]
        side, k = FROM1[(kind, x, i)]
        return unpack(left_ref, len(UP1), k) if side == "l" else unpack(right_ref, len(DOWN1), k)

    for i in range(Q):
        for n in range(4):
            main, rim = moved(*got("g", n - 1 - VEL[i][0], i), i, 1)
            f_scr[i, n, 0] = main
            f_scr[i, n, 1] = rim
            if n in (1, 2):
                f1_ref[i, n - 1] = main[0:OWN]
    for n in range(4):
        if n in (1, 2):
            b4_ref[n, 0] = b_ref[n - 1, 0]
            b4_ref[n, 1] = b_ref[n - 1, 1]
        else:
            main, rim = got("b", n - 1, 0)
            b4_ref[n, 0] = main
            b4_ref[n, 1] = rim

    for n, want in ((0, XP), (1, range(Q)), (2, range(Q)), (3, XM)):

        def body(lane, row, n=n, want=want):
            f = [f_scr[i, n, lane, pl.ds(row, 8), :] for i in range(Q)]
            rho, u = moments(f)
            for axis in range(3):
                u_ref[axis, n, lane, pl.ds(row, 8), :] = u[axis]
            g = collide(f, rho, u, b4_ref[n, lane, pl.ds(row, 8), :], want)
            for i in want:
                g_scr[i, n, lane, pl.ds(row, 8), :] = g[i]

        tiles_loop(6, body)

    for i in range(Q):
        for layer in range(2):
            n = layer + 1 - VEL[i][0]
            main, rim = moved(g_scr[i, n, 0], g_scr[i, n, 1], i, 1)
            f_scr[i, layer, 0] = main
            f_scr[i, layer, 1] = rim
            main, rim = moved(*got("s", layer + VEL[i][0], i), i, -1)
            adj_scr[i, layer, 0] = main
            adj_scr[i, layer, 1] = rim

    for layer in range(2):

        def body(lane, row, layer=layer, first=0):
            f = [f_scr[i, layer, lane, pl.ds(row, 8), :] for i in range(Q)]
            b = [adj_scr[i, layer, lane, pl.ds(row, 8), :] for i in range(Q)]
            rho, u = moments(f)
            a, grad = adjoint(b, u, b_ref[layer, lane, pl.ds(row, 8), :], range(Q), f, rho)
            for i in range(Q):
                a_ref[i, layer, lane, pl.ds(row, 8), :] = a[i]
            grad_ref[layer, lane, pl.ds(row, 8), :] = grad

        tiles_loop(6, body)

    def tile(field):
        _, layer, i = field
        return (lambda: a_ref[i, layer, 0]), (lambda: a_ref[i, layer, 1])

    pack(up_ref, [tile(field) for field in UP2])
    pack(down_ref, [tile(field) for field in DOWN2])


def last_kernel(
    a_ref, u_ref, b4_ref, f1_ref, grad_ref, left_ref, right_ref, f_ref, solid_ref,
    out_grad_ref, out_ref,
    b_scr, a_scr,
):
    def got(x, i):
        if x in (0, 1):
            return a_ref[i, x, 0], a_ref[i, x, 1]
        side, k = FROM2[("a", x, i)]
        return unpack(left_ref, len(UP2), k) if side == "l" else unpack(right_ref, len(DOWN2), k)

    for i in range(Q):
        for n in range(4):
            main, rim = moved(*got(n - 1 + VEL[i][0], i), i, -1)
            b_scr[i, n, 0] = main
            b_scr[i, n, 1] = rim

    for n, want in ((0, XM), (1, range(Q)), (2, range(Q)), (3, XP)):

        def body(lane, row, n=n, want=want):
            b = [b_scr[i, n, lane, pl.ds(row, 8), :] for i in range(Q)]
            u = [u_ref[axis, n, lane, pl.ds(row, 8), :] for axis in range(3)]
            a = adjoint(b, u, b4_ref[n, lane, pl.ds(row, 8), :], want)
            for i in want:
                a_scr[i, n, lane, pl.ds(row, 8), :] = a[i]

        tiles_loop(6, body)

    def own(n, carry):
        layer, row = n // 2, pl.multiple_of((n % 2) * 8, 8)
        f = [f1_ref[i, layer, pl.ds(row, 8), :] for i in range(Q)]
        b = [b_scr[i, layer + 1, 0, pl.ds(row, 8), :] for i in range(Q)]
        rho, u = moments(f)
        _, grad = adjoint(b, u, b4_ref[layer + 1, 0, pl.ds(row, 8), :], (), f, rho)
        out_grad_ref[layer, pl.ds(row, 8), :] = grad + grad_ref[layer, 0, pl.ds(row, 8), :]
        return carry

    lax.fori_loop(0, 4, own, 0)

    for i in range(Q):
        for layer in range(2):
            n = layer + 1 + VEL[i][0]
            main, _ = moved(a_scr[i, n, 0], a_scr[i, n, 1], i, -1)
            b_scr[i, layer, 0] = main

    def final(n, carry):
        layer, row = n // 2, pl.multiple_of((n % 2) * 8, 8)
        f = [f_ref[i, layer, pl.ds(row, 8), :] for i in range(Q)]
        b = [b_scr[i, layer, 0, pl.ds(row, 8), :] for i in range(Q)]
        rho, u = moments(f)
        a, grad = adjoint(b, u, b4_ref[layer + 1, 0, pl.ds(row, 8), :], range(Q), f, rho)
        for i in range(Q):
            out_ref[i, layer, pl.ds(row, 8), :] = a[i]
        grad = grad + out_grad_ref[layer, pl.ds(row, 8), :]
        out_grad_ref[layer, pl.ds(row, 8), :] = jnp.where(solid_ref[layer, pl.ds(row, 8), :] == 1, 0.0, grad)
        return carry

    lax.fori_loop(0, 4, final, 0)


def both_ways(up, down, axis):
    count = lax.axis_size(axis)
    ring = [(i, (i + 1) % count) for i in range(count)]
    return lax.ppermute(up, axis, ring), lax.ppermute(down, axis, [(j, i) for i, j in ring])


def body(populations, porosity, solid, seed_adjoint):
    layer = (2, 2, ROWS, LANES)
    inputs = (populations, porosity, solid, seed_adjoint)
    up, down = call(rows_kernel, [(FIELDS, 8, LANES)] * 2)(*inputs)
    below, above = both_ways(up, down, "gy")
    main, up, down = call(columns_kernel, [(FIELDS, 2, ROWS, LANES)] + [(ZTILES, ROWS, LANES)] * 2)(*inputs, below, above)
    before, beyond = both_ways(up, down, "gz")
    g, s, b, up, down = call(
        first_kernel,
        [(Q,) + layer, (Q,) + layer, layer] + [(packed(len(UP1)), ROWS, LANES)] * 2,
        [(Q,) + layer],
    )(main, before, beyond)
    left, right = both_ways(up, down, "gx")
    wide = (4, 2, ROWS, LANES)
    a, u, b4, f1, grad, up, down = call(
        middle_kernel,
        [(Q,) + layer, (3,) + wide, wide, (Q, 2, OWN, LANES), layer] + [(packed(len(UP2)), ROWS, LANES)] * 2,
        [(Q,) + wide, (Q,) + wide, (Q,) + layer],
    )(g, s, b, left, right)
    left, right = both_ways(up, down, "gx")
    gradient, adjoint_out = call(
        last_kernel, [(2, OWN, LANES), (Q, 2, OWN, LANES)], [(Q,) + wide, (Q,) + wide]
    )(a, u, b4, f1, grad, left, right, populations, solid)
    return gradient, adjoint_out


def solution(mesh):
    field, cell = P(None, "gx", "gy", "gz"), P("gx", "gy", "gz")
    return jax.shard_map(
        body, mesh=mesh, in_specs=(field, cell, cell, field), out_specs=(cell, field), check_vma=False
    )
```

```python
import jax
import jax.numpy as jnp
from jax import lax
from jax.experimental import pallas as pl
from jax.experimental.pallas import tpu as pltpu
from jax.sharding import PartitionSpec as P

INTERPRET = False

VEL = [
    (0, 0, 0),
    (1, 0, 0), (-1, 0, 0), (0, 1, 0), (0, -1, 0), (0, 0, 1), (0, 0, -1),
    (1, 1, 0), (-1, -1, 0), (1, -1, 0), (-1, 1, 0),
    (1, 0, 1), (-1, 0, -1), (1, 0, -1), (-1, 0, 1),
    (0, 1, 1), (0, -1, -1), (0, 1, -1), (0, -1, 1),
]
OPP = [0, 2, 1, 4, 3, 6, 5, 8, 7, 10, 9, 12, 11, 14, 13, 16, 15, 18, 17]
WEIGHT = [1.0 / 3.0] + [1.0 / 18.0] * 6 + [1.0 / 36.0] * 12
OMEGA = 1.25
Q = 19
XP = [i for i in range(Q) if VEL[i][0] == 1]
X0 = [i for i in range(Q) if VEL[i][0] == 0]
XM = [i for i in range(Q) if VEL[i][0] == -1]
PAIRS = [i for i in range(1, Q, 2)]

ROWS, OWN, LANES, RIM = 24, 16, 128, 4
FIELDS = 2 * Q + 1
ZTILES = -(-2 * FIELDS // 32)


def total(terms):
    terms = list(terms)
    while len(terms) > 1:
        terms = [a + b for a, b in zip(terms[::2], terms[1::2])] + (terms[-1:] if len(terms) % 2 else [])
    return terms[0]


def signed(values, axis):
    plus = total(values[i] for i in range(Q) if VEL[i][axis] == 1)
    minus = total(values[i] for i in range(Q) if VEL[i][axis] == -1)
    return plus - minus


def project(vector, i):
    out = None
    for axis in range(3):
        c = VEL[i][axis]
        if c == 0:
            continue
        if out is None:
            out = vector[axis] if c == 1 else -vector[axis]
        else:
            out = out + vector[axis] if c == 1 else out - vector[axis]
    return out


def moments(f):
    rho = total(f)
    inv = 1.0 / rho
    return rho, [signed(f, axis) * inv for axis in range(3)]


def moments_from(level, f):
    plus, minus = total(f[i] for i in XP), total(f[i] for i in XM)
    rho = level[0] + (plus + minus)
    inv = 1.0 / rho
    along = [level[axis] + total(f[i] if VEL[i][axis] == 1 else -f[i] for i in XP + XM if VEL[i][axis]) for axis in (1, 2)]
    return rho, [(plus - minus) * inv, along[0] * inv, along[1] * inv]


def collide(f, rho, u, blocking, want):
    keep = 1.0 - blocking
    own = (1.0 - OMEGA) * keep
    scale = OMEGA * keep * rho
    base = 1.0 - 1.5 * (u[0] * u[0] + u[1] * u[1] + u[2] * u[2])
    out = {}
    if 0 in want:
        out[0] = (own + blocking) * f[0] + (WEIGHT[0] * scale) * base
    for i in PAIRS:
        j = i + 1
        if i not in want and j not in want:
            continue
        s = WEIGHT[i] * scale
        p = project(u, i)
        even = s * (base + 4.5 * (p * p))
        odd = s * (3.0 * p)
        if i in want:
            out[i] = own * f[i] + blocking * f[j] + (even + odd)
        if j in want:
            out[j] = own * f[j] + blocking * f[i] + (even - odd)
    return out


def flow(b, u):
    base = 1.0 - 1.5 * (u[0] * u[0] + u[1] * u[1] + u[2] * u[2])
    weighted, value, slope = [], [], [[], [], []]
    if 0 in b:
        weighted.append(WEIGHT[0] * b[0])
    faces, edges = [], []
    for i in PAIRS:
        j = i + 1
        if i not in b and j not in b:
            continue
        p = project(u, i)
        if i in b and j in b:
            even, odd = b[i] + b[j], b[i] - b[j]
        elif i in b:
            even, odd = b[i], b[i]
        else:
            even, odd = b[j], -b[j]
        (faces if i < 7 else edges).append(even)
        ps = p * even
        d3 = 3.0 * odd
        value.append((WEIGHT[i] * p) * (d3 + 4.5 * ps))
        g = WEIGHT[i] * (d3 + 9.0 * ps)
        for axis in range(3):
            if VEL[i][axis]:
                slope[axis].append(g if VEL[i][axis] == 1 else -g)
    weighted = total(weighted + [WEIGHT[1] * total(faces), WEIGHT[7] * total(edges)])
    return [base * weighted + total(value)] + [total(slope[axis]) - 3.0 * (u[axis] * weighted) for axis in range(3)]


def back(b, sums, u, blocking, want):
    energy, *v = sums
    keep = 1.0 - blocking
    own = (1.0 - OMEGA) * keep
    mix = OMEGA * keep
    common = mix * (energy - (v[0] * u[0] + v[1] * u[1] + v[2] * u[2]))
    mv = [mix * v[axis] for axis in range(3)]
    out = {}
    if 0 in want:
        out[0] = (own + blocking) * b[0] + common
    for i in PAIRS:
        j = i + 1
        if i not in want and j not in want:
            continue
        p = project(mv, i)
        if i in want:
            out[i] = own * b[i] + blocking * b[j] + (common + p)
        if j in want:
            out[j] = own * b[j] + blocking * b[i] + (common - p)
    return out


def gradient_of(b, f, rho, energy):
    return total(b[i] * (f[OPP[i]] - (1.0 - OMEGA) * f[i]) for i in range(Q)) - (OMEGA * rho) * energy


def column(shape):
    return lax.broadcasted_iota(jnp.int32, shape, len(shape) - 1)


def turn(tile, shift, axis):
    shift = shift % tile.shape[axis]
    return tile if shift == 0 else pltpu.roll(tile, shift, axis)


def moved(main, rim, i, sign):
    y, z = sign * VEL[i][1], sign * VEL[i][2]
    if y:
        main, rim = turn(main, y, 0), turn(rim, y, 0)
    if z:
        at = column(main.shape)
        edge = at == (0 if z == 1 else LANES - 1)
        main, rim = turn(main, z, 1), turn(rim, z, 1)
        main, rim = jnp.where(edge, rim, main), jnp.where(edge, main, rim)
    return main, rim


def pack(ref, tiles):
    n = len(tiles)
    at = column((ROWS, LANES)) // 8
    for k, (main, _) in enumerate(tiles):
        ref[k] = main()
    for first in range(0, n, 16):
        joined = None
        for k in range(first, min(first + 16, n)):
            piece = turn(tiles[k][1](), 8 * (k - first) + 4, 1)
            joined = piece if joined is None else jnp.where(at == k - first, piece, joined)
        ref[n + first // 16] = joined


def unpack(ref, n, k):
    return ref[k], turn(ref[n + k // 16], -(8 * (k % 16) + 4), 1)


def packed(n):
    return n + -(-n // 16)


def rims(ref, n, out_ref):
    for k in range(n):
        out_ref[k] = unpack(ref, n, k)[1]


SEND1, SEND2 = 19, 14


def call(kernel, outs, scratch=(), more=(), space=None, cost=1000):
    specs = {} if space is None else {"in_specs": [pl.BlockSpec(memory_space=s) for s in space]}
    return pl.pallas_call(
        kernel,
        out_shape=[jax.ShapeDtypeStruct(shape, jnp.float32) for shape in outs],
        scratch_shapes=[pltpu.VMEM(shape, jnp.float32) for shape in scratch] + list(more),
        compiler_params=None if INTERPRET else pltpu.CompilerParams(vmem_limit_bytes=40 * 2**20),
        cost_estimate=pl.CostEstimate(flops=cost * 2000, bytes_accessed=cost * 1000, transcendentals=0),
        interpret=INTERPRET,
        **specs,
    )


def rows_kernel(f_hbm, por_hbm, solid_hbm, seed_hbm, up_ref, down_ref, f_ref, por_ref, seed_ref, solid_ref, sems):
    copies = [
        pltpu.make_async_copy(src, dst, sems.at[k])
        for k, (src, dst) in enumerate(
            [(f_hbm, f_ref), (seed_hbm, seed_ref), (por_hbm, por_ref), (solid_hbm, solid_ref)]
        )
    ]
    for copy in copies:
        copy.start()

    def send(k, layer, tile):
        up_ref[k, 4 * layer : 4 * layer + 4, :] = tile(12)
        down_ref[k, 4 * layer : 4 * layer + 4, :] = tile(0)

    copies[0].wait()
    for k in range(Q):
        for layer in range(2):
            send(k, layer, lambda row: f_ref[k, layer, row : row + 4, :])
    copies[1].wait()
    for k in range(Q):
        for layer in range(2):
            send(k + Q, layer, lambda row: seed_ref[k, layer, row : row + 4, :])
    copies[2].wait()
    copies[3].wait()
    for layer in range(2):
        send(2 * Q, layer, lambda row: jnp.where(solid_ref[layer, row : row + 4, :] == 1, 1.0, por_ref[layer, row : row + 4, :]))


def columns_kernel(f_ref, por_ref, solid_ref, seed_ref, below_ref, above_ref, main_ref, up_ref, down_ref):
    at = column((ROWS, LANES)) // 4
    high = low = None
    for k in range(FIELDS):
        for layer in range(2):
            if k < Q:
                own = f_ref[k, layer]
            elif k < 2 * Q:
                own = seed_ref[k - Q, layer]
            else:
                own = jnp.where(solid_ref[layer] == 1, 1.0, por_ref[layer])
            rows = slice(4 * layer, 4 * layer + 4)
            tile = jnp.concatenate([own, above_ref[k, rows, :], below_ref[k, rows, :]], axis=0)
            main_ref[k, layer] = tile
            slot = (2 * k + layer) % 32
            piece_up, piece_down = turn(tile, 4 * slot + 4, 1), turn(tile, 4 * slot, 1)
            high = piece_up if slot == 0 else jnp.where(at == slot, piece_up, high)
            low = piece_down if slot == 0 else jnp.where(at == slot, piece_down, low)
            if slot == 31 or 2 * k + layer == 2 * FIELDS - 1:
                up_ref[(2 * k + layer) // 32] = high
                down_ref[(2 * k + layer) // 32] = low


def tiles_loop(count, body):
    def step(n, carry):
        body(n // 3, pl.multiple_of((n % 3) * 8, 8))
        return carry

    lax.fori_loop(0, count, step, 0)


def main_kernel(main_ref, g_ref):
    for layer in range(2):

        def body(_, row, layer=layer):
            f = [main_ref[i, layer, pl.ds(row, 8), :] for i in range(Q)]
            rho, u = moments(f)
            g = collide(f, rho, u, main_ref[2 * Q, layer, pl.ds(row, 8), :], range(Q))
            for i in range(Q):
                g_ref[i, layer, pl.ds(row, 8), :] = g[i]

        tiles_loop(3, body)


def first_kernel(
    main_ref, g_ref, before_ref, beyond_ref,
    f1_ref, edge_ref, level_ref, s_ref, b_ref, up_ref, down_ref,
    f_scr, g_scr,
):
    at = column((ROWS, LANES))
    for k in range(FIELDS):
        for layer in range(2):
            n = 2 * k + layer
            slot, tile = n % 32, n // 32
            before = turn(before_ref[tile], -(4 * slot + 4), 1)
            beyond = turn(beyond_ref[tile], -4 * slot, 1)
            rim = jnp.where(at < RIM, beyond, before)
            if k < Q:
                f_scr[k, layer] = rim
            elif k < 2 * Q:
                s_ref[k - Q, layer] = rim
            else:
                b_ref[layer, 0] = main_ref[k, layer]
                b_ref[layer, 1] = rim

    for layer in range(2):

        def body(_, row, layer=layer):
            f = [f_scr[i, layer, pl.ds(row, 8), :] for i in range(Q)]
            rho, u = moments(f)
            g = collide(f, rho, u, b_ref[layer, 1, pl.ds(row, 8), :], range(Q))
            for i in range(Q):
                g_scr[i, layer, pl.ds(row, 8), :] = g[i]

        tiles_loop(3, body)

    for i in range(Q):
        for layer in range(2):
            to = layer + VEL[i][0]
            tiles = moved(g_ref[i, layer], g_scr[i, layer], i, 1)
            for lane in range(2):
                if to in (0, 1):
                    f1_ref[i, to, lane] = tiles[lane]
                else:
                    edge_ref[i, lane] = tiles[lane]
    for layer in range(2):
        for lane in range(2):
            stay = {i: f1_ref[i, layer, lane] for i in X0}
            level_ref[0, layer, lane] = total(stay.values())
            for axis in (1, 2):
                level_ref[axis, layer, lane] = total(
                    stay[i] if VEL[i][axis] == 1 else -stay[i] for i in X0 if VEL[i][axis]
                )

    def tiles_of(forward, backward, layer):
        def pick(ref, *where):
            return (lambda: ref[where + (0,)]), (lambda: ref[where + (1,)])

        out = [pick(f1_ref, i, layer) for i in forward]
        out += [pick(level_ref, k, layer) for k in range(3)]
        out.append(pick(b_ref, layer))
        out += [pick(edge_ref, i) for i in forward]
        for i in backward:
            pair = moved(main_ref[Q + i, layer], s_ref[i, layer], i, -1)
            out.append(((lambda pair=pair: pair[0]), (lambda pair=pair: pair[1])))
        return out

    pack(up_ref, tiles_of(XP, XM, 1))
    pack(down_ref, tiles_of(XM, XP, 0))


def seed_kernel(main_ref, s_ref, b2_ref):
    for i in range(Q):
        for layer in range(2):
            to = layer - VEL[i][0]
            if to in (0, 1):
                main, rim = moved(main_ref[Q + i, layer], s_ref[i, layer], i, -1)
                b2_ref[i, to, 0] = main
                b2_ref[i, to, 1] = rim


def middle_kernel(
    f1_ref, edge_ref, level_ref, b_ref, b2_ref, left_ref, right_ref,
    mom_ref, bh_ref, grad_ref, b1_ref, edge1_ref, sums_ref, up_ref, down_ref,
    l_scr, r_scr, g_scr, f_scr, a_scr,
):
    rims(left_ref, SEND1, l_scr)
    rims(right_ref, SEND1, r_scr)
    got = ((left_ref, right_ref), (l_scr, r_scr))
    for side in range(2):
        for lane in range(2):
            bh_ref[side, lane] = got[lane][side][8]

    for layer in range(2):
        for lane in range(2):

            def body(_, row, layer=layer, lane=lane):
                rows = pl.ds(row, 8)
                missing = XP if layer == 0 else XM
                f = [None if i in missing else f1_ref[i, layer, lane, rows, :] for i in range(Q)]
                for k, i in enumerate(missing):
                    f[i] = got[lane][layer][9 + k, rows, :]
                rho, u = moments_from([level_ref[k, layer, lane, rows, :] for k in range(3)], f)
                mom_ref[3, layer + 1, lane, rows, :] = rho
                for axis in range(3):
                    mom_ref[axis, layer + 1, lane, rows, :] = u[axis]
                g = collide(f, rho, u, b_ref[layer, lane, rows, :], range(Q))
                for i in range(Q):
                    g_scr[i, layer + 1, lane, rows, :] = g[i]

            tiles_loop(3, body)

    for side in range(2):
        for lane in range(2):

            def body(_, row, side=side, lane=lane):
                rows = pl.ds(row, 8)
                theirs, ours = (XP, XM) if side == 0 else (XM, XP)
                f = [None] * Q
                for k, i in enumerate(theirs):
                    f[i] = got[lane][side][k, rows, :]
                for i in ours:
                    f[i] = edge_ref[i, lane, rows, :]
                rho, u = moments_from([got[lane][side][5 + k, rows, :] for k in range(3)], f)
                for axis in range(3):
                    mom_ref[axis, 3 * side, lane, rows, :] = u[axis]
                g = collide(f, rho, u, got[lane][side][8, rows, :], theirs)
                for i in theirs:
                    g_scr[i, 3 * side, lane, rows, :] = g[i]

            tiles_loop(3, body)

    for i in range(Q):
        for layer in range(2):
            n = layer + 1 - VEL[i][0]
            main, rim = moved(g_scr[i, n, 0], g_scr[i, n, 1], i, 1)
            f_scr[i, layer, 0] = main
            f_scr[i, layer, 1] = rim

    for layer in range(2):
        for lane in range(2):

            def body(row, layer=layer, lane=lane, own=False):
                rows = pl.ds(row, 8)
                missing = XM if layer == 0 else XP
                f = [f_scr[i, layer, lane, rows, :] for i in range(Q)]
                b = {i: b2_ref[i, layer, lane, rows, :] for i in range(Q) if i not in missing}
                for k, i in enumerate(missing):
                    b[i] = got[lane][layer][14 + k, rows, :]
                rho, u = moments(f)
                sums = flow(b, u)
                a = back(b, sums, u, b_ref[layer, lane, rows, :], range(Q))
                for i in range(Q):
                    a_scr[i, layer, lane, rows, :] = a[i]
                if own:
                    grad_ref[layer, rows, :] = gradient_of(b, f, rho, sums[0])

            if lane == 0:

                def step(n, carry, body=body):
                    body(pl.multiple_of(n * 8, 8), own=True)
                    return carry

                lax.fori_loop(0, 2, step, 0)
                body(16)
            else:
                tiles_loop(3, lambda _, row, body=body: body(row))

    for i in range(Q):
        for layer in range(2):
            to = layer - VEL[i][0]
            tiles = moved(a_scr[i, layer, 0], a_scr[i, layer, 1], i, -1)
            for lane in range(2):
                if to in (0, 1):
                    b1_ref[i, to, lane] = tiles[lane]
                else:
                    edge1_ref[i, lane] = tiles[lane]

    for layer in range(2):
        for lane in range(2):

            def body(_, row, layer=layer, lane=lane):
                rows = pl.ds(row, 8)
                missing = XM if layer == 0 else XP
                b = {i: b1_ref[i, layer, lane, rows, :] for i in range(Q) if i not in missing}
                sums = flow(b, [mom_ref[axis, layer + 1, lane, rows, :] for axis in range(3)])
                for k in range(4):
                    sums_ref[k, layer, lane, rows, :] = sums[k]

            tiles_loop(3, body)

    def tiles_of(theirs, layer):
        def pick(ref, *where):
            return (lambda: ref[where + (0,)]), (lambda: ref[where + (1,)])

        return (
            [pick(edge1_ref, i) for i in theirs]
            + [pick(b1_ref, i, layer) for i in theirs]
            + [pick(sums_ref, k, layer) for k in range(4)]
        )

    pack(up_ref, tiles_of(XM, 1))
    pack(down_ref, tiles_of(XP, 0))


def last_kernel(
    b1_ref, edge1_ref, sums_ref, mom_ref, b_ref, bh_ref, f1_ref, left1_ref, right1_ref, grad_ref, left_ref, right_ref, f_ref, solid_ref,
    out_grad_ref, out_ref,
    l_scr, r_scr, a_scr, b0_scr,
):
    rims(left_ref, SEND2, l_scr)
    rims(right_ref, SEND2, r_scr)
    got = ((left_ref, right_ref), (l_scr, r_scr))
    got1 = (left1_ref, right1_ref)

    for layer in range(2):
        for lane in range(2):

            def body(row, layer=layer, lane=lane, own=False):
                rows = pl.ds(row, 8)
                missing = XM if layer == 0 else XP
                new = {i: got[lane][layer][k, rows, :] for k, i in enumerate(missing)}
                b = {i: b1_ref[i, layer, lane, rows, :] for i in range(Q) if i not in missing}
                b.update(new)
                u = [mom_ref[axis, layer + 1, lane, rows, :] for axis in range(3)]
                sums = [sums_ref[k, layer, lane, rows, :] + part for k, part in enumerate(flow(new, u))]
                a = back(b, sums, u, b_ref[layer, lane, rows, :], range(Q))
                for i in range(Q):
                    a_scr[i, layer + 1, lane, rows, :] = a[i]
                if own:
                    f = {i: f1_ref[i, layer, lane, rows, :] for i in range(Q) if OPP[i] not in missing}
                    for k, i in enumerate(XP if layer == 0 else XM):
                        f[i] = got1[layer][9 + k, rows, :]
                    grad = gradient_of(b, f, mom_ref[3, layer + 1, lane, rows, :], sums[0])
                    out_grad_ref[layer, rows, :] = grad + grad_ref[layer, rows, :]

            if lane == 0:

                def step(n, carry, body=body):
                    body(pl.multiple_of(n * 8, 8), own=True)
                    return carry

                lax.fori_loop(0, 2, step, 0)
                body(16)
            else:
                tiles_loop(3, lambda _, row, body=body: body(row))

    for side in range(2):
        for lane in range(2):

            def body(_, row, side=side, lane=lane):
                rows = pl.ds(row, 8)
                theirs, ours = (XM, XP) if side == 0 else (XP, XM)
                new = {i: edge1_ref[i, lane, rows, :] for i in ours}
                b = dict(new)
                for k, i in enumerate(theirs):
                    b[i] = got[lane][side][5 + k, rows, :]
                u = [mom_ref[axis, 3 * side, lane, rows, :] for axis in range(3)]
                sums = [got[lane][side][10 + k, rows, :] + part for k, part in enumerate(flow(new, u))]
                a = back(b, sums, u, bh_ref[side, lane, rows, :], theirs)
                for i in theirs:
                    a_scr[i, 3 * side, lane, rows, :] = a[i]

            tiles_loop(3, body)

    for i in range(Q):
        for layer in range(2):
            n = layer + 1 + VEL[i][0]
            main, _ = moved(a_scr[i, n, 0], a_scr[i, n, 1], i, -1)
            b0_scr[i, layer] = main[0:OWN]

    for layer in range(2):

        def final(n, carry, layer=layer):
            rows = pl.ds(pl.multiple_of(n * 8, 8), 8)
            f = [f_ref[i, layer, rows, :] for i in range(Q)]
            b = {i: b0_scr[i, layer, rows, :] for i in range(Q)}
            rho, u = moments(f)
            sums = flow(b, u)
            a = back(b, sums, u, b_ref[layer, 0, rows, :], range(Q))
            for i in range(Q):
                out_ref[i, layer, rows, :] = a[i]
            grad = gradient_of(b, f, rho, sums[0]) + out_grad_ref[layer, rows, :]
            out_grad_ref[layer, rows, :] = jnp.where(solid_ref[layer, rows, :] == 1, 0.0, grad)
            return carry

        lax.fori_loop(0, 2, final, 0)


def both_ways(up, down, axis):
    count = lax.axis_size(axis)
    ring = [(i, (i + 1) % count) for i in range(count)]
    return lax.ppermute(up, axis, ring), lax.ppermute(down, axis, [(j, i) for i, j in ring])


def body(populations, porosity, solid, seed_adjoint):
    half, tile = (2, 2, ROWS, LANES), (ROWS, LANES)
    inputs = (populations, porosity, solid, seed_adjoint)
    block = populations.shape
    up, down = call(
        rows_kernel,
        [(FIELDS, 8, LANES)] * 2,
        [block, block[1:], block],
        [pltpu.VMEM(block[1:], jnp.int32), pltpu.SemaphoreType.DMA((4,))],
        space=[pltpu.HBM] * 4,
    )(*inputs)
    below, above = both_ways(up, down, "gy")
    main, up, down = call(columns_kernel, [(FIELDS, 2) + tile] + [(ZTILES,) + tile] * 2)(*inputs, below, above)
    before, beyond = both_ways(up, down, "gz")
    (g,) = call(main_kernel, [(Q, 2) + tile])(main)
    f1, edge, level, s, b, up, down = call(
        first_kernel,
        [(Q,) + half, (Q, 2) + tile, (3,) + half, (Q, 2) + tile, half] + [(packed(SEND1),) + tile] * 2,
        [(Q, 2) + tile] * 2,
    )(main, g, before, beyond)
    left1, right1 = both_ways(up, down, "gx")
    (b2,) = call(seed_kernel, [(Q,) + half])(main, s)
    wide = (4, 2) + tile
    mom, bh, grad, b1, edge1, sums, up, down = call(
        middle_kernel,
        [(4,) + wide, half, (2, OWN, LANES), (Q,) + half, (Q, 2) + tile, (4,) + half] + [(packed(SEND2),) + tile] * 2,
        [(SEND1,) + tile] * 2 + [(Q,) + wide, (Q,) + half, (Q,) + half],
    )(f1, edge, level, b, b2, left1, right1)
    left, right = both_ways(up, down, "gx")
    gradient, adjoint_out = call(
        last_kernel,
        [(2, OWN, LANES), (Q, 2, OWN, LANES)],
        [(SEND2,) + tile] * 2 + [(Q,) + wide, (Q, 2, OWN, LANES)],
    )(b1, edge1, sums, mom, b, bh, f1, left1, right1, grad, left, right, populations, solid)
    return gradient, adjoint_out


def solution(mesh):
    field, cell = P(None, "gx", "gy", "gz"), P("gx", "gy", "gz")
    return jax.shard_map(
        body, mesh=mesh, in_specs=(field, cell, cell, field), out_specs=(cell, field), check_vma=False
    )
```

```python
import jax
import jax.numpy as jnp
from jax import lax
from jax.experimental import pallas as pl
from jax.experimental.pallas import tpu as pltpu
from jax.sharding import PartitionSpec as P

INTERPRET = False

VEL = [
    (0, 0, 0),
    (1, 0, 0), (-1, 0, 0), (0, 1, 0), (0, -1, 0), (0, 0, 1), (0, 0, -1),
    (1, 1, 0), (-1, -1, 0), (1, -1, 0), (-1, 1, 0),
    (1, 0, 1), (-1, 0, -1), (1, 0, -1), (-1, 0, 1),
    (0, 1, 1), (0, -1, -1), (0, 1, -1), (0, -1, 1),
]
OPP = [0, 2, 1, 4, 3, 6, 5, 8, 7, 10, 9, 12, 11, 14, 13, 16, 15, 18, 17]
WEIGHT = [1.0 / 3.0] + [1.0 / 18.0] * 6 + [1.0 / 36.0] * 12
OMEGA = 1.25
Q = 19
XP = [i for i in range(Q) if VEL[i][0] == 1]
X0 = [i for i in range(Q) if VEL[i][0] == 0]
XM = [i for i in range(Q) if VEL[i][0] == -1]
PAIRS = [i for i in range(1, Q, 2)]

ROWS, OWN, LANES, RIM = 24, 16, 128, 4
FIELDS = 2 * Q + 1
ZTILES = -(-2 * FIELDS // 32)


def total(terms):
    terms = list(terms)
    while len(terms) > 1:
        terms = [a + b for a, b in zip(terms[::2], terms[1::2])] + (terms[-1:] if len(terms) % 2 else [])
    return terms[0]


ROOT = 4.5**0.5
FACES = [i for i in PAIRS if i < 7]
EDGES = [i for i in PAIRS if i >= 7]


def project(vector, i):
    out = None
    for axis in range(3):
        c = VEL[i][axis]
        if c == 0:
            continue
        if out is None:
            out = vector[axis] if c == 1 else -vector[axis]
        else:
            out = out + vector[axis] if c == 1 else out - vector[axis]
    return out


def gathered(terms, axis):
    plus = [terms[i] for i in terms if VEL[i][axis] == 1]
    minus = [terms[i] for i in terms if VEL[i][axis] == -1]
    return total(plus) - total(minus) if minus else total(plus)


def split(f, pairs=PAIRS):
    return {i: f[i] + f[i + 1] for i in pairs}, {i: f[i] - f[i + 1] for i in pairs}


def moments(f0, even, odd):
    rho = f0 + total(even.values())
    inv = 1.0 / rho
    return rho, [gathered(odd, axis) * inv for axis in range(3)]


def moments_from(level, even, odd):
    rho = level[0] + total(even.values())
    inv = 1.0 / rho
    return rho, [gathered(odd, 0) * inv] + [(level[axis] + gathered(odd, axis)) * inv for axis in (1, 2)]


def weights(blocking):
    keep = 1.0 - blocking
    own = (1.0 - OMEGA) * keep
    return 0.5 * (own + blocking), 0.5 * (own - blocking), OMEGA * keep


def collide(f0, even, odd, rho, u, blocking, want):
    k_even, k_odd, mix = weights(blocking)
    scale = mix * rho
    v = [ROOT * part for part in u]
    squares = [part * part for part in v]
    base = 1.0 - (1.0 / 3.0) * (squares[0] + squares[1] + squares[2])
    out = {}
    if 0 in want:
        out[0] = (2.0 * k_even) * f0 + (WEIGHT[0] * scale) * base
    for group in (FACES, EDGES):
        s = WEIGHT[group[0]] * scale
        s_odd = (2.0**0.5) * s
        for i in group:
            if i not in want and i + 1 not in want:
                continue
            p = project(v, i)
            square = squares[VEL[i].index(1)] if i in FACES else p * p
            p_even = k_even * even[i] + s * (base + square)
            p_odd = k_odd * odd[i] + s_odd * p
            if i in want:
                out[i] = p_even + p_odd
            if i + 1 in want:
                out[i + 1] = p_even - p_odd
    return out


def flow(b0, even, odd, u):
    base = 1.0 - 1.5 * (u[0] * u[0] + u[1] * u[1] + u[2] * u[2])
    q = [1.5 * part for part in u]
    level = [] if b0 is None else [WEIGHT[0] * b0]
    value, slope = [], [[], [], []]
    for group in (FACES, EDGES):
        group = [i for i in group if i in even]
        w = WEIGHT[group[0]]
        level.append(w * total(even[i] for i in group))
        work, along = [], {}
        for i in group:
            p = project(q, i)
            t = p * even[i]
            h = odd[i] + t
            work.append(p * h)
            along[i] = h + t
        value.append((2.0 * w) * total(work))
        for axis in range(3):
            if any(VEL[i][axis] for i in group):
                slope[axis].append((3.0 * w) * gathered(along, axis))
    level = total(level)
    return [base * level + total(value)] + [total(slope[axis]) - 2.0 * (q[axis] * level) for axis in range(3)]


def back(b0, even, odd, sums, u, blocking, want):
    energy, *v = sums
    k_even, k_odd, mix = weights(blocking)
    common = mix * (energy - (v[0] * u[0] + v[1] * u[1] + v[2] * u[2]))
    mv = [mix * v[axis] for axis in range(3)]
    out = {}
    if 0 in want:
        out[0] = (2.0 * k_even) * b0 + common
    for i in PAIRS:
        if i not in want and i + 1 not in want:
            continue
        p_even = k_even * even[i] + common
        p_odd = k_odd * odd[i] + project(mv, i)
        if i in want:
            out[i] = p_even + p_odd
        if i + 1 in want:
            out[i + 1] = p_even - p_odd
    return out


def gradient_of(b, f, rho, energy):
    evens = total(b[1][i] * f[1][i] for i in PAIRS)
    odds = total(b[2][i] * f[2][i] for i in PAIRS)
    return OMEGA * (b[0] * f[0] - rho * energy) + (0.5 * OMEGA) * evens - (1.0 - 0.5 * OMEGA) * odds


def column(shape):
    return lax.broadcasted_iota(jnp.int32, shape, len(shape) - 1)


def turn(tile, shift, axis):
    shift = shift % tile.shape[axis]
    return tile if shift == 0 else pltpu.roll(tile, shift, axis)


def moved(main, rim, i, sign):
    y, z = sign * VEL[i][1], sign * VEL[i][2]
    if y:
        main, rim = turn(main, y, 0), turn(rim, y, 0)
    if z:
        at = column(main.shape)
        edge = at == (0 if z == 1 else LANES - 1)
        main, rim = turn(main, z, 1), turn(rim, z, 1)
        main, rim = jnp.where(edge, rim, main), jnp.where(edge, main, rim)
    return main, rim


def pack_rims(ref, place, tiles, width):
    at = column((ROWS, LANES))
    joined, first = None, 0
    for k, (_, rim) in enumerate(tiles):
        piece = turn(rim(), first + width[k] // 2, 1)
        joined = piece if joined is None else jnp.where(at >= first, piece, joined)
        first += width[k]
    ref[place] = joined


def unpack_rims(tile, width, out):
    first = 0
    for k in range(len(width)):
        out(k, turn(tile, -(first + width[k] // 2), 1))
        first += width[k]


SEND1, SEND2 = 19, 14
WIDTH1 = [6] * 14 + [4] * 5
WIDTH2 = [2] * SEND2
ROWTILES2 = 2 * SEND2 + -(-SEND2 // 4)


def pack1(ref, tiles):
    for k, (main, _) in enumerate(tiles):
        ref[k] = main()
    pack_rims(ref, SEND1, tiles, WIDTH1)


def unpack1(ref, rim_ref):
    def out(k, rim):
        rim_ref[k] = rim

    unpack_rims(ref[SEND1], WIDTH1, out)


def pack2(ref, rim_ref, tiles):
    at = lax.broadcasted_iota(jnp.int32, (8, LANES), 0)
    joined = None
    for k, (main, _) in enumerate(tiles):
        tile = main()
        ref[2 * k], ref[2 * k + 1] = tile[0:8], tile[8:16]
        slot = 2 * (k % 4)
        piece = turn(tile[16:24], slot + 1, 0)
        joined = piece if slot == 0 else jnp.where(at >= slot, piece, joined)
        if slot == 6 or k == SEND2 - 1:
            ref[2 * SEND2 + k // 4] = joined
    pack_rims(rim_ref, 0, tiles, WIDTH2)
    for k in range(3):
        ref[ROWTILES2 + k] = rim_ref[0, 8 * k : 8 * k + 8, :]


def unpack2(ref, out_ref):
    for k in range(SEND2):
        out_ref[k, 0, 0:8, :] = ref[2 * k]
        out_ref[k, 0, 8:16, :] = ref[2 * k + 1]
        out_ref[k, 0, 16:24, :] = turn(ref[2 * SEND2 + k // 4], -(2 * (k % 4) + 1), 0)

    def out(k, rim):
        out_ref[k, 1] = rim

    unpack_rims(jnp.concatenate([ref[ROWTILES2 + k] for k in range(3)], axis=0), WIDTH2, out)


def call(kernel, outs, scratch=(), more=(), space=None, cost=1000):
    specs = {} if space is None else {"in_specs": [pl.BlockSpec(memory_space=s) for s in space]}
    return pl.pallas_call(
        kernel,
        out_shape=[jax.ShapeDtypeStruct(shape, jnp.float32) for shape in outs],
        scratch_shapes=[pltpu.VMEM(shape, jnp.float32) for shape in scratch] + list(more),
        compiler_params=None if INTERPRET else pltpu.CompilerParams(vmem_limit_bytes=40 * 2**20),
        cost_estimate=pl.CostEstimate(flops=cost * 2000, bytes_accessed=cost * 1000, transcendentals=0),
        interpret=INTERPRET,
        **specs,
    )


def rows_kernel(f_hbm, por_hbm, solid_hbm, seed_hbm, up_ref, down_ref, f_ref, seed_ref, b_ref, por_ref, solid_ref, sems):
    copies = [
        pltpu.make_async_copy(src, dst, sems.at[k])
        for k, (src, dst) in enumerate(
            [(f_hbm, f_ref), (seed_hbm, seed_ref), (por_hbm, por_ref), (solid_hbm, solid_ref)]
        )
    ]
    for copy in copies:
        copy.start()

    def send(k, layer, ref, *where):
        up_ref[k, 4 * layer : 4 * layer + 4, :] = ref[where + (slice(12, 16), slice(None))]
        down_ref[k, 4 * layer : 4 * layer + 4, :] = ref[where + (slice(0, 4), slice(None))]

    copies[0].wait()
    for k in range(Q):
        for layer in range(2):
            send(k, layer, f_ref, k, layer)
    copies[1].wait()
    for k in range(Q):
        for layer in range(2):
            send(k + Q, layer, seed_ref, k, layer)
    copies[2].wait()
    copies[3].wait()
    for layer in range(2):
        b_ref[layer] = jnp.where(solid_ref[layer] == 1, 1.0, por_ref[layer])
        send(2 * Q, layer, b_ref, layer)


def columns_kernel(f_ref, seed_ref, b_ref, below_ref, above_ref, main_ref, up_ref, down_ref):
    at = column((ROWS, LANES)) // 4
    high = low = None
    for k in range(FIELDS):
        for layer in range(2):
            if k < Q:
                own = f_ref[k, layer]
            elif k < 2 * Q:
                own = seed_ref[k - Q, layer]
            else:
                own = b_ref[layer]
            rows = slice(4 * layer, 4 * layer + 4)
            tile = jnp.concatenate([own, above_ref[k, rows, :], below_ref[k, rows, :]], axis=0)
            main_ref[k, layer] = tile
            slot = (2 * k + layer) % 32
            piece_up, piece_down = turn(tile, 4 * slot + 4, 1), turn(tile, 4 * slot, 1)
            high = piece_up if slot == 0 else jnp.where(at == slot, piece_up, high)
            low = piece_down if slot == 0 else jnp.where(at == slot, piece_down, low)
            if slot == 31 or 2 * k + layer == 2 * FIELDS - 1:
                up_ref[(2 * k + layer) // 32] = high
                down_ref[(2 * k + layer) // 32] = low


def tiles_loop(count, body):
    def step(n, carry):
        body(n // 3, pl.multiple_of((n % 3) * 8, 8))
        return carry

    lax.fori_loop(0, count, step, 0)


def main_kernel(main_ref, g_ref):
    for layer in range(2):

        def body(_, row, layer=layer):
            f = [main_ref[i, layer, pl.ds(row, 8), :] for i in range(Q)]
            even, odd = split(f)
            rho, u = moments(f[0], even, odd)
            g = collide(f[0], even, odd, rho, u, main_ref[2 * Q, layer, pl.ds(row, 8), :], range(Q))
            for i in range(Q):
                g_ref[i, layer, pl.ds(row, 8), :] = g[i]

        tiles_loop(3, body)


def first_kernel(
    main_ref, g_ref, before_ref, beyond_ref,
    f1_ref, edge_ref, level_ref, s_ref, b_ref, up_ref, down_ref,
    f_scr, g_scr,
):
    at = column((ROWS, LANES))
    for k in range(FIELDS):
        for layer in range(2):
            n = 2 * k + layer
            slot, tile = n % 32, n // 32
            before = turn(before_ref[tile], -(4 * slot + 4), 1)
            beyond = turn(beyond_ref[tile], -4 * slot, 1)
            rim = jnp.where(at < RIM, beyond, before)
            if k < Q:
                f_scr[k, layer] = rim
            elif k < 2 * Q:
                s_ref[k - Q, layer] = rim
            else:
                b_ref[layer, 0] = main_ref[k, layer]
                b_ref[layer, 1] = rim

    for layer in range(2):

        def body(_, row, layer=layer):
            f = [f_scr[i, layer, pl.ds(row, 8), :] for i in range(Q)]
            even, odd = split(f)
            rho, u = moments(f[0], even, odd)
            g = collide(f[0], even, odd, rho, u, b_ref[layer, 1, pl.ds(row, 8), :], range(Q))
            for i in range(Q):
                g_scr[i, layer, pl.ds(row, 8), :] = g[i]

        tiles_loop(3, body)

    for i in range(Q):
        for layer in range(2):
            to = layer + VEL[i][0]
            tiles = moved(g_ref[i, layer], g_scr[i, layer], i, 1)
            for lane in range(2):
                if to in (0, 1):
                    f1_ref[i, to, lane] = tiles[lane]
                else:
                    edge_ref[i, lane] = tiles[lane]
    for layer in range(2):
        for lane in range(2):
            stay = {i: f1_ref[i, layer, lane] for i in X0}
            level_ref[0, layer, lane] = total(stay.values())
            for axis in (1, 2):
                level_ref[axis, layer, lane] = total(
                    stay[i] if VEL[i][axis] == 1 else -stay[i] for i in X0 if VEL[i][axis]
                )

    def tiles_of(forward, backward, layer):
        def pick(ref, *where):
            return (lambda: ref[where + (0,)]), (lambda: ref[where + (1,)])

        out = [pick(f1_ref, i, layer) for i in forward]
        out += [pick(level_ref, k, layer) for k in range(3)]
        out.append(pick(b_ref, layer))
        out += [pick(edge_ref, i) for i in forward]
        for i in backward:
            pair = moved(main_ref[Q + i, layer], s_ref[i, layer], i, -1)
            out.append(((lambda pair=pair: pair[0]), (lambda pair=pair: pair[1])))
        return out

    pack1(up_ref, tiles_of(XP, XM, 1))
    pack1(down_ref, tiles_of(XM, XP, 0))


def seed_kernel(main_ref, s_ref, b2_ref):
    for i in range(Q):
        for layer in range(2):
            to = layer - VEL[i][0]
            if to in (0, 1):
                main, rim = moved(main_ref[Q + i, layer], s_ref[i, layer], i, -1)
                b2_ref[i, to, 0] = main
                b2_ref[i, to, 1] = rim


def middle_kernel(
    f1_ref, edge_ref, level_ref, b_ref, b2_ref, left_ref, right_ref,
    mom_ref, bh_ref, grad_ref, b1_ref, edge1_ref, sums_ref, up_ref, down_ref,
    l_scr, r_scr, g_scr, f_scr, a_scr, rim_scr,
):
    unpack1(left_ref, l_scr)
    unpack1(right_ref, r_scr)
    got = ((left_ref, right_ref), (l_scr, r_scr))
    for side in range(2):
        for lane in range(2):
            bh_ref[side, lane] = got[lane][side][8]

    for layer in range(2):
        for lane in range(2):

            def body(_, row, layer=layer, lane=lane):
                rows = pl.ds(row, 8)
                missing = XP if layer == 0 else XM
                f = [None if i in missing else f1_ref[i, layer, lane, rows, :] for i in range(Q)]
                for k, i in enumerate(missing):
                    f[i] = got[lane][layer][9 + k, rows, :]
                even, odd = split(f)
                rho, u = moments(f[0], even, odd)
                mom_ref[3, layer + 1, lane, rows, :] = rho
                for axis in range(3):
                    mom_ref[axis, layer + 1, lane, rows, :] = u[axis]
                g = collide(f[0], even, odd, rho, u, b_ref[layer, lane, rows, :], range(Q))
                for i in range(Q):
                    g_scr[i, layer + 1, lane, rows, :] = g[i]

            tiles_loop(3, body)

    for side in range(2):
        for lane in range(2):

            def body(_, row, side=side, lane=lane):
                rows = pl.ds(row, 8)
                theirs, ours = (XP, XM) if side == 0 else (XM, XP)
                f = [None] * Q
                for k, i in enumerate(theirs):
                    f[i] = got[lane][side][k, rows, :]
                for i in ours:
                    f[i] = edge_ref[i, lane, rows, :]
                even, odd = split(f, XP)
                rho, u = moments_from([got[lane][side][5 + k, rows, :] for k in range(3)], even, odd)
                for axis in range(3):
                    mom_ref[axis, 3 * side, lane, rows, :] = u[axis]
                g = collide(None, even, odd, rho, u, got[lane][side][8, rows, :], theirs)
                for i in theirs:
                    g_scr[i, 3 * side, lane, rows, :] = g[i]

            tiles_loop(3, body)

    for i in range(Q):
        for layer in range(2):
            n = layer + 1 - VEL[i][0]
            main, rim = moved(g_scr[i, n, 0], g_scr[i, n, 1], i, 1)
            f_scr[i, layer, 0] = main
            f_scr[i, layer, 1] = rim

    for layer in range(2):
        for lane in range(2):

            def body(row, layer=layer, lane=lane, own=False):
                rows = pl.ds(row, 8)
                missing = XM if layer == 0 else XP
                f = [f_scr[i, layer, lane, rows, :] for i in range(Q)]
                b = {i: b2_ref[i, layer, lane, rows, :] for i in range(Q) if i not in missing}
                for k, i in enumerate(missing):
                    b[i] = got[lane][layer][14 + k, rows, :]
                even, odd = split(f)
                rho, u = moments(f[0], even, odd)
                b_even, b_odd = split(b)
                sums = flow(b[0], b_even, b_odd, u)
                a = back(b[0], b_even, b_odd, sums, u, b_ref[layer, lane, rows, :], range(Q))
                for i in range(Q):
                    a_scr[i, layer, lane, rows, :] = a[i]
                if own:
                    grad_ref[layer, rows, :] = gradient_of((b[0], b_even, b_odd), (f[0], even, odd), rho, sums[0])

            if lane == 0:

                def step(n, carry, body=body):
                    body(pl.multiple_of(n * 8, 8), own=True)
                    return carry

                lax.fori_loop(0, 2, step, 0)
                body(16)
            else:
                tiles_loop(3, lambda _, row, body=body: body(row))

    for i in range(Q):
        for layer in range(2):
            to = layer - VEL[i][0]
            tiles = moved(a_scr[i, layer, 0], a_scr[i, layer, 1], i, -1)
            for lane in range(2):
                if to in (0, 1):
                    b1_ref[i, to, lane] = tiles[lane]
                else:
                    edge1_ref[i, lane] = tiles[lane]

    for layer in range(2):
        for lane in range(2):

            def body(_, row, layer=layer, lane=lane):
                rows = pl.ds(row, 8)
                missing = XM if layer == 0 else XP
                b = {i: b1_ref[i, layer, lane, rows, :] for i in range(Q) if i not in missing}
                even, odd = split(b, [i for i in PAIRS if i in X0])
                for i in XP:
                    even[i], odd[i] = (b[i], b[i]) if layer == 0 else (b[i + 1], -b[i + 1])
                sums = flow(b[0], even, odd, [mom_ref[axis, layer + 1, lane, rows, :] for axis in range(3)])
                for k in range(4):
                    sums_ref[k, layer, lane, rows, :] = sums[k]

            tiles_loop(3, body)

    def tiles_of(theirs, layer):
        def pick(ref, *where):
            return (lambda: ref[where + (0,)]), (lambda: ref[where + (1,)])

        return (
            [pick(edge1_ref, i) for i in theirs]
            + [pick(b1_ref, i, layer) for i in theirs]
            + [pick(sums_ref, k, layer) for k in range(4)]
        )

    pack2(up_ref, rim_scr, tiles_of(XM, 1))
    pack2(down_ref, rim_scr, tiles_of(XP, 0))


def last_kernel(
    b1_ref, edge1_ref, sums_ref, mom_ref, b_ref, bh_ref, f1_ref, left1_ref, right1_ref, grad_ref, left_ref, right_ref, f_ref, solid_ref,
    out_grad_ref, out_ref,
    l_scr, r_scr, a_scr, b0_scr,
):
    unpack2(left_ref, l_scr)
    unpack2(right_ref, r_scr)
    got = (l_scr, r_scr)
    got1 = (left1_ref, right1_ref)

    for layer in range(2):
        for lane in range(2):

            def body(row, layer=layer, lane=lane, own=False):
                rows = pl.ds(row, 8)
                missing = XM if layer == 0 else XP
                b = {i: b1_ref[i, layer, lane, rows, :] for i in range(Q) if i not in missing}
                for k, i in enumerate(missing):
                    b[i] = got[layer][k, lane, rows, :]
                new_even = {i: b[i + 1] if layer == 0 else b[i] for i in XP}
                new_odd = {i: -b[i + 1] if layer == 0 else b[i] for i in XP}
                even, odd = split(b)
                u = [mom_ref[axis, layer + 1, lane, rows, :] for axis in range(3)]
                sums = [sums_ref[k, layer, lane, rows, :] + part for k, part in enumerate(flow(None, new_even, new_odd, u))]
                a = back(b[0], even, odd, sums, u, b_ref[layer, lane, rows, :], range(Q))
                for i in range(Q):
                    a_scr[i, layer + 1, lane, rows, :] = a[i]
                if own:
                    f = {i: f1_ref[i, layer, lane, rows, :] for i in range(Q) if OPP[i] not in missing}
                    for k, i in enumerate(XP if layer == 0 else XM):
                        f[i] = got1[layer][9 + k, rows, :]
                    grad = gradient_of((b[0], even, odd), (f[0],) + split(f), mom_ref[3, layer + 1, lane, rows, :], sums[0])
                    out_grad_ref[layer, rows, :] = grad + grad_ref[layer, rows, :]

            if lane == 0:

                def step(n, carry, body=body):
                    body(pl.multiple_of(n * 8, 8), own=True)
                    return carry

                lax.fori_loop(0, 2, step, 0)
                body(16)
            else:
                tiles_loop(3, lambda _, row, body=body: body(row))

    for side in range(2):
        for lane in range(2):

            def body(_, row, side=side, lane=lane):
                rows = pl.ds(row, 8)
                theirs, ours = (XM, XP) if side == 0 else (XP, XM)
                b = {i: edge1_ref[i, lane, rows, :] for i in ours}
                for k, i in enumerate(theirs):
                    b[i] = got[side][5 + k, lane, rows, :]
                new_even = {i: b[i] if side == 0 else b[i + 1] for i in XP}
                new_odd = {i: b[i] if side == 0 else -b[i + 1] for i in XP}
                even, odd = split(b, XP)
                u = [mom_ref[axis, 3 * side, lane, rows, :] for axis in range(3)]
                sums = [got[side][10 + k, lane, rows, :] + part for k, part in enumerate(flow(None, new_even, new_odd, u))]
                a = back(None, even, odd, sums, u, bh_ref[side, lane, rows, :], theirs)
                for i in theirs:
                    a_scr[i, 3 * side, lane, rows, :] = a[i]

            tiles_loop(3, body)

    for i in range(Q):
        for layer in range(2):
            n = layer + 1 + VEL[i][0]
            main, _ = moved(a_scr[i, n, 0], a_scr[i, n, 1], i, -1)
            b0_scr[i, layer] = main[0:OWN]

    for layer in range(2):

        def final(n, carry, layer=layer):
            rows = pl.ds(pl.multiple_of(n * 8, 8), 8)
            f = [f_ref[i, layer, rows, :] for i in range(Q)]
            b = {i: b0_scr[i, layer, rows, :] for i in range(Q)}
            even, odd = split(f)
            rho, u = moments(f[0], even, odd)
            b_even, b_odd = split(b)
            sums = flow(b[0], b_even, b_odd, u)
            a = back(b[0], b_even, b_odd, sums, u, b_ref[layer, 0, rows, :], range(Q))
            for i in range(Q):
                out_ref[i, layer, rows, :] = a[i]
            grad = gradient_of((b[0], b_even, b_odd), (f[0], even, odd), rho, sums[0]) + out_grad_ref[layer, rows, :]
            out_grad_ref[layer, rows, :] = jnp.where(solid_ref[layer, rows, :] == 1, 0.0, grad)
            return carry

        lax.fori_loop(0, 2, final, 0)


def placed(x):
    return x if INTERPRET else pltpu.with_memory_space_constraint(x, pltpu.HBM)


def both_ways(up, down, axis):
    count = lax.axis_size(axis)
    ring = [(i, (i + 1) % count) for i in range(count)]
    return lax.ppermute(up, axis, ring), lax.ppermute(down, axis, [(j, i) for i, j in ring])


def body(populations, porosity, solid, seed_adjoint):
    half, tile = (2, 2, ROWS, LANES), (ROWS, LANES)
    inputs = [placed(x) for x in (populations, porosity, solid, seed_adjoint)]
    block = populations.shape
    up, down, f, seed, b = call(
        rows_kernel,
        [(FIELDS, 8, LANES)] * 2 + [block, block, block[1:]],
        [block[1:]],
        [pltpu.VMEM(block[1:], jnp.int32), pltpu.SemaphoreType.DMA((4,))],
        space=[pltpu.HBM] * 4,
    )(*inputs)
    below, above = both_ways(up, down, "gy")
    main, up, down = call(columns_kernel, [(FIELDS, 2) + tile] + [(ZTILES,) + tile] * 2)(f, seed, b, below, above)
    before, beyond = both_ways(up, down, "gz")
    (g,) = call(main_kernel, [(Q, 2) + tile])(main)
    f1, edge, level, s, b, up, down = call(
        first_kernel,
        [(Q,) + half, (Q, 2) + tile, (3,) + half, (Q, 2) + tile, half] + [(SEND1 + 1,) + tile] * 2,
        [(Q, 2) + tile] * 2,
    )(main, g, before, beyond)
    left1, right1 = both_ways(up, down, "gx")
    (b2,) = call(seed_kernel, [(Q,) + half])(main, s)
    wide = (4, 2) + tile
    mom, bh, grad, b1, edge1, sums, up, down = call(
        middle_kernel,
        [(4,) + wide, half, (2, OWN, LANES), (Q,) + half, (Q, 2) + tile, (4,) + half] + [(ROWTILES2 + 3, 8, LANES)] * 2,
        [(SEND1,) + tile] * 2 + [(Q,) + wide, (Q,) + half, (Q,) + half, (1,) + tile],
    )(f1, edge, level, b, b2, left1, right1)
    left, right = both_ways(up, down, "gx")
    gradient, adjoint_out = call(
        last_kernel,
        [(2, OWN, LANES), (Q, 2, OWN, LANES)],
        [(SEND2, 2) + tile] * 2 + [(Q,) + wide, (Q, 2, OWN, LANES)],
    )(b1, edge1, sums, mom, b, bh, f1, left1, right1, grad, left, right, f, solid)
    return gradient, adjoint_out


def solution(mesh):
    field, cell = P(None, "gx", "gy", "gz"), P("gx", "gy", "gz")
    return jax.shard_map(
        body, mesh=mesh, in_specs=(field, cell, cell, field), out_specs=(cell, field), check_vma=False
    )
```

```python
import functools

import jax
import jax.numpy as jnp
from jax import lax
from jax.experimental import pallas as pl
from jax.experimental.pallas import tpu as pltpu
from jax.sharding import PartitionSpec as P

INTERPRET = False

VEL = [
    (0, 0, 0),
    (1, 0, 0), (-1, 0, 0), (0, 1, 0), (0, -1, 0), (0, 0, 1), (0, 0, -1),
    (1, 1, 0), (-1, -1, 0), (1, -1, 0), (-1, 1, 0),
    (1, 0, 1), (-1, 0, -1), (1, 0, -1), (-1, 0, 1),
    (0, 1, 1), (0, -1, -1), (0, 1, -1), (0, -1, 1),
]
OPP = [0, 2, 1, 4, 3, 6, 5, 8, 7, 10, 9, 12, 11, 14, 13, 16, 15, 18, 17]
WEIGHT = [1.0 / 3.0] + [1.0 / 18.0] * 6 + [1.0 / 36.0] * 12
OMEGA = 1.25
Q = 19
XP = [i for i in range(Q) if VEL[i][0] == 1]
X0 = [i for i in range(Q) if VEL[i][0] == 0]
XM = [i for i in range(Q) if VEL[i][0] == -1]
PAIRS = [i for i in range(1, Q, 2)]

ROWS, OWN, LANES, RIM = 24, 16, 128, 4
FIELDS = 2 * Q + 1
ZTILES = -(-2 * FIELDS // 32)


def total(terms):
    terms = list(terms)
    while len(terms) > 1:
        terms = [a + b for a, b in zip(terms[::2], terms[1::2])] + (terms[-1:] if len(terms) % 2 else [])
    return terms[0]


ROOT = 4.5**0.5
FACES = [i for i in PAIRS if i < 7]
EDGES = [i for i in PAIRS if i >= 7]


def project(vector, i):
    out = None
    for axis in range(3):
        c = VEL[i][axis]
        if c == 0:
            continue
        if out is None:
            out = vector[axis] if c == 1 else -vector[axis]
        else:
            out = out + vector[axis] if c == 1 else out - vector[axis]
    return out


def gathered(terms, axis):
    plus = [terms[i] for i in terms if VEL[i][axis] == 1]
    minus = [terms[i] for i in terms if VEL[i][axis] == -1]
    return total(plus) - total(minus) if minus else total(plus)


def split(f, pairs=PAIRS):
    return {i: f[i] + f[i + 1] for i in pairs}, {i: f[i] - f[i + 1] for i in pairs}


def moments(f0, even, odd):
    rho = f0 + total(even.values())
    inv = 1.0 / rho
    return rho, [gathered(odd, axis) * inv for axis in range(3)]


def moments_from(level, even, odd):
    rho = level[0] + total(even.values())
    inv = 1.0 / rho
    return rho, [gathered(odd, 0) * inv] + [(level[axis] + gathered(odd, axis)) * inv for axis in (1, 2)]


def weights(blocking):
    keep = 1.0 - blocking
    own = (1.0 - OMEGA) * keep
    return 0.5 * (own + blocking), 0.5 * (own - blocking), OMEGA * keep


def collide(f0, even, odd, rho, u, blocking, want):
    k_even, k_odd, mix = weights(blocking)
    scale = mix * rho
    v = [ROOT * part for part in u]
    squares = [part * part for part in v]
    base = 1.0 - (1.0 / 3.0) * (squares[0] + squares[1] + squares[2])
    out = {}
    if 0 in want:
        out[0] = (2.0 * k_even) * f0 + (WEIGHT[0] * scale) * base
    for group in (FACES, EDGES):
        s = WEIGHT[group[0]] * scale
        s_odd = (2.0**0.5) * s
        for i in group:
            if i not in want and i + 1 not in want:
                continue
            p = project(v, i)
            square = squares[VEL[i].index(1)] if i in FACES else p * p
            p_even = k_even * even[i] + s * (base + square)
            p_odd = k_odd * odd[i] + s_odd * p
            if i in want:
                out[i] = p_even + p_odd
            if i + 1 in want:
                out[i + 1] = p_even - p_odd
    return out


def flow(b0, even, odd, u):
    base = 1.0 - 1.5 * (u[0] * u[0] + u[1] * u[1] + u[2] * u[2])
    q = [1.5 * part for part in u]
    level = [] if b0 is None else [WEIGHT[0] * b0]
    value, slope = [], [[], [], []]
    for group in (FACES, EDGES):
        group = [i for i in group if i in even]
        w = WEIGHT[group[0]]
        level.append(w * total(even[i] for i in group))
        work, along = [], {}
        for i in group:
            p = project(q, i)
            t = p * even[i]
            h = odd[i] + t
            work.append(p * h)
            along[i] = h + t
        value.append((2.0 * w) * total(work))
        for axis in range(3):
            if any(VEL[i][axis] for i in group):
                slope[axis].append((3.0 * w) * gathered(along, axis))
    level = total(level)
    return [base * level + total(value)] + [total(slope[axis]) - 2.0 * (q[axis] * level) for axis in range(3)]


def back(b0, even, odd, sums, u, blocking, want):
    energy, *v = sums
    k_even, k_odd, mix = weights(blocking)
    common = mix * (energy - (v[0] * u[0] + v[1] * u[1] + v[2] * u[2]))
    mv = [mix * v[axis] for axis in range(3)]
    out = {}
    if 0 in want:
        out[0] = (2.0 * k_even) * b0 + common
    for i in PAIRS:
        if i not in want and i + 1 not in want:
            continue
        p_even = k_even * even[i] + common
        p_odd = k_odd * odd[i] + project(mv, i)
        if i in want:
            out[i] = p_even + p_odd
        if i + 1 in want:
            out[i + 1] = p_even - p_odd
    return out


def gradient_of(b, f, rho, energy):
    evens = total(b[1][i] * f[1][i] for i in PAIRS)
    odds = total(b[2][i] * f[2][i] for i in PAIRS)
    return OMEGA * (b[0] * f[0] - rho * energy) + (0.5 * OMEGA) * evens - (1.0 - 0.5 * OMEGA) * odds


def column(shape):
    return lax.broadcasted_iota(jnp.int32, shape, len(shape) - 1)


def turn(tile, shift, axis):
    shift = shift % tile.shape[axis]
    return tile if shift == 0 else pltpu.roll(tile, shift, axis)


def moved(main, rim, i, sign):
    y, z = sign * VEL[i][1], sign * VEL[i][2]
    if y:
        main, rim = turn(main, y, 0), turn(rim, y, 0)
    if z:
        at = column(main.shape)
        edge = at == (0 if z == 1 else LANES - 1)
        main, rim = turn(main, z, 1), turn(rim, z, 1)
        main, rim = jnp.where(edge, rim, main), jnp.where(edge, main, rim)
    return main, rim


def pack_rims(ref, place, tiles, width):
    at = column((ROWS, LANES))
    joined, first = None, 0
    for k, (_, rim) in enumerate(tiles):
        piece = turn(rim(), first + width[k] // 2, 1)
        joined = piece if joined is None else jnp.where(at >= first, piece, joined)
        first += width[k]
    ref[place] = joined


def unpack_rims(tile, width, out):
    first = 0
    for k in range(len(width)):
        out(k, turn(tile, -(first + width[k] // 2), 1))
        first += width[k]


SEND1, SEND2 = 19, 14
WIDTH1 = [6] * 14 + [4] * 5
WIDTH2 = [2] * SEND2
ROWTILES2 = 2 * SEND2 + -(-SEND2 // 4)


def pack1(ref, tiles):
    for k, (main, _) in enumerate(tiles):
        ref[k] = main()
    pack_rims(ref, SEND1, tiles, WIDTH1)


def unpack1(ref, rim_ref):
    def out(k, rim):
        rim_ref[k] = rim

    unpack_rims(ref[SEND1], WIDTH1, out)


def pack2(ref, rim_ref, tiles):
    at = lax.broadcasted_iota(jnp.int32, (8, LANES), 0)
    joined = None
    for k, (main, _) in enumerate(tiles):
        tile = main()
        ref[2 * k], ref[2 * k + 1] = tile[0:8], tile[8:16]
        slot = 2 * (k % 4)
        piece = turn(tile[16:24], slot + 1, 0)
        joined = piece if slot == 0 else jnp.where(at >= slot, piece, joined)
        if slot == 6 or k == SEND2 - 1:
            ref[2 * SEND2 + k // 4] = joined
    pack_rims(rim_ref, 0, tiles, WIDTH2)
    for k in range(3):
        ref[ROWTILES2 + k] = rim_ref[0, 8 * k : 8 * k + 8, :]


def unpack2(ref, out_ref):
    for k in range(SEND2):
        out_ref[k, 0, 0:8, :] = ref[2 * k]
        out_ref[k, 0, 8:16, :] = ref[2 * k + 1]
        out_ref[k, 0, 16:24, :] = turn(ref[2 * SEND2 + k // 4], -(2 * (k % 4) + 1), 0)

    def out(k, rim):
        out_ref[k, 1] = rim

    unpack_rims(jnp.concatenate([ref[ROWTILES2 + k] for k in range(3)], axis=0), WIDTH2, out)


def call(kernel, outs, scratch=(), more=(), space=None, cost=1000):
    specs = {} if space is None else {"in_specs": [pl.BlockSpec(memory_space=s) for s in space]}
    return pl.pallas_call(
        kernel,
        out_shape=[jax.ShapeDtypeStruct(shape, jnp.float32) for shape in outs],
        scratch_shapes=[pltpu.VMEM(shape, jnp.float32) for shape in scratch] + list(more),
        compiler_params=None if INTERPRET else pltpu.CompilerParams(vmem_limit_bytes=40 * 2**20),
        cost_estimate=pl.CostEstimate(flops=cost * 2000, bytes_accessed=cost * 1000, transcendentals=0),
        interpret=INTERPRET,
        **specs,
    )


def rows_kernel(f_hbm, por_hbm, solid_hbm, seed_hbm, up_ref, down_ref, f_ref, seed_ref, b_ref, fluid_ref, por_ref, solid_ref, sems):
    copies = [
        pltpu.make_async_copy(src, dst, sems.at[k])
        for k, (src, dst) in enumerate(
            [(f_hbm, f_ref), (seed_hbm, seed_ref), (por_hbm, por_ref), (solid_hbm, solid_ref)]
        )
    ]
    for copy in copies:
        copy.start()

    def send(k, layer, ref, *where):
        up_ref[k, 4 * layer : 4 * layer + 4, :] = ref[where + (slice(12, 16), slice(None))]
        down_ref[k, 4 * layer : 4 * layer + 4, :] = ref[where + (slice(0, 4), slice(None))]

    copies[0].wait()
    for k in range(Q):
        for layer in range(2):
            send(k, layer, f_ref, k, layer)
    copies[1].wait()
    for k in range(Q):
        for layer in range(2):
            send(k + Q, layer, seed_ref, k, layer)
    copies[2].wait()
    copies[3].wait()
    for layer in range(2):
        b_ref[layer] = jnp.where(solid_ref[layer] == 1, 1.0, por_ref[layer])
        fluid_ref[layer] = jnp.where(solid_ref[layer] == 1, 0.0, 1.0)
        send(2 * Q, layer, b_ref, layer)


def columns_kernel(f_ref, seed_ref, b_ref, below_ref, above_ref, main_ref, up_ref, down_ref):
    at = column((ROWS, LANES)) // 4
    high = low = None
    for k in range(FIELDS):
        for layer in range(2):
            if k < Q:
                own = f_ref[k, layer]
            elif k < 2 * Q:
                own = seed_ref[k - Q, layer]
            else:
                own = b_ref[layer]
            rows = slice(4 * layer, 4 * layer + 4)
            tile = jnp.concatenate([own, above_ref[k, rows, :], below_ref[k, rows, :]], axis=0)
            main_ref[k, layer] = tile
            slot = (2 * k + layer) % 32
            piece_up, piece_down = turn(tile, 4 * slot + 4, 1), turn(tile, 4 * slot, 1)
            high = piece_up if slot == 0 else jnp.where(at == slot, piece_up, high)
            low = piece_down if slot == 0 else jnp.where(at == slot, piece_down, low)
            if slot == 31 or 2 * k + layer == 2 * FIELDS - 1:
                up_ref[(2 * k + layer) // 32] = high
                down_ref[(2 * k + layer) // 32] = low


def tiles_loop(count, body):
    for n in range(count):
        body(8 * n)


def main_kernel(main_ref, g_ref):
    for layer in range(2):

        def body(row, layer=layer):
            f = [main_ref[i, layer, slice(row, row + 8), :] for i in range(Q)]
            even, odd = split(f)
            rho, u = moments(f[0], even, odd)
            g = collide(f[0], even, odd, rho, u, main_ref[2 * Q, layer, slice(row, row + 8), :], range(Q))
            for i in range(Q):
                g_ref[i, layer, slice(row, row + 8), :] = g[i]

        tiles_loop(3, body)


def first_kernel(
    main_ref, g_ref, before_ref, beyond_ref,
    f1_ref, edge_ref, s_ref, b_ref, up_ref, down_ref,
    f_scr, g_scr, level_ref,
):
    at = column((ROWS, LANES))
    for k in range(FIELDS):
        for layer in range(2):
            n = 2 * k + layer
            slot, tile = n % 32, n // 32
            before = turn(before_ref[tile], -(4 * slot + 4), 1)
            beyond = turn(beyond_ref[tile], -4 * slot, 1)
            rim = jnp.where(at < RIM, beyond, before)
            if k < Q:
                f_scr[k, layer] = rim
            elif k < 2 * Q:
                s_ref[k - Q, layer] = rim
            else:
                b_ref[layer, 0] = main_ref[k, layer]
                b_ref[layer, 1] = rim

    for layer in range(2):

        def body(row, layer=layer):
            f = [f_scr[i, layer, slice(row, row + 8), :] for i in range(Q)]
            even, odd = split(f)
            rho, u = moments(f[0], even, odd)
            g = collide(f[0], even, odd, rho, u, b_ref[layer, 1, slice(row, row + 8), :], range(Q))
            for i in range(Q):
                g_scr[i, layer, slice(row, row + 8), :] = g[i]

        tiles_loop(3, body)

    for i in range(Q):
        for layer in range(2):
            to = layer + VEL[i][0]
            tiles = moved(g_ref[i, layer], g_scr[i, layer], i, 1)
            for lane in range(2):
                if to in (0, 1):
                    f1_ref[i, to, lane] = tiles[lane]
                else:
                    edge_ref[i, lane] = tiles[lane]
    for layer in range(2):
        for lane in range(2):
            stay = {i: f1_ref[i, layer, lane] for i in X0}
            level_ref[0, layer, lane] = total(stay.values())
            for axis in (1, 2):
                level_ref[axis, layer, lane] = total(
                    stay[i] if VEL[i][axis] == 1 else -stay[i] for i in X0 if VEL[i][axis]
                )

    def tiles_of(forward, backward, layer):
        def pick(ref, *where):
            return (lambda: ref[where + (0,)]), (lambda: ref[where + (1,)])

        out = [pick(f1_ref, i, layer) for i in forward]
        out += [pick(level_ref, k, layer) for k in range(3)]
        out.append(pick(b_ref, layer))
        out += [pick(edge_ref, i) for i in forward]
        for i in backward:
            pair = moved(main_ref[Q + i, layer], s_ref[i, layer], i, -1)
            out.append(((lambda pair=pair: pair[0]), (lambda pair=pair: pair[1])))
        return out

    pack1(up_ref, tiles_of(XP, XM, 1))
    pack1(down_ref, tiles_of(XM, XP, 0))


def seed_kernel(main_ref, s_ref, b2_ref):
    for i in range(Q):
        for layer in range(2):
            to = layer - VEL[i][0]
            if to in (0, 1):
                main, rim = moved(main_ref[Q + i, layer], s_ref[i, layer], i, -1)
                b2_ref[i, to, 0] = main
                b2_ref[i, to, 1] = rim


def side_kernel(side, f1_ref, edge_ref, b_ref, got_ref, mom_ref, far_ref, bh_ref, g_ref, far_g_ref, rim_scr):
    unpack1(got_ref, rim_scr)
    got = (got_ref, rim_scr)
    theirs, ours = (XP, XM) if side == 0 else (XM, XP)
    for lane in range(2):
        bh_ref[lane] = got[lane][8]

        def near(row, lane=lane):
            rows = slice(row, row + 8)
            f = [None if i in theirs else f1_ref[i, side, lane, rows, :] for i in range(Q)]
            for k, i in enumerate(theirs):
                f[i] = got[lane][9 + k, rows, :]
            even, odd = split(f)
            rho, u = moments(f[0], even, odd)
            mom_ref[3, lane, rows, :] = rho
            for axis in range(3):
                mom_ref[axis, lane, rows, :] = u[axis]
            g = collide(f[0], even, odd, rho, u, b_ref[side, lane, rows, :], range(Q))
            for i in range(Q):
                g_ref[i, lane, rows, :] = g[i]

        def far(row, lane=lane):
            rows = slice(row, row + 8)
            f = [None] * Q
            for k, i in enumerate(theirs):
                f[i] = got[lane][k, rows, :]
            for i in ours:
                f[i] = edge_ref[i, lane, rows, :]
            even, odd = split(f, XP)
            rho, u = moments_from([got[lane][5 + k, rows, :] for k in range(3)], even, odd)
            for axis in range(3):
                far_ref[axis, lane, rows, :] = u[axis]
            g = collide(None, even, odd, rho, u, got[lane][8, rows, :], theirs)
            for i in theirs:
                far_g_ref[i, lane, rows, :] = g[i]

        tiles_loop(3, near)
        tiles_loop(3, far)


def middle_kernel(
    b_ref, b2_ref, left_ref, right_ref, mom0_ref, mom1_ref, g0_ref, g1_ref, g_left_ref, g_right_ref,
    grad_ref, b1_ref, edge1_ref, sums_ref, up_ref, down_ref,
    l_scr, r_scr, f_scr, a_scr, rim_scr,
):
    def out(scr):
        def put(k, rim):
            if k >= 14:
                scr[k] = rim

        return put

    unpack_rims(left_ref[SEND1], WIDTH1, out(l_scr))
    unpack_rims(right_ref[SEND1], WIDTH1, out(r_scr))
    got = ((left_ref, right_ref), (l_scr, r_scr))
    g_refs = (g_left_ref, g0_ref, g1_ref, g_right_ref)
    mom = (mom0_ref, mom1_ref)

    for i in range(Q):
        for layer in range(2):
            ref = g_refs[layer + 1 - VEL[i][0]]
            main, rim = moved(ref[i, 0], ref[i, 1], i, 1)
            f_scr[i, layer, 0] = main
            f_scr[i, layer, 1] = rim

    for layer in range(2):
        for lane in range(2):

            def body(row, layer=layer, lane=lane):
                rows = slice(row, row + 8)
                missing = XM if layer == 0 else XP
                f = [f_scr[i, layer, lane, rows, :] for i in range(Q)]
                b = {i: b2_ref[i, layer, lane, rows, :] for i in range(Q) if i not in missing}
                for k, i in enumerate(missing):
                    b[i] = got[lane][layer][14 + k, rows, :]
                even, odd = split(f)
                rho, u = moments(f[0], even, odd)
                b_even, b_odd = split(b)
                sums = flow(b[0], b_even, b_odd, u)
                a = back(b[0], b_even, b_odd, sums, u, b_ref[layer, lane, rows, :], range(Q))
                for i in range(Q):
                    a_scr[i, layer, lane, rows, :] = a[i]
                if lane == 0 and row < OWN:
                    grad_ref[layer, rows, :] = gradient_of((b[0], b_even, b_odd), (f[0], even, odd), rho, sums[0])

            tiles_loop(3, body)

    for i in range(Q):
        for layer in range(2):
            to = layer - VEL[i][0]
            tiles = moved(a_scr[i, layer, 0], a_scr[i, layer, 1], i, -1)
            for lane in range(2):
                if to in (0, 1):
                    b1_ref[i, to, lane] = tiles[lane]
                else:
                    edge1_ref[i, lane] = tiles[lane]

    for layer in range(2):
        for lane in range(2):

            def body(row, layer=layer, lane=lane):
                rows = slice(row, row + 8)
                missing = XM if layer == 0 else XP
                b = {i: b1_ref[i, layer, lane, rows, :] for i in range(Q) if i not in missing}
                even, odd = split(b, [i for i in PAIRS if i in X0])
                for i in XP:
                    even[i], odd[i] = (b[i], b[i]) if layer == 0 else (b[i + 1], -b[i + 1])
                sums = flow(b[0], even, odd, [mom[layer][axis, lane, rows, :] for axis in range(3)])
                for k in range(4):
                    sums_ref[k, layer, lane, rows, :] = sums[k]

            tiles_loop(3, body)

    def tiles_of(theirs, layer):
        def pick(ref, *where):
            return (lambda: ref[where + (0,)]), (lambda: ref[where + (1,)])

        return (
            [pick(edge1_ref, i) for i in theirs]
            + [pick(b1_ref, i, layer) for i in theirs]
            + [pick(sums_ref, k, layer) for k in range(4)]
        )

    pack2(up_ref, rim_scr, tiles_of(XM, 1))
    pack2(down_ref, rim_scr, tiles_of(XP, 0))


def side_back_kernel(
    side, b1_ref, edge1_ref, sums_ref, mom_ref, far_ref, b_ref, bh_ref, f1_ref, got1_ref, grad_ref, got_ref,
    out_grad_ref, a_ref, far_a_ref,
    got,
):
    unpack2(got_ref, got)
    near_pops, far_pops = (XM, XP) if side == 0 else (XP, XM)

    def halves(b, plus):
        return {i: b[i] if plus else b[i + 1] for i in XP}, {i: b[i] if plus else -b[i + 1] for i in XP}

    for lane in range(2):

        def near(row, lane=lane):
            rows = slice(row, row + 8)
            b = {i: b1_ref[i, side, lane, rows, :] for i in range(Q) if i not in near_pops}
            for k, i in enumerate(near_pops):
                b[i] = got[k, lane, rows, :]
            even, odd = split(b)
            u = [mom_ref[axis, lane, rows, :] for axis in range(3)]
            parts = flow(None, *halves(b, side == 1), u)
            sums = [sums_ref[k, side, lane, rows, :] + part for k, part in enumerate(parts)]
            a = back(b[0], even, odd, sums, u, b_ref[side, lane, rows, :], range(Q))
            for i in range(Q):
                a_ref[i, lane, rows, :] = a[i]
            if lane == 0 and row < OWN:
                f = {i: f1_ref[i, side, lane, rows, :] for i in range(Q) if i not in far_pops}
                for k, i in enumerate(far_pops):
                    f[i] = got1_ref[9 + k, rows, :]
                grad = gradient_of((b[0], even, odd), (f[0],) + split(f), mom_ref[3, lane, rows, :], sums[0])
                out_grad_ref[rows, :] = grad + grad_ref[side, rows, :]

        def far(row, lane=lane):
            rows = slice(row, row + 8)
            b = {i: edge1_ref[i, lane, rows, :] for i in far_pops}
            for k, i in enumerate(near_pops):
                b[i] = got[5 + k, lane, rows, :]
            even, odd = split(b, XP)
            u = [far_ref[axis, lane, rows, :] for axis in range(3)]
            parts = flow(None, *halves(b, side == 0), u)
            sums = [got[10 + k, lane, rows, :] + part for k, part in enumerate(parts)]
            a = back(None, even, odd, sums, u, bh_ref[lane, rows, :], near_pops)
            for i in near_pops:
                far_a_ref[i, lane, rows, :] = a[i]

        tiles_loop(3, near)
        tiles_loop(3, far)


def last_kernel(
    b_ref, grad0_ref, grad1_ref, a_left_ref, a0_ref, a1_ref, a_right_ref, f_ref, fluid_ref,
    out_grad_ref, out_ref,
    b_scr,
):
    a_refs = (a_left_ref, a0_ref, a1_ref, a_right_ref)
    grads = (grad0_ref, grad1_ref)
    for i in range(Q):
        for layer in range(2):
            ref = a_refs[layer + 1 + VEL[i][0]]
            main, _ = moved(ref[i, 0], ref[i, 1], i, -1)
            b_scr[i, layer] = main[0:OWN]

    for layer in range(2):

        def body(row, layer=layer):
            rows = slice(row, row + 8)
            f = [f_ref[i, layer, rows, :] for i in range(Q)]
            b = {i: b_scr[i, layer, rows, :] for i in range(Q)}
            even, odd = split(f)
            rho, u = moments(f[0], even, odd)
            b_even, b_odd = split(b)
            sums = flow(b[0], b_even, b_odd, u)
            a = back(b[0], b_even, b_odd, sums, u, b_ref[layer, 0, rows, :], range(Q))
            for i in range(Q):
                out_ref[i, layer, rows, :] = a[i]
            grad = gradient_of((b[0], b_even, b_odd), (f[0], even, odd), rho, sums[0]) + grads[layer][rows, :]
            out_grad_ref[layer, rows, :] = jnp.where(fluid_ref[layer, rows, :] == 0.0, 0.0, grad)

        tiles_loop(2, body)


def placed(x):
    return x if INTERPRET else pltpu.with_memory_space_constraint(x, pltpu.HBM)


def both_ways(up, down, axis):
    count = lax.axis_size(axis)
    ring = [(i, (i + 1) % count) for i in range(count)]
    return lax.ppermute(up, axis, ring), lax.ppermute(down, axis, [(j, i) for i, j in ring])


def body(populations, porosity, solid, seed_adjoint):
    half, tile = (2, 2, ROWS, LANES), (ROWS, LANES)
    inputs = [placed(x) for x in (populations, porosity, solid, seed_adjoint)]
    block = populations.shape
    up, down, f, seed, b, fluid = call(
        rows_kernel,
        [(FIELDS, 8, LANES)] * 2 + [block, block, block[1:], block[1:]],
        [block[1:]],
        [pltpu.VMEM(block[1:], jnp.int32), pltpu.SemaphoreType.DMA((4,))],
        space=[pltpu.HBM] * 4,
    )(*inputs)
    below, above = both_ways(up, down, "gy")
    main, up, down = call(columns_kernel, [(FIELDS, 2) + tile] + [(ZTILES,) + tile] * 2)(f, seed, b, below, above)
    before, beyond = both_ways(up, down, "gz")
    (g,) = call(main_kernel, [(Q, 2) + tile])(main)
    f1, edge, s, b, up, down = call(
        first_kernel,
        [(Q,) + half, (Q, 2) + tile, (Q, 2) + tile, half] + [(SEND1 + 1,) + tile] * 2,
        [(Q, 2) + tile] * 2 + [(3,) + half],
    )(main, g, before, beyond)
    left1, right1 = both_ways(up, down, "gx")
    (b2,) = call(seed_kernel, [(Q,) + half])(main, s)
    sides = []
    for side, got in enumerate((left1, right1)):
        sides.append(
            call(
                functools.partial(side_kernel, side),
                [(4, 2) + tile, (3, 2) + tile, (2,) + tile, (Q, 2) + tile, (Q, 2) + tile],
                [(SEND1,) + tile],
            )(f1, edge, b, got)
        )
    (mom0, far0, bh0, g0, g_left), (mom1, far1, bh1, g1, g_right) = sides
    grad, b1, edge1, sums, up, down = call(
        middle_kernel,
        [(2, OWN, LANES), (Q,) + half, (Q, 2) + tile, (4,) + half] + [(ROWTILES2 + 3, 8, LANES)] * 2,
        [(SEND1,) + tile] * 2 + [(Q,) + half, (Q,) + half, (1,) + tile],
    )(b, b2, left1, right1, mom0, mom1, g0, g1, g_left, g_right)
    left, right = both_ways(up, down, "gx")
    sides = []
    for side, (mom, far, bh, got1, got) in enumerate(((mom0, far0, bh0, left1, left), (mom1, far1, bh1, right1, right))):
        sides.append(
            call(
                functools.partial(side_back_kernel, side),
                [(OWN, LANES), (Q, 2) + tile, (Q, 2) + tile],
                [(SEND2, 2) + tile],
            )(b1, edge1, sums, mom, far, b, bh, f1, got1, grad, got)
        )
    (grad0, a0, a_left), (grad1, a1, a_right) = sides
    gradient, adjoint_out = call(last_kernel, [(2, OWN, LANES), (Q, 2, OWN, LANES)], [(Q, 2, OWN, LANES)])(
        b, grad0, grad1, a_left, a0, a1, a_right, f, fluid
    )
    return gradient, adjoint_out


def solution(mesh):
    field, cell = P(None, "gx", "gy", "gz"), P("gx", "gy", "gz")
    return jax.shard_map(
        body, mesh=mesh, in_specs=(field, cell, cell, field), out_specs=(cell, field), check_vma=False
    )
```

```python
import functools

import jax
import jax.numpy as jnp
from jax import lax
from jax.experimental import pallas as pl
from jax.experimental.pallas import tpu as pltpu
from jax.sharding import PartitionSpec as P

INTERPRET = False

VEL = [
    (0, 0, 0),
    (1, 0, 0), (-1, 0, 0), (0, 1, 0), (0, -1, 0), (0, 0, 1), (0, 0, -1),
    (1, 1, 0), (-1, -1, 0), (1, -1, 0), (-1, 1, 0),
    (1, 0, 1), (-1, 0, -1), (1, 0, -1), (-1, 0, 1),
    (0, 1, 1), (0, -1, -1), (0, 1, -1), (0, -1, 1),
]
OPP = [0, 2, 1, 4, 3, 6, 5, 8, 7, 10, 9, 12, 11, 14, 13, 16, 15, 18, 17]
WEIGHT = [1.0 / 3.0] + [1.0 / 18.0] * 6 + [1.0 / 36.0] * 12
OMEGA = 1.25
Q = 19
XP = [i for i in range(Q) if VEL[i][0] == 1]
X0 = [i for i in range(Q) if VEL[i][0] == 0]
XM = [i for i in range(Q) if VEL[i][0] == -1]
PAIRS = [i for i in range(1, Q, 2)]

ROWS, OWN, LANES, RIM = 24, 16, 128, 4
FIELDS = 2 * Q + 1
ZTILES = -(-2 * FIELDS // 32)


def total(terms):
    terms = list(terms)
    while len(terms) > 1:
        terms = [a + b for a, b in zip(terms[::2], terms[1::2])] + (terms[-1:] if len(terms) % 2 else [])
    return terms[0]


ROOT = 4.5**0.5
FACES = [i for i in PAIRS if i < 7]
EDGES = [i for i in PAIRS if i >= 7]


def project(vector, i):
    out = None
    for axis in range(3):
        c = VEL[i][axis]
        if c == 0:
            continue
        if out is None:
            out = vector[axis] if c == 1 else -vector[axis]
        else:
            out = out + vector[axis] if c == 1 else out - vector[axis]
    return out


def gathered(terms, axis):
    plus = [terms[i] for i in terms if VEL[i][axis] == 1]
    minus = [terms[i] for i in terms if VEL[i][axis] == -1]
    return total(plus) - total(minus) if minus else total(plus)


def split(f, pairs=PAIRS):
    return {i: f[i] + f[i + 1] for i in pairs}, {i: f[i] - f[i + 1] for i in pairs}


def moments(f0, even, odd):
    rho = f0 + total(even.values())
    inv = 1.0 / rho
    return rho, [gathered(odd, axis) * inv for axis in range(3)]


def moments_from(level, even, odd):
    rho = level[0] + total(even.values())
    inv = 1.0 / rho
    return rho, [gathered(odd, 0) * inv] + [(level[axis] + gathered(odd, axis)) * inv for axis in (1, 2)]


def weights(blocking):
    keep = 1.0 - blocking
    own = (1.0 - OMEGA) * keep
    return 0.5 * (own + blocking), 0.5 * (own - blocking), OMEGA * keep


def collide(f0, even, odd, rho, u, blocking, want):
    k_even, k_odd, mix = weights(blocking)
    scale = mix * rho
    v = [ROOT * part for part in u]
    squares = [part * part for part in v]
    base = 1.0 - (1.0 / 3.0) * (squares[0] + squares[1] + squares[2])
    out = {}
    if 0 in want:
        out[0] = (2.0 * k_even) * f0 + (WEIGHT[0] * scale) * base
    for group in (FACES, EDGES):
        s = WEIGHT[group[0]] * scale
        s_odd = (2.0**0.5) * s
        for i in group:
            if i not in want and i + 1 not in want:
                continue
            p = project(v, i)
            square = squares[VEL[i].index(1)] if i in FACES else p * p
            p_even = k_even * even[i] + s * (base + square)
            p_odd = k_odd * odd[i] + s_odd * p
            if i in want:
                out[i] = p_even + p_odd
            if i + 1 in want:
                out[i + 1] = p_even - p_odd
    return out


def flow(b0, even, odd, u):
    base = 1.0 - 1.5 * (u[0] * u[0] + u[1] * u[1] + u[2] * u[2])
    q = [1.5 * part for part in u]
    level = [] if b0 is None else [WEIGHT[0] * b0]
    value, slope = [], [[], [], []]
    for group in (FACES, EDGES):
        group = [i for i in group if i in even]
        w = WEIGHT[group[0]]
        level.append(w * total(even[i] for i in group))
        work, along = [], {}
        for i in group:
            p = project(q, i)
            t = p * even[i]
            h = odd[i] + t
            work.append(p * h)
            along[i] = h + t
        value.append((2.0 * w) * total(work))
        for axis in range(3):
            if any(VEL[i][axis] for i in group):
                slope[axis].append((3.0 * w) * gathered(along, axis))
    level = total(level)
    return [base * level + total(value)] + [total(slope[axis]) - 2.0 * (q[axis] * level) for axis in range(3)]


def back(b0, even, odd, sums, u, blocking, want):
    energy, *v = sums
    k_even, k_odd, mix = weights(blocking)
    common = mix * (energy - (v[0] * u[0] + v[1] * u[1] + v[2] * u[2]))
    mv = [mix * v[axis] for axis in range(3)]
    out = {}
    if 0 in want:
        out[0] = (2.0 * k_even) * b0 + common
    for i in PAIRS:
        if i not in want and i + 1 not in want:
            continue
        p_even = k_even * even[i] + common
        p_odd = k_odd * odd[i] + project(mv, i)
        if i in want:
            out[i] = p_even + p_odd
        if i + 1 in want:
            out[i + 1] = p_even - p_odd
    return out


def gradient_of(b, f, rho, energy):
    evens = total(b[1][i] * f[1][i] for i in PAIRS)
    odds = total(b[2][i] * f[2][i] for i in PAIRS)
    return OMEGA * (b[0] * f[0] - rho * energy) + (0.5 * OMEGA) * evens - (1.0 - 0.5 * OMEGA) * odds


def column(shape):
    return lax.broadcasted_iota(jnp.int32, shape, len(shape) - 1)


def turn(tile, shift, axis):
    shift = shift % tile.shape[axis]
    return tile if shift == 0 else pltpu.roll(tile, shift, axis)


def moved(main, rim, i, sign):
    y, z = sign * VEL[i][1], sign * VEL[i][2]
    if y:
        main, rim = turn(main, y, 0), turn(rim, y, 0)
    if z:
        at = column(main.shape)
        edge = at == (0 if z == 1 else LANES - 1)
        main, rim = turn(main, z, 1), turn(rim, z, 1)
        main, rim = jnp.where(edge, rim, main), jnp.where(edge, main, rim)
    return main, rim


def pack_rims(ref, place, tiles, width):
    at = column((ROWS, LANES))
    joined, first = None, 0
    for k, (_, rim) in enumerate(tiles):
        piece = turn(rim(), first + width[k] // 2, 1)
        joined = piece if joined is None else jnp.where(at >= first, piece, joined)
        first += width[k]
    ref[place] = joined


def unpack_rims(tile, width, out):
    first = 0
    for k in range(len(width)):
        out(k, turn(tile, -(first + width[k] // 2), 1))
        first += width[k]


SEND1, SEND2 = 19, 14
WIDTH1 = [6] * 14 + [4] * 5
WIDTH2 = [2] * SEND2
ROWTILES2 = 2 * SEND2 + -(-SEND2 // 4)


def pack1(ref, tiles):
    for k, (main, _) in enumerate(tiles):
        ref[k] = main()
    pack_rims(ref, SEND1, tiles, WIDTH1)


def unpack1(ref, rim_ref):
    def out(k, rim):
        rim_ref[k] = rim

    unpack_rims(ref[SEND1], WIDTH1, out)


def pack2(ref, rim_ref, tiles):
    at = lax.broadcasted_iota(jnp.int32, (8, LANES), 0)
    joined = None
    for k, (main, _) in enumerate(tiles):
        tile = main()
        ref[2 * k], ref[2 * k + 1] = tile[0:8], tile[8:16]
        slot = 2 * (k % 4)
        piece = turn(tile[16:24], slot + 1, 0)
        joined = piece if slot == 0 else jnp.where(at >= slot, piece, joined)
        if slot == 6 or k == SEND2 - 1:
            ref[2 * SEND2 + k // 4] = joined
    pack_rims(rim_ref, 0, tiles, WIDTH2)
    for k in range(3):
        ref[ROWTILES2 + k] = rim_ref[0, 8 * k : 8 * k + 8, :]


def unpack2(ref, out_ref):
    for k in range(SEND2):
        out_ref[k, 0, 0:8, :] = ref[2 * k]
        out_ref[k, 0, 8:16, :] = ref[2 * k + 1]
        out_ref[k, 0, 16:24, :] = turn(ref[2 * SEND2 + k // 4], -(2 * (k % 4) + 1), 0)

    def out(k, rim):
        out_ref[k, 1] = rim

    unpack_rims(jnp.concatenate([ref[ROWTILES2 + k] for k in range(3)], axis=0), WIDTH2, out)


def call(kernel, outs, scratch=(), more=(), space=None, cost=1000):
    specs = {} if space is None else {"in_specs": [pl.BlockSpec(memory_space=s) for s in space]}
    return pl.pallas_call(
        kernel,
        out_shape=[jax.ShapeDtypeStruct(shape, jnp.float32) for shape in outs],
        scratch_shapes=[pltpu.VMEM(shape, jnp.float32) for shape in scratch] + list(more),
        compiler_params=None if INTERPRET else pltpu.CompilerParams(vmem_limit_bytes=40 * 2**20),
        cost_estimate=pl.CostEstimate(flops=cost * 2000, bytes_accessed=cost * 1000, transcendentals=0),
        interpret=INTERPRET,
        **specs,
    )


LEVEL_Y = [i for i in range(Q) if VEL[i][1] == 0][:3]
YTILES = Q + (Q + 1) // 2


def rows_moves(up):
    inwards = 1 if up else -1
    first = lambda count: OWN - count if up else 0
    fourth, third = (OWN - 4, OWN - 3) if up else (3, 2)
    out = []
    for i in range(Q):
        for layer in range(2):
            out.append((0, i, layer, first(3), 3, i, 3 * layer))
            out.append((1, i, layer, first(2), 2, Q + i // 2, 4 * (i % 2) + 2 * layer))
            if VEL[i][1] == inwards:
                out.append((0, i, layer, fourth, 1, i, 6 + layer))
            elif VEL[i][1] == -inwards:
                out.append((1, i, layer, third, 1, i, 6 + layer))
            elif i in LEVEL_Y:
                out.append((2, 0, layer, first(3) + LEVEL_Y.index(i), 1, i, 6 + layer))
    return out


def collided(f, blocking):
    even, odd = split(f)
    rho, u = moments(f[0], even, odd)
    return collide(f[0], even, odd, rho, u, blocking, range(Q))


def rows_kernel(
    f_hbm, por_hbm, solid_hbm, seed_hbm,
    up_ref, down_ref, f_ref, seed_ref, g_ref, b_ref, fluid_ref,
    por_ref, solid_ref, sems,
):
    copies = [
        pltpu.make_async_copy(src, dst, sems.at[k])
        for k, (src, dst) in enumerate(
            [(f_hbm, f_ref), (por_hbm, por_ref), (solid_hbm, solid_ref), (seed_hbm, seed_ref)]
        )
    ]
    for copy in copies:
        copy.start()
    for copy in copies[:3]:
        copy.wait()
    for layer in range(2):
        solid = solid_ref[layer] == 1
        b_ref[0, layer] = jnp.where(solid, 1.0, por_ref[layer])
        fluid_ref[layer] = jnp.where(solid, 0.0, 1.0)

        def body(row, layer=layer):
            rows = slice(row, row + 8)
            g = collided([f_ref[i, layer, rows, :] for i in range(Q)], b_ref[0, layer, rows, :])
            for i in range(Q):
                g_ref[i, layer, rows, :] = g[i]

        tiles_loop(2, body)
    copies[3].wait()
    arrays = (g_ref, seed_ref, b_ref)
    for ref, up in ((up_ref, True), (down_ref, False)):
        for which, i, layer, row, count, tile, at in rows_moves(up):
            ref[tile, at : at + count, :] = arrays[which][i, layer, row : row + count, :]


def columns_kernel(g_ref, seed_ref, b_ref, below_ref, above_ref, main_ref, up_ref, down_ref):
    for k in range(FIELDS):
        for layer in range(2):
            own = g_ref[k, layer] if k < Q else seed_ref[k - Q, layer] if k < 2 * Q else b_ref[0, layer]
            main_ref[k, layer, 0:OWN, :] = own
    for ref, up, shift in ((below_ref, True, ROWS - OWN), (above_ref, False, OWN)):
        for which, i, layer, row, count, tile, at in rows_moves(up):
            main_ref[which * Q + i, layer, row + shift : row + shift + count, :] = ref[tile, at : at + count, :]
    at = column((ROWS, LANES))
    high = low = None
    for k in range(FIELDS):
        for layer in range(2):
            tile = main_ref[k, layer]
            n = 2 * k + layer
            slot = n % 32
            piece_up, piece_down = turn(tile, 4 * slot + 4, 1), turn(tile, 4 * slot, 1)
            high = piece_up if slot == 0 else jnp.where(at >= 4 * slot, piece_up, high)
            low = piece_down if slot == 0 else jnp.where(at >= 4 * slot, piece_down, low)
            if slot == 31 or n == 2 * FIELDS - 1:
                up_ref[n // 32] = high
                down_ref[n // 32] = low


def tiles_loop(count, body):
    for n in range(count):
        body(8 * n)


def rim_of(before_ref, beyond_ref, k, layer):
    n = 2 * k + layer
    slot, tile = n % 32, n // 32
    before = turn(before_ref[tile], -(4 * slot + 4), 1)
    beyond = turn(beyond_ref[tile], -4 * slot, 1)
    return jnp.where(column((ROWS, LANES)) < RIM, beyond, before)


def first_kernel(
    main_ref, before_ref, beyond_ref,
    f1_ref, edge_ref, b_ref, up_ref, down_ref,
    level_ref, rim_ref, seed_ref,
):
    for i in range(Q):
        for layer in range(2):
            rim_ref[i, layer] = rim_of(before_ref, beyond_ref, i, layer)
    for layer, pops in ((1, XM), (0, XP)):
        for i in pops:
            seed_ref[i, 0] = rim_of(before_ref, beyond_ref, Q + i, layer)
    for layer in range(2):
        b_ref[layer, 0] = main_ref[2 * Q, layer]
        b_ref[layer, 1] = rim_of(before_ref, beyond_ref, 2 * Q, layer)
    for i in range(Q):
        for layer in range(2):
            to = layer + VEL[i][0]
            tiles = moved(main_ref[i, layer], rim_ref[i, layer], i, 1)
            for lane in range(2):
                if to in (0, 1):
                    f1_ref[i, to, lane] = tiles[lane]
                else:
                    edge_ref[i, lane] = tiles[lane]
    for layer in range(2):
        for lane in range(2):
            stay = {i: f1_ref[i, layer, lane] for i in X0}
            level_ref[0, layer, lane] = total(stay.values())
            for axis in (1, 2):
                level_ref[axis, layer, lane] = total(
                    stay[i] if VEL[i][axis] == 1 else -stay[i] for i in X0 if VEL[i][axis]
                )

    def tiles_of(forward, backward, layer):
        def pick(ref, *where):
            return (lambda: ref[where + (0,)]), (lambda: ref[where + (1,)])

        out = [pick(f1_ref, i, layer) for i in forward]
        out += [pick(level_ref, k, layer) for k in range(3)]
        out.append(pick(b_ref, layer))
        out += [pick(edge_ref, i) for i in forward]
        for i in backward:
            seed_ref[i, 0], seed_ref[i, 1] = moved(main_ref[Q + i, layer], seed_ref[i, 0], i, -1)
            out.append(pick(seed_ref, i))
        return out

    pack1(up_ref, tiles_of(XP, XM, 1))
    pack1(down_ref, tiles_of(XM, XP, 0))


def seed_kernel(main_ref, before_ref, beyond_ref, b2_ref, rim_ref):
    for i in range(Q):
        for layer in range(2):
            if layer - VEL[i][0] in (0, 1):
                rim_ref[i, layer] = rim_of(before_ref, beyond_ref, Q + i, layer)
    for i in range(Q):
        for layer in range(2):
            to = layer - VEL[i][0]
            if to in (0, 1):
                main, rim = moved(main_ref[Q + i, layer], rim_ref[i, layer], i, -1)
                b2_ref[i, to, 0] = main
                b2_ref[i, to, 1] = rim


def side_kernel(side, f1_ref, edge_ref, b_ref, got_ref, mom_ref, far_ref, bh_ref, g_ref, far_g_ref, rim_scr):
    unpack1(got_ref, rim_scr)
    got = (got_ref, rim_scr)
    theirs, ours = (XP, XM) if side == 0 else (XM, XP)
    for lane in range(2):
        bh_ref[lane] = got[lane][8]

        def near(row, lane=lane):
            rows = slice(row, row + 8)
            f = [None if i in theirs else f1_ref[i, side, lane, rows, :] for i in range(Q)]
            for k, i in enumerate(theirs):
                f[i] = got[lane][9 + k, rows, :]
            even, odd = split(f)
            rho, u = moments(f[0], even, odd)
            mom_ref[3, lane, rows, :] = rho
            for axis in range(3):
                mom_ref[axis, lane, rows, :] = u[axis]
            g = collide(f[0], even, odd, rho, u, b_ref[side, lane, rows, :], range(Q))
            for i in range(Q):
                g_ref[i, lane, rows, :] = g[i]

        def far(row, lane=lane):
            rows = slice(row, row + 8)
            f = [None] * Q
            for k, i in enumerate(theirs):
                f[i] = got[lane][k, rows, :]
            for i in ours:
                f[i] = edge_ref[i, lane, rows, :]
            even, odd = split(f, XP)
            rho, u = moments_from([got[lane][5 + k, rows, :] for k in range(3)], even, odd)
            for axis in range(3):
                far_ref[axis, lane, rows, :] = u[axis]
            g = collide(None, even, odd, rho, u, got[lane][8, rows, :], theirs)
            for i in theirs:
                far_g_ref[i, lane, rows, :] = g[i]

        tiles_loop(3, near)
        tiles_loop(3, far)


def middle_kernel(
    b_ref, b2_ref, left_ref, right_ref, mom0_ref, mom1_ref, g0_ref, g1_ref, g_left_ref, g_right_ref,
    grad_ref, b1_ref, edge1_ref, sums_ref, up_ref, down_ref,
    l_scr, r_scr, f_scr, a_scr, rim_scr,
):
    def out(scr):
        def put(k, rim):
            if k >= 14:
                scr[k] = rim

        return put

    unpack_rims(left_ref[SEND1], WIDTH1, out(l_scr))
    unpack_rims(right_ref[SEND1], WIDTH1, out(r_scr))
    got = ((left_ref, right_ref), (l_scr, r_scr))
    g_refs = (g_left_ref, g0_ref, g1_ref, g_right_ref)
    mom = (mom0_ref, mom1_ref)

    for i in range(Q):
        for layer in range(2):
            ref = g_refs[layer + 1 - VEL[i][0]]
            main, rim = moved(ref[i, 0], ref[i, 1], i, 1)
            f_scr[i, layer, 0] = main
            f_scr[i, layer, 1] = rim

    for layer in range(2):
        for lane in range(2):

            def body(row, layer=layer, lane=lane):
                rows = slice(row, row + 8)
                missing = XM if layer == 0 else XP
                f = [f_scr[i, layer, lane, rows, :] for i in range(Q)]
                b = {i: b2_ref[i, layer, lane, rows, :] for i in range(Q) if i not in missing}
                for k, i in enumerate(missing):
                    b[i] = got[lane][layer][14 + k, rows, :]
                even, odd = split(f)
                rho, u = moments(f[0], even, odd)
                b_even, b_odd = split(b)
                sums = flow(b[0], b_even, b_odd, u)
                a = back(b[0], b_even, b_odd, sums, u, b_ref[layer, lane, rows, :], range(Q))
                for i in range(Q):
                    a_scr[i, layer, lane, rows, :] = a[i]
                if lane == 0 and row < OWN:
                    grad_ref[layer, rows, :] = gradient_of((b[0], b_even, b_odd), (f[0], even, odd), rho, sums[0])

            tiles_loop(3, body)

    for i in range(Q):
        for layer in range(2):
            to = layer - VEL[i][0]
            tiles = moved(a_scr[i, layer, 0], a_scr[i, layer, 1], i, -1)
            for lane in range(2):
                if to in (0, 1):
                    b1_ref[i, to, lane] = tiles[lane]
                else:
                    edge1_ref[i, lane] = tiles[lane]

    for layer in range(2):
        for lane in range(2):

            def body(row, layer=layer, lane=lane):
                rows = slice(row, row + 8)
                missing = XM if layer == 0 else XP
                b = {i: b1_ref[i, layer, lane, rows, :] for i in range(Q) if i not in missing}
                even, odd = split(b, [i for i in PAIRS if i in X0])
                for i in XP:
                    even[i], odd[i] = (b[i], b[i]) if layer == 0 else (b[i + 1], -b[i + 1])
                sums = flow(b[0], even, odd, [mom[layer][axis, lane, rows, :] for axis in range(3)])
                for k in range(4):
                    sums_ref[k, layer, lane, rows, :] = sums[k]

            tiles_loop(3, body)

    def tiles_of(theirs, layer):
        def pick(ref, *where):
            return (lambda: ref[where + (0,)]), (lambda: ref[where + (1,)])

        return (
            [pick(edge1_ref, i) for i in theirs]
            + [pick(b1_ref, i, layer) for i in theirs]
            + [pick(sums_ref, k, layer) for k in range(4)]
        )

    pack2(up_ref, rim_scr, tiles_of(XM, 1))
    pack2(down_ref, rim_scr, tiles_of(XP, 0))


def side_back_kernel(
    side, b1_ref, edge1_ref, sums_ref, mom_ref, far_ref, b_ref, bh_ref, f1_ref, got1_ref, grad_ref, got_ref,
    out_grad_ref, a_ref, far_a_ref,
    got,
):
    unpack2(got_ref, got)
    near_pops, far_pops = (XM, XP) if side == 0 else (XP, XM)

    def halves(b, plus):
        return {i: b[i] if plus else b[i + 1] for i in XP}, {i: b[i] if plus else -b[i + 1] for i in XP}

    for lane in range(2):

        def near(row, lane=lane):
            rows = slice(row, row + 8)
            b = {i: b1_ref[i, side, lane, rows, :] for i in range(Q) if i not in near_pops}
            for k, i in enumerate(near_pops):
                b[i] = got[k, lane, rows, :]
            even, odd = split(b)
            u = [mom_ref[axis, lane, rows, :] for axis in range(3)]
            parts = flow(None, *halves(b, side == 1), u)
            sums = [sums_ref[k, side, lane, rows, :] + part for k, part in enumerate(parts)]
            a = back(b[0], even, odd, sums, u, b_ref[side, lane, rows, :], range(Q))
            for i in range(Q):
                a_ref[i, lane, rows, :] = a[i]
            if lane == 0 and row < OWN:
                f = {i: f1_ref[i, side, lane, rows, :] for i in range(Q) if i not in far_pops}
                for k, i in enumerate(far_pops):
                    f[i] = got1_ref[9 + k, rows, :]
                grad = gradient_of((b[0], even, odd), (f[0],) + split(f), mom_ref[3, lane, rows, :], sums[0])
                out_grad_ref[rows, :] = grad + grad_ref[side, rows, :]

        def far(row, lane=lane):
            rows = slice(row, row + 8)
            b = {i: edge1_ref[i, lane, rows, :] for i in far_pops}
            for k, i in enumerate(near_pops):
                b[i] = got[5 + k, lane, rows, :]
            even, odd = split(b, XP)
            u = [far_ref[axis, lane, rows, :] for axis in range(3)]
            parts = flow(None, *halves(b, side == 0), u)
            sums = [got[10 + k, lane, rows, :] + part for k, part in enumerate(parts)]
            a = back(None, even, odd, sums, u, bh_ref[lane, rows, :], near_pops)
            for i in near_pops:
                far_a_ref[i, lane, rows, :] = a[i]

        tiles_loop(3, near)
        tiles_loop(3, far)


def last_kernel(
    b_ref, grad0_ref, grad1_ref, a_left_ref, a0_ref, a1_ref, a_right_ref, f_ref, fluid_ref,
    out_grad_ref, out_ref,
    b_scr,
):
    a_refs = (a_left_ref, a0_ref, a1_ref, a_right_ref)
    grads = (grad0_ref, grad1_ref)
    for i in range(Q):
        for layer in range(2):
            ref = a_refs[layer + 1 + VEL[i][0]]
            main, _ = moved(ref[i, 0], ref[i, 1], i, -1)
            b_scr[i, layer] = main[0:OWN]

    for layer in range(2):

        def body(row, layer=layer):
            rows = slice(row, row + 8)
            f = [f_ref[i, layer, rows, :] for i in range(Q)]
            b = {i: b_scr[i, layer, rows, :] for i in range(Q)}
            even, odd = split(f)
            rho, u = moments(f[0], even, odd)
            b_even, b_odd = split(b)
            sums = flow(b[0], b_even, b_odd, u)
            a = back(b[0], b_even, b_odd, sums, u, b_ref[layer, 0, rows, :], range(Q))
            for i in range(Q):
                out_ref[i, layer, rows, :] = a[i]
            grad = gradient_of((b[0], b_even, b_odd), (f[0], even, odd), rho, sums[0]) + grads[layer][rows, :]
            out_grad_ref[layer, rows, :] = jnp.where(fluid_ref[layer, rows, :] == 0.0, 0.0, grad)

        tiles_loop(2, body)


def placed(x):
    return x if INTERPRET else pltpu.with_memory_space_constraint(x, pltpu.HBM)


def both_ways(up, down, axis):
    count = lax.axis_size(axis)
    ring = [(i, (i + 1) % count) for i in range(count)]
    return lax.ppermute(up, axis, ring), lax.ppermute(down, axis, [(j, i) for i, j in ring])


def body(populations, porosity, solid, seed_adjoint):
    half, tile = (2, 2, ROWS, LANES), (ROWS, LANES)
    inputs = [placed(x) for x in (populations, porosity, solid, seed_adjoint)]
    block = populations.shape
    cells = block[1:]
    up, down, f, seed, g, own_b, fluid = call(
        rows_kernel,
        [(YTILES, 8, LANES)] * 2 + [block, block, block, (1,) + cells, cells],
        [cells],
        [pltpu.VMEM(cells, jnp.int32), pltpu.SemaphoreType.DMA((4,))],
        space=[pltpu.HBM] * 4,
    )(*inputs)
    below, above = both_ways(up, down, "gy")
    main, up, down = call(columns_kernel, [(FIELDS, 2) + tile] + [(ZTILES,) + tile] * 2)(g, seed, own_b, below, above)
    before, beyond = both_ways(up, down, "gz")
    f1, edge, b, up, down = call(
        first_kernel,
        [(Q,) + half, (Q, 2) + tile, half] + [(SEND1 + 1,) + tile] * 2,
        [(3,) + half, (Q, 2) + tile, (Q, 2) + tile],
    )(main, before, beyond)
    left1, right1 = both_ways(up, down, "gx")
    (b2,) = call(seed_kernel, [(Q,) + half], [(Q, 2) + tile])(main, before, beyond)
    sides = []
    for side, got in enumerate((left1, right1)):
        sides.append(
            call(
                functools.partial(side_kernel, side),
                [(4, 2) + tile, (3, 2) + tile, (2,) + tile, (Q, 2) + tile, (Q, 2) + tile],
                [(SEND1,) + tile],
            )(f1, edge, b, got)
        )
    (mom0, far0, bh0, g0, g_left), (mom1, far1, bh1, g1, g_right) = sides
    grad, b1, edge1, sums, up, down = call(
        middle_kernel,
        [(2, OWN, LANES), (Q,) + half, (Q, 2) + tile, (4,) + half] + [(ROWTILES2 + 3, 8, LANES)] * 2,
        [(SEND1,) + tile] * 2 + [(Q,) + half, (Q,) + half, (1,) + tile],
    )(b, b2, left1, right1, mom0, mom1, g0, g1, g_left, g_right)
    left, right = both_ways(up, down, "gx")
    sides = []
    for side, (mom, far, bh, got1, got) in enumerate(((mom0, far0, bh0, left1, left), (mom1, far1, bh1, right1, right))):
        sides.append(
            call(
                functools.partial(side_back_kernel, side),
                [(OWN, LANES), (Q, 2) + tile, (Q, 2) + tile],
                [(SEND2, 2) + tile],
            )(b1, edge1, sums, mom, far, b, bh, f1, got1, grad, got)
        )
    (grad0, a0, a_left), (grad1, a1, a_right) = sides
    gradient, adjoint_out = call(last_kernel, [(2, OWN, LANES), (Q, 2, OWN, LANES)], [(Q, 2, OWN, LANES)])(
        b, grad0, grad1, a_left, a0, a1, a_right, f, fluid
    )
    return gradient, adjoint_out


def solution(mesh):
    field, cell = P(None, "gx", "gy", "gz"), P("gx", "gy", "gz")
    return jax.shard_map(
        body, mesh=mesh, in_specs=(field, cell, cell, field), out_specs=(cell, field), check_vma=False
    )
```

```python
import functools

import jax
import jax.numpy as jnp
from jax import lax
from jax.experimental import pallas as pl
from jax.experimental.pallas import tpu as pltpu
from jax.sharding import PartitionSpec as P

INTERPRET = False

VEL = [
    (0, 0, 0),
    (1, 0, 0), (-1, 0, 0), (0, 1, 0), (0, -1, 0), (0, 0, 1), (0, 0, -1),
    (1, 1, 0), (-1, -1, 0), (1, -1, 0), (-1, 1, 0),
    (1, 0, 1), (-1, 0, -1), (1, 0, -1), (-1, 0, 1),
    (0, 1, 1), (0, -1, -1), (0, 1, -1), (0, -1, 1),
]
OPP = [0, 2, 1, 4, 3, 6, 5, 8, 7, 10, 9, 12, 11, 14, 13, 16, 15, 18, 17]
WEIGHT = [1.0 / 3.0] + [1.0 / 18.0] * 6 + [1.0 / 36.0] * 12
OMEGA = 1.25
Q = 19
XP = [i for i in range(Q) if VEL[i][0] == 1]
X0 = [i for i in range(Q) if VEL[i][0] == 0]
XM = [i for i in range(Q) if VEL[i][0] == -1]
PAIRS = [i for i in range(1, Q, 2)]

ROWS, OWN, LANES, RIM = 24, 16, 128, 4
FIELDS = 2 * Q + 1
ZTILES = -(-2 * FIELDS // 32)


def total(terms):
    terms = list(terms)
    while len(terms) > 1:
        terms = [a + b for a, b in zip(terms[::2], terms[1::2])] + (terms[-1:] if len(terms) % 2 else [])
    return terms[0]


ROOT = 4.5**0.5
FACES = [i for i in PAIRS if i < 7]
EDGES = [i for i in PAIRS if i >= 7]


def project(vector, i):
    out = None
    for axis in range(3):
        c = VEL[i][axis]
        if c == 0:
            continue
        if out is None:
            out = vector[axis] if c == 1 else -vector[axis]
        else:
            out = out + vector[axis] if c == 1 else out - vector[axis]
    return out


def gathered(terms, axis):
    plus = [terms[i] for i in terms if VEL[i][axis] == 1]
    minus = [terms[i] for i in terms if VEL[i][axis] == -1]
    return total(plus) - total(minus) if minus else total(plus)


def split(f, pairs=PAIRS):
    return {i: f[i] + f[i + 1] for i in pairs}, {i: f[i] - f[i + 1] for i in pairs}


def moments(f0, even, odd):
    rho = f0 + total(even.values())
    inv = 1.0 / rho
    return rho, [gathered(odd, axis) * inv for axis in range(3)]


def moments_from(level, even, odd):
    rho = level[0] + total(even.values())
    inv = 1.0 / rho
    return rho, [gathered(odd, 0) * inv] + [(level[axis] + gathered(odd, axis)) * inv for axis in (1, 2)]


def weights(blocking):
    keep = 1.0 - blocking
    own = (1.0 - OMEGA) * keep
    return 0.5 * (own + blocking), 0.5 * (own - blocking), OMEGA * keep


def collide(f0, even, odd, rho, u, blocking, want):
    k_even, k_odd, mix = weights(blocking)
    scale = mix * rho
    v = [ROOT * part for part in u]
    squares = [part * part for part in v]
    base = 1.0 - (1.0 / 3.0) * (squares[0] + squares[1] + squares[2])
    out = {}
    if 0 in want:
        out[0] = (2.0 * k_even) * f0 + (WEIGHT[0] * scale) * base
    for group in (FACES, EDGES):
        s = WEIGHT[group[0]] * scale
        s_odd = (2.0**0.5) * s
        for i in group:
            if i not in want and i + 1 not in want:
                continue
            p = project(v, i)
            square = squares[VEL[i].index(1)] if i in FACES else p * p
            p_even = k_even * even[i] + s * (base + square)
            p_odd = k_odd * odd[i] + s_odd * p
            if i in want:
                out[i] = p_even + p_odd
            if i + 1 in want:
                out[i + 1] = p_even - p_odd
    return out


def flow(b0, even, odd, u):
    base = 1.0 - 1.5 * (u[0] * u[0] + u[1] * u[1] + u[2] * u[2])
    q = [1.5 * part for part in u]
    level = [] if b0 is None else [WEIGHT[0] * b0]
    value, slope = [], [[], [], []]
    for group in (FACES, EDGES):
        group = [i for i in group if i in even]
        w = WEIGHT[group[0]]
        level.append(w * total(even[i] for i in group))
        work, along = [], {}
        for i in group:
            p = project(q, i)
            t = p * even[i]
            h = odd[i] + t
            work.append(p * h)
            along[i] = h + t
        value.append((2.0 * w) * total(work))
        for axis in range(3):
            if any(VEL[i][axis] for i in group):
                slope[axis].append((3.0 * w) * gathered(along, axis))
    level = total(level)
    return [base * level + total(value)] + [total(slope[axis]) - 2.0 * (q[axis] * level) for axis in range(3)]


def back(b0, even, odd, sums, u, blocking, want):
    energy, *v = sums
    k_even, k_odd, mix = weights(blocking)
    common = mix * (energy - (v[0] * u[0] + v[1] * u[1] + v[2] * u[2]))
    mv = [mix * v[axis] for axis in range(3)]
    out = {}
    if 0 in want:
        out[0] = (2.0 * k_even) * b0 + common
    for i in PAIRS:
        if i not in want and i + 1 not in want:
            continue
        p_even = k_even * even[i] + common
        p_odd = k_odd * odd[i] + project(mv, i)
        if i in want:
            out[i] = p_even + p_odd
        if i + 1 in want:
            out[i + 1] = p_even - p_odd
    return out


def gradient_of(b, f, rho, energy):
    evens = total(b[1][i] * f[1][i] for i in PAIRS)
    odds = total(b[2][i] * f[2][i] for i in PAIRS)
    return OMEGA * (b[0] * f[0] - rho * energy) + (0.5 * OMEGA) * evens - (1.0 - 0.5 * OMEGA) * odds


def column(shape):
    return lax.broadcasted_iota(jnp.int32, shape, len(shape) - 1)


def turn(tile, shift, axis):
    shift = shift % tile.shape[axis]
    return tile if shift == 0 else pltpu.roll(tile, shift, axis)


def moved(main, rim, i, sign):
    y, z = sign * VEL[i][1], sign * VEL[i][2]
    if y:
        main, rim = turn(main, y, 0), turn(rim, y, 0)
    if z:
        at = column(main.shape)
        edge = at == (0 if z == 1 else LANES - 1)
        main, rim = turn(main, z, 1), turn(rim, z, 1)
        main, rim = jnp.where(edge, rim, main), jnp.where(edge, main, rim)
    return main, rim


def packed_rims(tiles, width):
    at = column((ROWS, LANES))
    joined, first = None, 0
    for k, (_, rim) in enumerate(tiles):
        piece = turn(rim(), first + width[k] // 2, 1)
        joined = piece if joined is None else jnp.where(at >= first, piece, joined)
        first += width[k]
    return joined


def unpack_rims(tile, width, out):
    first = 0
    for k in range(len(width)):
        out(k, turn(tile, -(first + width[k] // 2), 1))
        first += width[k]


SEND1, SEND2 = 19, 14
WIDTH1 = [6] * 14 + [4] * 5
WIDTH2 = [2] * SEND2
ROWTILES2 = 2 * SEND2 + -(-SEND2 // 4)


STRIPS1 = [sum(WIDTH1[:k]) + OWN * SEND1 for k in range(SEND1 + 1)]


def pack1(ref, tiles):
    for k, (main, _) in enumerate(tiles):
        tile, half, at = main(), WIDTH1[k] // 2, STRIPS1[k]
        ref[OWN * k : OWN * k + OWN, :] = tile[0:OWN]
        ref[at : at + half, :] = tile[ROWS - half : ROWS]
        ref[at + half : at + 2 * half, :] = tile[OWN : OWN + half]
    ref[STRIPS1[-1] : STRIPS1[-1] + ROWS, :] = packed_rims(tiles, WIDTH1)


def unpack1(ref, beyond_ref, rim_ref, first=0):
    for k in range(first, SEND1):
        half, at = WIDTH1[k] // 2, STRIPS1[k]
        beyond_ref[k, 8 - half : 8, :] = ref[at : at + half, :]
        beyond_ref[k, 0:half, :] = ref[at + half : at + 2 * half, :]

    def out(k, rim):
        if k >= first:
            rim_ref[k] = rim

    unpack_rims(ref[STRIPS1[-1] : STRIPS1[-1] + ROWS, :], WIDTH1, out)

    def tile(k, lane, row):
        if lane:
            return rim_ref[k, row : row + 8, :]
        return ref[OWN * k + row : OWN * k + row + 8, :] if row < OWN else beyond_ref[k]

    return tile


def pack2(ref, rim_ref, tiles):
    at = lax.broadcasted_iota(jnp.int32, (8, LANES), 0)
    joined = None
    for k, (main, _) in enumerate(tiles):
        tile = main()
        ref[2 * k], ref[2 * k + 1] = tile[0:8], tile[8:16]
        slot = 2 * (k % 4)
        piece = turn(tile[16:24], slot + 1, 0)
        joined = piece if slot == 0 else jnp.where(at >= slot, piece, joined)
        if slot == 6 or k == SEND2 - 1:
            ref[2 * SEND2 + k // 4] = joined
    rim_ref[0] = packed_rims(tiles, WIDTH2)
    for k in range(3):
        ref[ROWTILES2 + k] = rim_ref[0, 8 * k : 8 * k + 8, :]


def unpack2(ref, out_ref):
    for k in range(SEND2):
        out_ref[k, 0, 0:8, :] = ref[2 * k]
        out_ref[k, 0, 8:16, :] = ref[2 * k + 1]
        out_ref[k, 0, 16:24, :] = turn(ref[2 * SEND2 + k // 4], -(2 * (k % 4) + 1), 0)

    def out(k, rim):
        out_ref[k, 1] = rim

    unpack_rims(jnp.concatenate([ref[ROWTILES2 + k] for k in range(3)], axis=0), WIDTH2, out)


def call(kernel, outs, scratch=(), more=(), space=None, cost=1000):
    specs = {} if space is None else {"in_specs": [pl.BlockSpec(memory_space=s) for s in space]}
    return pl.pallas_call(
        kernel,
        out_shape=[jax.ShapeDtypeStruct(shape, jnp.float32) for shape in outs],
        scratch_shapes=[pltpu.VMEM(shape, jnp.float32) for shape in scratch] + list(more),
        compiler_params=None if INTERPRET else pltpu.CompilerParams(vmem_limit_bytes=40 * 2**20),
        cost_estimate=pl.CostEstimate(flops=cost * 2000, bytes_accessed=cost * 1000, transcendentals=0),
        interpret=INTERPRET,
        **specs,
    )


LEVEL_Y = [i for i in range(Q) if VEL[i][1] == 0][:3]
YTILES = Q + (Q + 1) // 2


def rows_moves(up):
    inwards = 1 if up else -1
    first = lambda count: OWN - count if up else 0
    fourth, third = (OWN - 4, OWN - 3) if up else (3, 2)
    out = []
    for i in range(Q):
        for layer in range(2):
            out.append((0, i, layer, first(3), 3, i, 3 * layer))
            out.append((1, i, layer, first(2), 2, Q + i // 2, 4 * (i % 2) + 2 * layer))
            if VEL[i][1] == inwards:
                out.append((0, i, layer, fourth, 1, i, 6 + layer))
            elif VEL[i][1] == -inwards:
                out.append((1, i, layer, third, 1, i, 6 + layer))
            elif i in LEVEL_Y:
                out.append((2, 0, layer, first(3) + LEVEL_Y.index(i), 1, i, 6 + layer))
    return out


def collided(f, blocking):
    even, odd = split(f)
    rho, u = moments(f[0], even, odd)
    return collide(f[0], even, odd, rho, u, blocking, range(Q))


def rows_kernel(
    f_hbm, por_hbm, solid_hbm, seed_hbm,
    up_ref, down_ref, f_ref, seed_ref, g_ref, b_ref, fluid_ref,
    por_ref, solid_ref, sems,
):
    copies = [
        pltpu.make_async_copy(src, dst, sems.at[k])
        for k, (src, dst) in enumerate(
            [(f_hbm, f_ref), (por_hbm, por_ref), (solid_hbm, solid_ref), (seed_hbm, seed_ref)]
        )
    ]
    for copy in copies:
        copy.start()
    for copy in copies[:3]:
        copy.wait()
    for layer in range(2):
        solid = solid_ref[layer] == 1
        b_ref[0, layer] = jnp.where(solid, 1.0, por_ref[layer])
        fluid_ref[layer] = jnp.where(solid, 0.0, 1.0)

        def body(row, layer=layer):
            rows = slice(row, row + 8)
            g = collided([f_ref[i, layer, rows, :] for i in range(Q)], b_ref[0, layer, rows, :])
            for i in range(Q):
                g_ref[i, layer, rows, :] = g[i]

        tiles_loop(2, body)
    copies[3].wait()
    arrays = (g_ref, seed_ref, b_ref)
    for ref, up in ((up_ref, True), (down_ref, False)):
        for which, i, layer, row, count, tile, at in rows_moves(up):
            ref[tile, at : at + count, :] = arrays[which][i, layer, row : row + count, :]


def columns_kernel(g_ref, seed_ref, b_ref, below_ref, above_ref, main_ref, up_ref, down_ref):
    for k in range(FIELDS):
        for layer in range(2):
            own = g_ref[k, layer] if k < Q else seed_ref[k - Q, layer] if k < 2 * Q else b_ref[0, layer]
            main_ref[k, layer, 0:OWN, :] = own
    for ref, up, shift in ((below_ref, True, ROWS - OWN), (above_ref, False, OWN)):
        for which, i, layer, row, count, tile, at in rows_moves(up):
            main_ref[which * Q + i, layer, row + shift : row + shift + count, :] = ref[tile, at : at + count, :]
    at = column((ROWS, LANES))
    high = low = None
    for k in range(FIELDS):
        for layer in range(2):
            tile = main_ref[k, layer]
            n = 2 * k + layer
            slot = n % 32
            piece_up, piece_down = turn(tile, 4 * slot + 4, 1), turn(tile, 4 * slot, 1)
            high = piece_up if slot == 0 else jnp.where(at >= 4 * slot, piece_up, high)
            low = piece_down if slot == 0 else jnp.where(at >= 4 * slot, piece_down, low)
            if slot == 31 or n == 2 * FIELDS - 1:
                up_ref[n // 32] = high
                down_ref[n // 32] = low


def tiles_loop(count, body):
    for n in range(count):
        body(8 * n)


def rim_of(before_ref, beyond_ref, k, layer):
    n = 2 * k + layer
    slot, tile = n % 32, n // 32
    before = turn(before_ref[tile], -(4 * slot + 4), 1)
    beyond = turn(beyond_ref[tile], -4 * slot, 1)
    return jnp.where(column((ROWS, LANES)) < RIM, beyond, before)


def first_kernel(
    main_ref, before_ref, beyond_ref,
    f1_ref, edge_ref, b_ref, up_ref, down_ref,
    level_ref, rim_ref, seed_ref,
):
    for i in range(Q):
        for layer in range(2):
            rim_ref[i, layer] = rim_of(before_ref, beyond_ref, i, layer)
    for layer, pops in ((1, XM), (0, XP)):
        for i in pops:
            seed_ref[i, 0] = rim_of(before_ref, beyond_ref, Q + i, layer)
    for layer in range(2):
        b_ref[layer, 0] = main_ref[2 * Q, layer]
        b_ref[layer, 1] = rim_of(before_ref, beyond_ref, 2 * Q, layer)
    for i in range(Q):
        for layer in range(2):
            to = layer + VEL[i][0]
            tiles = moved(main_ref[i, layer], rim_ref[i, layer], i, 1)
            for lane in range(2):
                if to in (0, 1):
                    f1_ref[i, to, lane] = tiles[lane]
                else:
                    edge_ref[i, lane] = tiles[lane]
    for layer in range(2):
        for lane in range(2):
            stay = {i: f1_ref[i, layer, lane] for i in X0}
            level_ref[0, layer, lane] = total(stay.values())
            for axis in (1, 2):
                level_ref[axis, layer, lane] = total(
                    stay[i] if VEL[i][axis] == 1 else -stay[i] for i in X0 if VEL[i][axis]
                )

    def tiles_of(forward, backward, layer):
        def pick(ref, *where):
            return (lambda: ref[where + (0,)]), (lambda: ref[where + (1,)])

        out = [pick(f1_ref, i, layer) for i in forward]
        out += [pick(level_ref, k, layer) for k in range(3)]
        out.append(pick(b_ref, layer))
        out += [pick(edge_ref, i) for i in forward]
        for i in backward:
            seed_ref[i, 0], seed_ref[i, 1] = moved(main_ref[Q + i, layer], seed_ref[i, 0], i, -1)
            out.append(pick(seed_ref, i))
        return out

    pack1(up_ref, tiles_of(XP, XM, 1))
    pack1(down_ref, tiles_of(XM, XP, 0))


def seed_kernel(main_ref, before_ref, beyond_ref, b2_ref, rim_ref):
    for i in range(Q):
        for layer in range(2):
            if layer - VEL[i][0] in (0, 1):
                rim_ref[i, layer] = rim_of(before_ref, beyond_ref, Q + i, layer)
    for i in range(Q):
        for layer in range(2):
            to = layer - VEL[i][0]
            if to in (0, 1):
                main, rim = moved(main_ref[Q + i, layer], rim_ref[i, layer], i, -1)
                b2_ref[i, to, 0] = main
                b2_ref[i, to, 1] = rim


def side_kernel(side, f1_ref, edge_ref, b_ref, got_ref, mom_ref, far_ref, bh_ref, g_ref, far_g_ref, beyond_scr, rim_scr):
    got = unpack1(got_ref, beyond_scr, rim_scr)
    theirs, ours = (XP, XM) if side == 0 else (XM, XP)
    for lane in range(2):
        def near(row, lane=lane):
            rows = slice(row, row + 8)
            f = [None if i in theirs else f1_ref[i, side, lane, rows, :] for i in range(Q)]
            for k, i in enumerate(theirs):
                f[i] = got(9 + k, lane, row)
            even, odd = split(f)
            rho, u = moments(f[0], even, odd)
            mom_ref[3, lane, rows, :] = rho
            for axis in range(3):
                mom_ref[axis, lane, rows, :] = u[axis]
            g = collide(f[0], even, odd, rho, u, b_ref[side, lane, rows, :], range(Q))
            for i in range(Q):
                g_ref[i, lane, rows, :] = g[i]

        def far(row, lane=lane):
            rows = slice(row, row + 8)
            f = [None] * Q
            for k, i in enumerate(theirs):
                f[i] = got(k, lane, row)
            for i in ours:
                f[i] = edge_ref[i, lane, rows, :]
            even, odd = split(f, XP)
            rho, u = moments_from([got(5 + k, lane, row) for k in range(3)], even, odd)
            for axis in range(3):
                far_ref[axis, lane, rows, :] = u[axis]
            blocking = got(8, lane, row)
            bh_ref[lane, rows, :] = blocking
            g = collide(None, even, odd, rho, u, blocking, theirs)
            for i in theirs:
                far_g_ref[i, lane, rows, :] = g[i]

        tiles_loop(3, near)
        tiles_loop(3, far)


def middle_kernel(
    b_ref, b2_ref, left_ref, right_ref, mom0_ref, mom1_ref, g0_ref, g1_ref, g_left_ref, g_right_ref,
    grad_ref, b1_ref, edge1_ref, sums_ref, up_ref, down_ref,
    l_beyond, l_scr, r_beyond, r_scr, f_scr, a_scr, rim_scr,
):
    got = (unpack1(left_ref, l_beyond, l_scr, 14), unpack1(right_ref, r_beyond, r_scr, 14))
    g_refs = (g_left_ref, g0_ref, g1_ref, g_right_ref)
    mom = (mom0_ref, mom1_ref)

    for i in range(Q):
        for layer in range(2):
            ref = g_refs[layer + 1 - VEL[i][0]]
            main, rim = moved(ref[i, 0], ref[i, 1], i, 1)
            f_scr[i, layer, 0] = main
            f_scr[i, layer, 1] = rim

    for layer in range(2):
        for lane in range(2):

            def body(row, layer=layer, lane=lane):
                rows = slice(row, row + 8)
                missing = XM if layer == 0 else XP
                f = [f_scr[i, layer, lane, rows, :] for i in range(Q)]
                b = {i: b2_ref[i, layer, lane, rows, :] for i in range(Q) if i not in missing}
                for k, i in enumerate(missing):
                    b[i] = got[layer](14 + k, lane, row)
                even, odd = split(f)
                rho, u = moments(f[0], even, odd)
                b_even, b_odd = split(b)
                sums = flow(b[0], b_even, b_odd, u)
                a = back(b[0], b_even, b_odd, sums, u, b_ref[layer, lane, rows, :], range(Q))
                for i in range(Q):
                    a_scr[i, layer, lane, rows, :] = a[i]
                if lane == 0 and row < OWN:
                    grad_ref[layer, rows, :] = gradient_of((b[0], b_even, b_odd), (f[0], even, odd), rho, sums[0])

            tiles_loop(3, body)

    for i in range(Q):
        for layer in range(2):
            to = layer - VEL[i][0]
            tiles = moved(a_scr[i, layer, 0], a_scr[i, layer, 1], i, -1)
            for lane in range(2):
                if to in (0, 1):
                    b1_ref[i, to, lane] = tiles[lane]
                else:
                    edge1_ref[i, lane] = tiles[lane]

    for layer in range(2):
        for lane in range(2):

            def body(row, layer=layer, lane=lane):
                rows = slice(row, row + 8)
                missing = XM if layer == 0 else XP
                b = {i: b1_ref[i, layer, lane, rows, :] for i in range(Q) if i not in missing}
                even, odd = split(b, [i for i in PAIRS if i in X0])
                for i in XP:
                    even[i], odd[i] = (b[i], b[i]) if layer == 0 else (b[i + 1], -b[i + 1])
                sums = flow(b[0], even, odd, [mom[layer][axis, lane, rows, :] for axis in range(3)])
                for k in range(4):
                    sums_ref[k, layer, lane, rows, :] = sums[k]

            tiles_loop(3, body)

    def tiles_of(theirs, layer):
        def pick(ref, *where):
            return (lambda: ref[where + (0,)]), (lambda: ref[where + (1,)])

        return (
            [pick(edge1_ref, i) for i in theirs]
            + [pick(b1_ref, i, layer) for i in theirs]
            + [pick(sums_ref, k, layer) for k in range(4)]
        )

    pack2(up_ref, rim_scr, tiles_of(XM, 1))
    pack2(down_ref, rim_scr, tiles_of(XP, 0))


def side_back_kernel(
    side, b1_ref, edge1_ref, sums_ref, mom_ref, far_ref, b_ref, bh_ref, f1_ref, got1_ref, grad_ref, got_ref,
    out_grad_ref, a_ref, far_a_ref,
    got,
):
    unpack2(got_ref, got)
    near_pops, far_pops = (XM, XP) if side == 0 else (XP, XM)

    def halves(b, plus):
        return {i: b[i] if plus else b[i + 1] for i in XP}, {i: b[i] if plus else -b[i + 1] for i in XP}

    for lane in range(2):

        def near(row, lane=lane):
            rows = slice(row, row + 8)
            b = {i: b1_ref[i, side, lane, rows, :] for i in range(Q) if i not in near_pops}
            for k, i in enumerate(near_pops):
                b[i] = got[k, lane, rows, :]
            even, odd = split(b)
            u = [mom_ref[axis, lane, rows, :] for axis in range(3)]
            parts = flow(None, *halves(b, side == 1), u)
            sums = [sums_ref[k, side, lane, rows, :] + part for k, part in enumerate(parts)]
            a = back(b[0], even, odd, sums, u, b_ref[side, lane, rows, :], range(Q))
            for i in range(Q):
                a_ref[i, lane, rows, :] = a[i]
            if lane == 0 and row < OWN:
                f = {i: f1_ref[i, side, lane, rows, :] for i in range(Q) if i not in far_pops}
                for k, i in enumerate(far_pops):
                    f[i] = got1_ref[OWN * (9 + k) + row : OWN * (9 + k) + row + 8, :]
                grad = gradient_of((b[0], even, odd), (f[0],) + split(f), mom_ref[3, lane, rows, :], sums[0])
                out_grad_ref[rows, :] = grad + grad_ref[side, rows, :]

        def far(row, lane=lane):
            rows = slice(row, row + 8)
            b = {i: edge1_ref[i, lane, rows, :] for i in far_pops}
            for k, i in enumerate(near_pops):
                b[i] = got[5 + k, lane, rows, :]
            even, odd = split(b, XP)
            u = [far_ref[axis, lane, rows, :] for axis in range(3)]
            parts = flow(None, *halves(b, side == 0), u)
            sums = [got[10 + k, lane, rows, :] + part for k, part in enumerate(parts)]
            a = back(None, even, odd, sums, u, bh_ref[lane, rows, :], near_pops)
            for i in near_pops:
                far_a_ref[i, lane, rows, :] = a[i]

        tiles_loop(3, near)
        tiles_loop(3, far)


def last_kernel(
    b_ref, grad0_ref, grad1_ref, a_left_ref, a0_ref, a1_ref, a_right_ref, f_ref, fluid_ref,
    out_grad_ref, out_ref,
    b_scr,
):
    a_refs = (a_left_ref, a0_ref, a1_ref, a_right_ref)
    grads = (grad0_ref, grad1_ref)
    for i in range(Q):
        for layer in range(2):
            ref = a_refs[layer + 1 + VEL[i][0]]
            main, _ = moved(ref[i, 0], ref[i, 1], i, -1)
            b_scr[i, layer] = main[0:OWN]

    for layer in range(2):

        def body(row, layer=layer):
            rows = slice(row, row + 8)
            f = [f_ref[i, layer, rows, :] for i in range(Q)]
            b = {i: b_scr[i, layer, rows, :] for i in range(Q)}
            even, odd = split(f)
            rho, u = moments(f[0], even, odd)
            b_even, b_odd = split(b)
            sums = flow(b[0], b_even, b_odd, u)
            a = back(b[0], b_even, b_odd, sums, u, b_ref[layer, 0, rows, :], range(Q))
            for i in range(Q):
                out_ref[i, layer, rows, :] = a[i]
            grad = gradient_of((b[0], b_even, b_odd), (f[0], even, odd), rho, sums[0]) + grads[layer][rows, :]
            out_grad_ref[layer, rows, :] = jnp.where(fluid_ref[layer, rows, :] == 0.0, 0.0, grad)

        tiles_loop(2, body)


def placed(x):
    return x if INTERPRET else pltpu.with_memory_space_constraint(x, pltpu.HBM)


def both_ways(up, down, axis):
    count = lax.axis_size(axis)
    ring = [(i, (i + 1) % count) for i in range(count)]
    return lax.ppermute(up, axis, ring), lax.ppermute(down, axis, [(j, i) for i, j in ring])


def body(populations, porosity, solid, seed_adjoint):
    half, tile = (2, 2, ROWS, LANES), (ROWS, LANES)
    inputs = [placed(x) for x in (populations, porosity, solid, seed_adjoint)]
    block = populations.shape
    cells = block[1:]
    up, down, f, seed, g, own_b, fluid = call(
        rows_kernel,
        [(YTILES, 8, LANES)] * 2 + [block, block, block, (1,) + cells, cells],
        [cells],
        [pltpu.VMEM(cells, jnp.int32), pltpu.SemaphoreType.DMA((4,))],
        space=[pltpu.HBM] * 4,
    )(*inputs)
    below, above = both_ways(up, down, "gy")
    main, up, down = call(columns_kernel, [(FIELDS, 2) + tile] + [(ZTILES,) + tile] * 2)(g, seed, own_b, below, above)
    before, beyond = both_ways(up, down, "gz")
    f1, edge, b, up, down = call(
        first_kernel,
        [(Q,) + half, (Q, 2) + tile, half] + [(STRIPS1[-1] + ROWS, LANES)] * 2,
        [(3,) + half, (Q, 2) + tile, (Q, 2) + tile],
    )(main, before, beyond)
    left1, right1 = both_ways(up, down, "gx")
    (b2,) = call(seed_kernel, [(Q,) + half], [(Q, 2) + tile])(main, before, beyond)
    sides = []
    for side, got in enumerate((left1, right1)):
        sides.append(
            call(
                functools.partial(side_kernel, side),
                [(4, 2) + tile, (3, 2) + tile, (2,) + tile, (Q, 2) + tile, (Q, 2) + tile],
                [(SEND1, 8, LANES), (SEND1,) + tile],
            )(f1, edge, b, got)
        )
    (mom0, far0, bh0, g0, g_left), (mom1, far1, bh1, g1, g_right) = sides
    grad, b1, edge1, sums, up, down = call(
        middle_kernel,
        [(2, OWN, LANES), (Q,) + half, (Q, 2) + tile, (4,) + half] + [(ROWTILES2 + 3, 8, LANES)] * 2,
        [(SEND1, 8, LANES), (SEND1,) + tile] * 2 + [(Q,) + half, (Q,) + half, (1,) + tile],
    )(b, b2, left1, right1, mom0, mom1, g0, g1, g_left, g_right)
    left, right = both_ways(up, down, "gx")
    sides = []
    for side, (mom, far, bh, got1, got) in enumerate(((mom0, far0, bh0, left1, left), (mom1, far1, bh1, right1, right))):
        sides.append(
            call(
                functools.partial(side_back_kernel, side),
                [(OWN, LANES), (Q, 2) + tile, (Q, 2) + tile],
                [(SEND2, 2) + tile],
            )(b1, edge1, sums, mom, far, b, bh, f1, got1, grad, got)
        )
    (grad0, a0, a_left), (grad1, a1, a_right) = sides
    gradient, adjoint_out = call(last_kernel, [(2, OWN, LANES), (Q, 2, OWN, LANES)], [(Q, 2, OWN, LANES)])(
        b, grad0, grad1, a_left, a0, a1, a_right, f, fluid
    )
    return gradient, adjoint_out


def solution(mesh):
    field, cell = P(None, "gx", "gy", "gz"), P("gx", "gy", "gz")
    return jax.shard_map(
        body, mesh=mesh, in_specs=(field, cell, cell, field), out_specs=(cell, field), check_vma=False
    )
```

```python
import functools

import jax
import jax.numpy as jnp
from jax import lax
from jax.experimental import pallas as pl
from jax.experimental.pallas import tpu as pltpu
from jax.sharding import PartitionSpec as P

INTERPRET = False

VEL = [
    (0, 0, 0),
    (1, 0, 0), (-1, 0, 0), (0, 1, 0), (0, -1, 0), (0, 0, 1), (0, 0, -1),
    (1, 1, 0), (-1, -1, 0), (1, -1, 0), (-1, 1, 0),
    (1, 0, 1), (-1, 0, -1), (1, 0, -1), (-1, 0, 1),
    (0, 1, 1), (0, -1, -1), (0, 1, -1), (0, -1, 1),
]
OPP = [0, 2, 1, 4, 3, 6, 5, 8, 7, 10, 9, 12, 11, 14, 13, 16, 15, 18, 17]
WEIGHT = [1.0 / 3.0] + [1.0 / 18.0] * 6 + [1.0 / 36.0] * 12
OMEGA = 1.25
Q = 19
XP = [i for i in range(Q) if VEL[i][0] == 1]
X0 = [i for i in range(Q) if VEL[i][0] == 0]
XM = [i for i in range(Q) if VEL[i][0] == -1]
PAIRS = [i for i in range(1, Q, 2)]

ROWS, OWN, LANES, RIM = 24, 16, 128, 4
FIELDS = 2 * Q + 1
ZTILES = -(-2 * FIELDS // 32)


def total(terms):
    terms = list(terms)
    while len(terms) > 1:
        terms = [a + b for a, b in zip(terms[::2], terms[1::2])] + (terms[-1:] if len(terms) % 2 else [])
    return terms[0]


ROOT = 4.5**0.5
FACES = [i for i in PAIRS if i < 7]
EDGES = [i for i in PAIRS if i >= 7]


def project(vector, i):
    out = None
    for axis in range(3):
        c = VEL[i][axis]
        if c == 0:
            continue
        if out is None:
            out = vector[axis] if c == 1 else -vector[axis]
        else:
            out = out + vector[axis] if c == 1 else out - vector[axis]
    return out


def gathered(terms, axis):
    plus = [terms[i] for i in terms if VEL[i][axis] == 1]
    minus = [terms[i] for i in terms if VEL[i][axis] == -1]
    return total(plus) - total(minus) if minus else total(plus)


def split(f, pairs=PAIRS):
    return {i: f[i] + f[i + 1] for i in pairs}, {i: f[i] - f[i + 1] for i in pairs}


def moments(f0, even, odd):
    rho = f0 + total(even.values())
    inv = 1.0 / rho
    return rho, [gathered(odd, axis) * inv for axis in range(3)]


def moments_from(level, even, odd):
    rho = level[0] + total(even.values())
    inv = 1.0 / rho
    return rho, [gathered(odd, 0) * inv] + [(level[axis] + gathered(odd, axis)) * inv for axis in (1, 2)]


def weights(blocking):
    keep = 1.0 - blocking
    own = (1.0 - OMEGA) * keep
    return 0.5 * (own + blocking), 0.5 * (own - blocking), OMEGA * keep


def collide(f0, even, odd, rho, u, blocking, want):
    k_even, k_odd, mix = weights(blocking)
    scale = mix * rho
    v = [ROOT * part for part in u]
    squares = [part * part for part in v]
    base = 1.0 - (1.0 / 3.0) * (squares[0] + squares[1] + squares[2])
    out = {}
    if 0 in want:
        out[0] = (2.0 * k_even) * f0 + (WEIGHT[0] * scale) * base
    for group in (FACES, EDGES):
        s = WEIGHT[group[0]] * scale
        s_odd = (2.0**0.5) * s
        for i in group:
            if i not in want and i + 1 not in want:
                continue
            p = project(v, i)
            square = squares[VEL[i].index(1)] if i in FACES else p * p
            p_even = k_even * even[i] + s * (base + square)
            p_odd = k_odd * odd[i] + s_odd * p
            if i in want:
                out[i] = p_even + p_odd
            if i + 1 in want:
                out[i + 1] = p_even - p_odd
    return out


def flow(b0, even, odd, u):
    base = 1.0 - 1.5 * (u[0] * u[0] + u[1] * u[1] + u[2] * u[2])
    q = [1.5 * part for part in u]
    level = [] if b0 is None else [WEIGHT[0] * b0]
    value, slope = [], [[], [], []]
    for group in (FACES, EDGES):
        group = [i for i in group if i in even]
        w = WEIGHT[group[0]]
        level.append(w * total(even[i] for i in group))
        work, along = [], {}
        for i in group:
            p = project(q, i)
            t = p * even[i]
            h = odd[i] + t
            work.append(p * h)
            along[i] = h + t
        value.append((2.0 * w) * total(work))
        for axis in range(3):
            if any(VEL[i][axis] for i in group):
                slope[axis].append((3.0 * w) * gathered(along, axis))
    level = total(level)
    return [base * level + total(value)] + [total(slope[axis]) - 2.0 * (q[axis] * level) for axis in range(3)]


def back(b0, even, odd, sums, u, blocking, want):
    energy, *v = sums
    k_even, k_odd, mix = weights(blocking)
    common = mix * (energy - (v[0] * u[0] + v[1] * u[1] + v[2] * u[2]))
    mv = [mix * v[axis] for axis in range(3)]
    out = {}
    if 0 in want:
        out[0] = (2.0 * k_even) * b0 + common
    for i in PAIRS:
        if i not in want and i + 1 not in want:
            continue
        p_even = k_even * even[i] + common
        p_odd = k_odd * odd[i] + project(mv, i)
        if i in want:
            out[i] = p_even + p_odd
        if i + 1 in want:
            out[i + 1] = p_even - p_odd
    return out


def gradient_of(b, f, rho, energy):
    evens = total(b[1][i] * f[1][i] for i in PAIRS)
    odds = total(b[2][i] * f[2][i] for i in PAIRS)
    return OMEGA * (b[0] * f[0] - rho * energy) + (0.5 * OMEGA) * evens - (1.0 - 0.5 * OMEGA) * odds


def column(shape):
    return lax.broadcasted_iota(jnp.int32, shape, len(shape) - 1)


def turn(tile, shift, axis):
    shift = shift % tile.shape[axis]
    return tile if shift == 0 else pltpu.roll(tile, shift, axis)


def moved(main, rim, i, sign):
    y, z = sign * VEL[i][1], sign * VEL[i][2]
    if y:
        main, rim = turn(main, y, 0), turn(rim, y, 0)
    if z:
        at = column(main.shape)
        edge = at == (0 if z == 1 else LANES - 1)
        main, rim = turn(main, z, 1), turn(rim, z, 1)
        main, rim = jnp.where(edge, rim, main), jnp.where(edge, main, rim)
    return main, rim


def packed_rims(tiles, width):
    at = column((ROWS, LANES))
    joined, first = None, 0
    for k, (_, rim) in enumerate(tiles):
        piece = turn(rim(), first + width[k] // 2, 1)
        joined = piece if joined is None else jnp.where(at >= first, piece, joined)
        first += width[k]
    return joined


def unpack_rims(tile, width, out):
    first = 0
    for k in range(len(width)):
        out(k, turn(tile, -(first + width[k] // 2), 1))
        first += width[k]


SEND1, SEND2 = 19, 14
WIDTH1 = [6] * 14 + [4] * 5
WIDTH2 = [2] * SEND2
ROWTILES2 = 2 * SEND2 + -(-SEND2 // 4)


STRIPS1 = [sum(WIDTH1[:k]) + OWN * SEND1 for k in range(SEND1 + 1)]


def pack1(ref, tiles):
    for k, (main, _) in enumerate(tiles):
        tile, half, at = main(), WIDTH1[k] // 2, STRIPS1[k]
        ref[OWN * k : OWN * k + OWN, :] = tile[0:OWN]
        ref[at : at + half, :] = tile[ROWS - half : ROWS]
        ref[at + half : at + 2 * half, :] = tile[OWN : OWN + half]
    ref[STRIPS1[-1] : STRIPS1[-1] + ROWS, :] = packed_rims(tiles, WIDTH1)


def unpack1(ref, beyond_ref, rim_ref, first=0):
    for k in range(first, SEND1):
        half, at = WIDTH1[k] // 2, STRIPS1[k]
        beyond_ref[k, 8 - half : 8, :] = ref[at : at + half, :]
        beyond_ref[k, 0:half, :] = ref[at + half : at + 2 * half, :]

    def out(k, rim):
        if k >= first:
            rim_ref[k] = rim

    unpack_rims(ref[STRIPS1[-1] : STRIPS1[-1] + ROWS, :], WIDTH1, out)

    def tile(k, lane, row):
        if lane:
            return rim_ref[k, row : row + 8, :]
        return ref[OWN * k + row : OWN * k + row + 8, :] if row < OWN else beyond_ref[k]

    return tile


def pack2(ref, rim_ref, tiles):
    at = lax.broadcasted_iota(jnp.int32, (8, LANES), 0)
    joined = None
    for k, (main, _) in enumerate(tiles):
        tile = main()
        ref[2 * k], ref[2 * k + 1] = tile[0:8], tile[8:16]
        slot = 2 * (k % 4)
        piece = turn(tile[16:24], slot + 1, 0)
        joined = piece if slot == 0 else jnp.where(at >= slot, piece, joined)
        if slot == 6 or k == SEND2 - 1:
            ref[2 * SEND2 + k // 4] = joined
    rim_ref[0] = packed_rims(tiles, WIDTH2)
    for k in range(3):
        ref[ROWTILES2 + k] = rim_ref[0, 8 * k : 8 * k + 8, :]


def unpack2(ref, out_ref):
    for k in range(SEND2):
        out_ref[k, 0, 0:8, :] = ref[2 * k]
        out_ref[k, 0, 8:16, :] = ref[2 * k + 1]
        out_ref[k, 0, 16:24, :] = turn(ref[2 * SEND2 + k // 4], -(2 * (k % 4) + 1), 0)

    def out(k, rim):
        out_ref[k, 1] = rim

    unpack_rims(jnp.concatenate([ref[ROWTILES2 + k] for k in range(3)], axis=0), WIDTH2, out)


def call(kernel, outs, scratch=(), more=(), space=None, cost=1000):
    specs = {} if space is None else {"in_specs": [pl.BlockSpec(memory_space=s) for s in space]}
    return pl.pallas_call(
        kernel,
        out_shape=[jax.ShapeDtypeStruct(shape, jnp.float32) for shape in outs],
        scratch_shapes=[pltpu.VMEM(shape, jnp.float32) for shape in scratch] + list(more),
        compiler_params=None if INTERPRET else pltpu.CompilerParams(vmem_limit_bytes=40 * 2**20),
        cost_estimate=pl.CostEstimate(flops=cost * 2000, bytes_accessed=cost * 1000, transcendentals=0),
        interpret=INTERPRET,
        **specs,
    )


LEVEL_Y = [i for i in range(Q) if VEL[i][1] == 0][:3]
YTILES = Q + (Q + 1) // 2


def rows_moves(up):
    inwards = 1 if up else -1
    first = lambda count: OWN - count if up else 0
    fourth, third = (OWN - 4, OWN - 3) if up else (3, 2)
    out = []
    for i in range(Q):
        for layer in range(2):
            out.append((0, i, layer, first(3), 3, i, 3 * layer))
            out.append((1, i, layer, first(2), 2, Q + i // 2, 4 * (i % 2) + 2 * layer))
            if VEL[i][1] == inwards:
                out.append((0, i, layer, fourth, 1, i, 6 + layer))
            elif VEL[i][1] == -inwards:
                out.append((1, i, layer, third, 1, i, 6 + layer))
            elif i in LEVEL_Y:
                out.append((2, 0, layer, first(3) + LEVEL_Y.index(i), 1, i, 6 + layer))
    return out


def collided(f, blocking):
    even, odd = split(f)
    rho, u = moments(f[0], even, odd)
    return collide(f[0], even, odd, rho, u, blocking, range(Q))


def rows_kernel(
    f_hbm, por_hbm, solid_hbm, seed_hbm,
    up_ref, down_ref, f_ref, seed_ref, g_ref, b_ref, fluid_ref,
    por_ref, solid_ref, sems,
):
    copies = [
        pltpu.make_async_copy(src, dst, sems.at[k])
        for k, (src, dst) in enumerate(
            [(f_hbm, f_ref), (por_hbm, por_ref), (solid_hbm, solid_ref), (seed_hbm, seed_ref)]
        )
    ]
    for copy in copies:
        copy.start()
    for copy in copies[:3]:
        copy.wait()
    for layer in range(2):
        solid = solid_ref[layer] == 1
        b_ref[0, layer] = jnp.where(solid, 1.0, por_ref[layer])
        fluid_ref[layer] = jnp.where(solid, 0.0, 1.0)

        def body(row, layer=layer):
            rows = slice(row, row + 8)
            g = collided([f_ref[i, layer, rows, :] for i in range(Q)], b_ref[0, layer, rows, :])
            for i in range(Q):
                g_ref[i, layer, rows, :] = g[i]

        tiles_loop(2, body)
    copies[3].wait()
    arrays = (g_ref, seed_ref, b_ref)
    for ref, up in ((up_ref, True), (down_ref, False)):
        for which, i, layer, row, count, tile, at in rows_moves(up):
            ref[tile, at : at + count, :] = arrays[which][i, layer, row : row + count, :]


def columns_kernel(g_ref, seed_ref, b_ref, below_ref, above_ref, main_ref, up_ref, down_ref):
    for k in range(FIELDS):
        for layer in range(2):
            own = g_ref[k, layer] if k < Q else seed_ref[k - Q, layer] if k < 2 * Q else b_ref[0, layer]
            main_ref[k, layer, 0:OWN, :] = own
    for ref, up, shift in ((below_ref, True, ROWS - OWN), (above_ref, False, OWN)):
        for which, i, layer, row, count, tile, at in rows_moves(up):
            main_ref[which * Q + i, layer, row + shift : row + shift + count, :] = ref[tile, at : at + count, :]
    at = column((ROWS, LANES))
    high = low = None
    for k in range(FIELDS):
        for layer in range(2):
            tile = main_ref[k, layer]
            n = 2 * k + layer
            slot = n % 32
            piece = turn(tile, 4 * slot + 4, 1)
            high = piece if slot == 0 else jnp.where(at >= 4 * slot, piece, high)
            low = piece if slot == 0 else jnp.where((at >= 4 * slot + 4) if slot < 31 else (at < 4), piece, low)
            if slot == 31 or n == 2 * FIELDS - 1:
                up_ref[n // 32] = high
                down_ref[n // 32] = low


def tiles_loop(count, body):
    for n in range(count):
        body(8 * n)


def joined_columns(before_ref, beyond_ref, out_ref):
    odd = (column((ROWS, LANES)) // 4) % 2
    for tile in range(ZTILES):
        for part in range(2):
            out_ref[2 * tile + part] = jnp.where(odd == part, before_ref[tile], beyond_ref[tile])


def rim_of(columns_ref, k, layer):
    slot = (2 * k + layer) % 32
    return turn(columns_ref[2 * ((2 * k + layer) // 32) + slot % 2], -(4 * slot + 4), 1)


def first_kernel(
    main_ref, before_ref, beyond_ref,
    f1_ref, edge_ref, b_ref, up_ref, down_ref,
    level_ref, rim_ref, seed_ref, columns_ref,
):
    joined_columns(before_ref, beyond_ref, columns_ref)
    for i in range(Q):
        for layer in range(2):
            rim_ref[i, layer] = rim_of(columns_ref, i, layer)
    for layer, pops in ((1, XM), (0, XP)):
        for i in pops:
            seed_ref[i, 0] = rim_of(columns_ref, Q + i, layer)
    for layer in range(2):
        b_ref[layer, 0] = main_ref[2 * Q, layer]
        b_ref[layer, 1] = rim_of(columns_ref, 2 * Q, layer)
    for i in range(Q):
        for layer in range(2):
            to = layer + VEL[i][0]
            tiles = moved(main_ref[i, layer], rim_ref[i, layer], i, 1)
            for lane in range(2):
                if to in (0, 1):
                    f1_ref[i, to, lane] = tiles[lane]
                else:
                    edge_ref[i, lane] = tiles[lane]
    for layer in range(2):
        for lane in range(2):
            stay = {i: f1_ref[i, layer, lane] for i in X0}
            level_ref[0, layer, lane] = total(stay.values())
            for axis in (1, 2):
                level_ref[axis, layer, lane] = total(
                    stay[i] if VEL[i][axis] == 1 else -stay[i] for i in X0 if VEL[i][axis]
                )

    def tiles_of(forward, backward, layer):
        def pick(ref, *where):
            return (lambda: ref[where + (0,)]), (lambda: ref[where + (1,)])

        out = [pick(f1_ref, i, layer) for i in forward]
        out += [pick(level_ref, k, layer) for k in range(3)]
        out.append(pick(b_ref, layer))
        out += [pick(edge_ref, i) for i in forward]
        for i in backward:
            seed_ref[i, 0], seed_ref[i, 1] = moved(main_ref[Q + i, layer], seed_ref[i, 0], i, -1)
            out.append(pick(seed_ref, i))
        return out

    pack1(up_ref, tiles_of(XP, XM, 1))
    pack1(down_ref, tiles_of(XM, XP, 0))


def seed_kernel(main_ref, before_ref, beyond_ref, b2_ref, rim_ref, columns_ref):
    joined_columns(before_ref, beyond_ref, columns_ref)
    for i in range(Q):
        for layer in range(2):
            if layer - VEL[i][0] in (0, 1):
                rim_ref[i, layer] = rim_of(columns_ref, Q + i, layer)
    for i in range(Q):
        for layer in range(2):
            to = layer - VEL[i][0]
            if to in (0, 1):
                main, rim = moved(main_ref[Q + i, layer], rim_ref[i, layer], i, -1)
                b2_ref[i, to, 0] = main
                b2_ref[i, to, 1] = rim


def side_kernel(side, f1_ref, edge_ref, b_ref, got_ref, mom_ref, far_ref, bh_ref, g_ref, far_g_ref, beyond_scr, rim_scr):
    got = unpack1(got_ref, beyond_scr, rim_scr)
    theirs, ours = (XP, XM) if side == 0 else (XM, XP)
    for lane in range(2):
        def near(row, lane=lane):
            rows = slice(row, row + 8)
            f = [None if i in theirs else f1_ref[i, side, lane, rows, :] for i in range(Q)]
            for k, i in enumerate(theirs):
                f[i] = got(9 + k, lane, row)
            even, odd = split(f)
            rho, u = moments(f[0], even, odd)
            mom_ref[3, lane, rows, :] = rho
            for axis in range(3):
                mom_ref[axis, lane, rows, :] = u[axis]
            g = collide(f[0], even, odd, rho, u, b_ref[side, lane, rows, :], range(Q))
            for i in range(Q):
                g_ref[i, lane, rows, :] = g[i]

        def far(row, lane=lane):
            rows = slice(row, row + 8)
            f = [None] * Q
            for k, i in enumerate(theirs):
                f[i] = got(k, lane, row)
            for i in ours:
                f[i] = edge_ref[i, lane, rows, :]
            even, odd = split(f, XP)
            rho, u = moments_from([got(5 + k, lane, row) for k in range(3)], even, odd)
            for axis in range(3):
                far_ref[axis, lane, rows, :] = u[axis]
            blocking = got(8, lane, row)
            bh_ref[lane, rows, :] = blocking
            g = collide(None, even, odd, rho, u, blocking, theirs)
            for i in theirs:
                far_g_ref[i, lane, rows, :] = g[i]

        tiles_loop(3, near)
        tiles_loop(3, far)


def middle_kernel(
    b_ref, b2_ref, left_ref, right_ref, mom0_ref, mom1_ref, g0_ref, g1_ref, g_left_ref, g_right_ref,
    grad_ref, b1_ref, edge1_ref, sums_ref, up_ref, down_ref,
    l_beyond, l_scr, r_beyond, r_scr, f_scr, a_scr, rim_scr,
):
    got = (unpack1(left_ref, l_beyond, l_scr, 14), unpack1(right_ref, r_beyond, r_scr, 14))
    g_refs = (g_left_ref, g0_ref, g1_ref, g_right_ref)
    mom = (mom0_ref, mom1_ref)

    for i in range(Q):
        for layer in range(2):
            ref = g_refs[layer + 1 - VEL[i][0]]
            main, rim = moved(ref[i, 0], ref[i, 1], i, 1)
            f_scr[i, layer, 0] = main
            f_scr[i, layer, 1] = rim

    for layer in range(2):
        for lane in range(2):

            def body(row, layer=layer, lane=lane):
                rows = slice(row, row + 8)
                missing = XM if layer == 0 else XP
                f = [f_scr[i, layer, lane, rows, :] for i in range(Q)]
                b = {i: b2_ref[i, layer, lane, rows, :] for i in range(Q) if i not in missing}
                for k, i in enumerate(missing):
                    b[i] = got[layer](14 + k, lane, row)
                even, odd = split(f)
                rho, u = moments(f[0], even, odd)
                b_even, b_odd = split(b)
                sums = flow(b[0], b_even, b_odd, u)
                a = back(b[0], b_even, b_odd, sums, u, b_ref[layer, lane, rows, :], range(Q))
                for i in range(Q):
                    a_scr[i, layer, lane, rows, :] = a[i]
                if lane == 0 and row < OWN:
                    grad_ref[layer, rows, :] = gradient_of((b[0], b_even, b_odd), (f[0], even, odd), rho, sums[0])

            tiles_loop(3, body)

    for i in range(Q):
        for layer in range(2):
            to = layer - VEL[i][0]
            tiles = moved(a_scr[i, layer, 0], a_scr[i, layer, 1], i, -1)
            for lane in range(2):
                if to in (0, 1):
                    b1_ref[i, to, lane] = tiles[lane]
                else:
                    edge1_ref[i, lane] = tiles[lane]

    for layer in range(2):
        for lane in range(2):

            def body(row, layer=layer, lane=lane):
                rows = slice(row, row + 8)
                missing = XM if layer == 0 else XP
                b = {i: b1_ref[i, layer, lane, rows, :] for i in range(Q) if i not in missing}
                even, odd = split(b, [i for i in PAIRS if i in X0])
                for i in XP:
                    even[i], odd[i] = (b[i], b[i]) if layer == 0 else (b[i + 1], -b[i + 1])
                sums = flow(b[0], even, odd, [mom[layer][axis, lane, rows, :] for axis in range(3)])
                for k in range(4):
                    sums_ref[k, layer, lane, rows, :] = sums[k]

            tiles_loop(3, body)

    def tiles_of(theirs, layer):
        def pick(ref, *where):
            return (lambda: ref[where + (0,)]), (lambda: ref[where + (1,)])

        return (
            [pick(edge1_ref, i) for i in theirs]
            + [pick(b1_ref, i, layer) for i in theirs]
            + [pick(sums_ref, k, layer) for k in range(4)]
        )

    pack2(up_ref, rim_scr, tiles_of(XM, 1))
    pack2(down_ref, rim_scr, tiles_of(XP, 0))


def side_back_kernel(
    side, b1_ref, edge1_ref, sums_ref, mom_ref, far_ref, b_ref, bh_ref, f1_ref, got1_ref, grad_ref, got_ref,
    out_grad_ref, a_ref, far_a_ref,
    got,
):
    unpack2(got_ref, got)
    near_pops, far_pops = (XM, XP) if side == 0 else (XP, XM)

    def halves(b, plus):
        return {i: b[i] if plus else b[i + 1] for i in XP}, {i: b[i] if plus else -b[i + 1] for i in XP}

    for lane in range(2):

        def near(row, lane=lane):
            rows = slice(row, row + 8)
            b = {i: b1_ref[i, side, lane, rows, :] for i in range(Q) if i not in near_pops}
            for k, i in enumerate(near_pops):
                b[i] = got[k, lane, rows, :]
            even, odd = split(b)
            u = [mom_ref[axis, lane, rows, :] for axis in range(3)]
            parts = flow(None, *halves(b, side == 1), u)
            sums = [sums_ref[k, side, lane, rows, :] + part for k, part in enumerate(parts)]
            a = back(b[0], even, odd, sums, u, b_ref[side, lane, rows, :], range(Q))
            for i in range(Q):
                a_ref[i, lane, rows, :] = a[i]
            if lane == 0 and row < OWN:
                f = {i: f1_ref[i, side, lane, rows, :] for i in range(Q) if i not in far_pops}
                for k, i in enumerate(far_pops):
                    f[i] = got1_ref[OWN * (9 + k) + row : OWN * (9 + k) + row + 8, :]
                grad = gradient_of((b[0], even, odd), (f[0],) + split(f), mom_ref[3, lane, rows, :], sums[0])
                out_grad_ref[rows, :] = grad + grad_ref[side, rows, :]

        def far(row, lane=lane):
            rows = slice(row, row + 8)
            b = {i: edge1_ref[i, lane, rows, :] for i in far_pops}
            for k, i in enumerate(near_pops):
                b[i] = got[5 + k, lane, rows, :]
            even, odd = split(b, XP)
            u = [far_ref[axis, lane, rows, :] for axis in range(3)]
            parts = flow(None, *halves(b, side == 0), u)
            sums = [got[10 + k, lane, rows, :] + part for k, part in enumerate(parts)]
            a = back(None, even, odd, sums, u, bh_ref[lane, rows, :], near_pops)
            for i in near_pops:
                far_a_ref[i, lane, rows, :] = a[i]

        tiles_loop(3, near)
        tiles_loop(3, far)


def last_kernel(
    b_ref, grad0_ref, grad1_ref, a_left_ref, a0_ref, a1_ref, a_right_ref, f_ref, fluid_ref,
    out_grad_ref, out_ref,
    b_scr,
):
    a_refs = (a_left_ref, a0_ref, a1_ref, a_right_ref)
    grads = (grad0_ref, grad1_ref)
    for i in range(Q):
        for layer in range(2):
            ref = a_refs[layer + 1 + VEL[i][0]]
            main, _ = moved(ref[i, 0], ref[i, 1], i, -1)
            b_scr[i, layer] = main[0:OWN]

    for layer in range(2):

        def body(row, layer=layer):
            rows = slice(row, row + 8)
            f = [f_ref[i, layer, rows, :] for i in range(Q)]
            b = {i: b_scr[i, layer, rows, :] for i in range(Q)}
            even, odd = split(f)
            rho, u = moments(f[0], even, odd)
            b_even, b_odd = split(b)
            sums = flow(b[0], b_even, b_odd, u)
            a = back(b[0], b_even, b_odd, sums, u, b_ref[layer, 0, rows, :], range(Q))
            for i in range(Q):
                out_ref[i, layer, rows, :] = a[i]
            grad = gradient_of((b[0], b_even, b_odd), (f[0], even, odd), rho, sums[0]) + grads[layer][rows, :]
            out_grad_ref[layer, rows, :] = jnp.where(fluid_ref[layer, rows, :] == 0.0, 0.0, grad)

        tiles_loop(2, body)


def placed(x):
    return x if INTERPRET else pltpu.with_memory_space_constraint(x, pltpu.HBM)


def both_ways(up, down, axis):
    count = lax.axis_size(axis)
    ring = [(i, (i + 1) % count) for i in range(count)]
    return lax.ppermute(up, axis, ring), lax.ppermute(down, axis, [(j, i) for i, j in ring])


def body(populations, porosity, solid, seed_adjoint):
    half, tile = (2, 2, ROWS, LANES), (ROWS, LANES)
    inputs = [placed(x) for x in (populations, porosity, solid, seed_adjoint)]
    block = populations.shape
    cells = block[1:]
    up, down, f, seed, g, own_b, fluid = call(
        rows_kernel,
        [(YTILES, 8, LANES)] * 2 + [block, block, block, (1,) + cells, cells],
        [cells],
        [pltpu.VMEM(cells, jnp.int32), pltpu.SemaphoreType.DMA((4,))],
        space=[pltpu.HBM] * 4,
    )(*inputs)
    below, above = both_ways(up, down, "gy")
    main, up, down = call(columns_kernel, [(FIELDS, 2) + tile] + [(ZTILES,) + tile] * 2)(g, seed, own_b, below, above)
    before, beyond = both_ways(up, down, "gz")
    f1, edge, b, up, down = call(
        first_kernel,
        [(Q,) + half, (Q, 2) + tile, half] + [(STRIPS1[-1] + ROWS, LANES)] * 2,
        [(3,) + half, (Q, 2) + tile, (Q, 2) + tile, (2 * ZTILES,) + tile],
    )(main, before, beyond)
    left1, right1 = both_ways(up, down, "gx")
    (b2,) = call(seed_kernel, [(Q,) + half], [(Q, 2) + tile, (2 * ZTILES,) + tile])(main, before, beyond)
    sides = []
    for side, got in enumerate((left1, right1)):
        sides.append(
            call(
                functools.partial(side_kernel, side),
                [(4, 2) + tile, (3, 2) + tile, (2,) + tile, (Q, 2) + tile, (Q, 2) + tile],
                [(SEND1, 8, LANES), (SEND1,) + tile],
            )(f1, edge, b, got)
        )
    (mom0, far0, bh0, g0, g_left), (mom1, far1, bh1, g1, g_right) = sides
    grad, b1, edge1, sums, up, down = call(
        middle_kernel,
        [(2, OWN, LANES), (Q,) + half, (Q, 2) + tile, (4,) + half] + [(ROWTILES2 + 3, 8, LANES)] * 2,
        [(SEND1, 8, LANES), (SEND1,) + tile] * 2 + [(Q,) + half, (Q,) + half, (1,) + tile],
    )(b, b2, left1, right1, mom0, mom1, g0, g1, g_left, g_right)
    left, right = both_ways(up, down, "gx")
    sides = []
    for side, (mom, far, bh, got1, got) in enumerate(((mom0, far0, bh0, left1, left), (mom1, far1, bh1, right1, right))):
        sides.append(
            call(
                functools.partial(side_back_kernel, side),
                [(OWN, LANES), (Q, 2) + tile, (Q, 2) + tile],
                [(SEND2, 2) + tile],
            )(b1, edge1, sums, mom, far, b, bh, f1, got1, grad, got)
        )
    (grad0, a0, a_left), (grad1, a1, a_right) = sides
    gradient, adjoint_out = call(last_kernel, [(2, OWN, LANES), (Q, 2, OWN, LANES)], [(Q, 2, OWN, LANES)])(
        b, grad0, grad1, a_left, a0, a1, a_right, f, fluid
    )
    return gradient, adjoint_out


def solution(mesh):
    field, cell = P(None, "gx", "gy", "gz"), P("gx", "gy", "gz")
    return jax.shard_map(
        body, mesh=mesh, in_specs=(field, cell, cell, field), out_specs=(cell, field), check_vma=False
    )
```

```python
import functools

import jax
import jax.numpy as jnp
from jax import lax
from jax.experimental import pallas as pl
from jax.experimental.pallas import tpu as pltpu
from jax.sharding import PartitionSpec as P

INTERPRET = False

VEL = [
    (0, 0, 0),
    (1, 0, 0), (-1, 0, 0), (0, 1, 0), (0, -1, 0), (0, 0, 1), (0, 0, -1),
    (1, 1, 0), (-1, -1, 0), (1, -1, 0), (-1, 1, 0),
    (1, 0, 1), (-1, 0, -1), (1, 0, -1), (-1, 0, 1),
    (0, 1, 1), (0, -1, -1), (0, 1, -1), (0, -1, 1),
]
OPP = [0, 2, 1, 4, 3, 6, 5, 8, 7, 10, 9, 12, 11, 14, 13, 16, 15, 18, 17]
WEIGHT = [1.0 / 3.0] + [1.0 / 18.0] * 6 + [1.0 / 36.0] * 12
OMEGA = 1.25
Q = 19
XP = [i for i in range(Q) if VEL[i][0] == 1]
X0 = [i for i in range(Q) if VEL[i][0] == 0]
XM = [i for i in range(Q) if VEL[i][0] == -1]
PAIRS = [i for i in range(1, Q, 2)]

ROWS, OWN, LANES, RIM = 24, 16, 128, 4
FIELDS = 2 * Q + 1
ZTILES = -(-2 * FIELDS // 32)


def total(terms):
    terms = list(terms)
    while len(terms) > 1:
        terms = [a + b for a, b in zip(terms[::2], terms[1::2])] + (terms[-1:] if len(terms) % 2 else [])
    return terms[0]


ROOT = 4.5**0.5
FACES = [i for i in PAIRS if i < 7]
EDGES = [i for i in PAIRS if i >= 7]


def project(vector, i):
    out = None
    for axis in range(3):
        c = VEL[i][axis]
        if c == 0:
            continue
        if out is None:
            out = vector[axis] if c == 1 else -vector[axis]
        else:
            out = out + vector[axis] if c == 1 else out - vector[axis]
    return out


def gathered(terms, axis):
    plus = [terms[i] for i in terms if VEL[i][axis] == 1]
    minus = [terms[i] for i in terms if VEL[i][axis] == -1]
    return total(plus) - total(minus) if minus else total(plus)


def split(f, pairs=PAIRS):
    return {i: f[i] + f[i + 1] for i in pairs}, {i: f[i] - f[i + 1] for i in pairs}


def moments(f0, even, odd):
    rho = f0 + total(even.values())
    inv = 1.0 / rho
    return rho, [gathered(odd, axis) * inv for axis in range(3)]


def moments_from(level, even, odd):
    rho = level[0] + total(even.values())
    inv = 1.0 / rho
    return rho, [gathered(odd, 0) * inv] + [(level[axis] + gathered(odd, axis)) * inv for axis in (1, 2)]


def weights(blocking):
    keep = 1.0 - blocking
    own = (1.0 - OMEGA) * keep
    return 0.5 * (own + blocking), 0.5 * (own - blocking), OMEGA * keep


def collide(f0, even, odd, rho, u, blocking, want):
    k_even, k_odd, mix = weights(blocking)
    scale = mix * rho
    v = [ROOT * part for part in u]
    squares = [part * part for part in v]
    base = 1.0 - (1.0 / 3.0) * (squares[0] + squares[1] + squares[2])
    out = {}
    if 0 in want:
        out[0] = (2.0 * k_even) * f0 + (WEIGHT[0] * scale) * base
    for group in (FACES, EDGES):
        s = WEIGHT[group[0]] * scale
        s_odd = (2.0**0.5) * s
        for i in group:
            if i not in want and i + 1 not in want:
                continue
            p = project(v, i)
            square = squares[VEL[i].index(1)] if i in FACES else p * p
            p_even = k_even * even[i] + s * (base + square)
            p_odd = k_odd * odd[i] + s_odd * p
            if i in want:
                out[i] = p_even + p_odd
            if i + 1 in want:
                out[i + 1] = p_even - p_odd
    return out


def flow(b0, even, odd, u):
    base = 1.0 - 1.5 * (u[0] * u[0] + u[1] * u[1] + u[2] * u[2])
    q = [1.5 * part for part in u]
    level = [] if b0 is None else [WEIGHT[0] * b0]
    value, slope = [], [[], [], []]
    for group in (FACES, EDGES):
        group = [i for i in group if i in even]
        w = WEIGHT[group[0]]
        level.append(w * total(even[i] for i in group))
        work, along = [], {}
        for i in group:
            p = project(q, i)
            t = p * even[i]
            h = odd[i] + t
            work.append(p * h)
            along[i] = h + t
        value.append((2.0 * w) * total(work))
        for axis in range(3):
            if any(VEL[i][axis] for i in group):
                slope[axis].append((3.0 * w) * gathered(along, axis))
    level = total(level)
    return [base * level + total(value)] + [total(slope[axis]) - 2.0 * (q[axis] * level) for axis in range(3)]


def back(b0, even, odd, sums, u, blocking, want):
    energy, *v = sums
    k_even, k_odd, mix = weights(blocking)
    common = mix * (energy - (v[0] * u[0] + v[1] * u[1] + v[2] * u[2]))
    mv = [mix * v[axis] for axis in range(3)]
    out = {}
    if 0 in want:
        out[0] = (2.0 * k_even) * b0 + common
    for i in PAIRS:
        if i not in want and i + 1 not in want:
            continue
        p_even = k_even * even[i] + common
        p_odd = k_odd * odd[i] + project(mv, i)
        if i in want:
            out[i] = p_even + p_odd
        if i + 1 in want:
            out[i + 1] = p_even - p_odd
    return out


def gradient_of(b, f, rho, energy):
    evens = total(b[1][i] * f[1][i] for i in PAIRS)
    odds = total(b[2][i] * f[2][i] for i in PAIRS)
    return OMEGA * (b[0] * f[0] - rho * energy) + (0.5 * OMEGA) * evens - (1.0 - 0.5 * OMEGA) * odds


def column(shape):
    return lax.broadcasted_iota(jnp.int32, shape, len(shape) - 1)


def turn(tile, shift, axis):
    shift = shift % tile.shape[axis]
    return tile if shift == 0 else pltpu.roll(tile, shift, axis)


def moved(main, rim, i, sign):
    y, z = sign * VEL[i][1], sign * VEL[i][2]
    if y:
        main, rim = turn(main, y, 0), turn(rim, y, 0)
    if z:
        at = column(main.shape)
        edge = at == (0 if z == 1 else LANES - 1)
        main, rim = turn(main, z, 1), turn(rim, z, 1)
        main, rim = jnp.where(edge, rim, main), jnp.where(edge, main, rim)
    return main, rim


def packed_rims(tiles, width):
    at = column((ROWS, LANES))
    joined, first = None, 0
    for k, (_, rim) in enumerate(tiles):
        piece = turn(rim(), first + width[k] // 2, 1)
        joined = piece if joined is None else jnp.where(at >= first, piece, joined)
        first += width[k]
    return joined


def unpack_rims(tile, width, out):
    first = 0
    for k in range(len(width)):
        out(k, turn(tile, -(first + width[k] // 2), 1))
        first += width[k]


SEND1, SEND2 = 19, 14
WIDTH1 = [6] * 14 + [4] * 5
WIDTH2 = [2] * SEND2
ROWTILES2 = 2 * SEND2 + -(-SEND2 // 4)


STRIPS1 = [sum(WIDTH1[:k]) + OWN * SEND1 for k in range(SEND1 + 1)]


def pack1(ref, tiles):
    for k, (main, _) in enumerate(tiles):
        tile, half, at = main(), WIDTH1[k] // 2, STRIPS1[k]
        ref[OWN * k : OWN * k + OWN, :] = tile[0:OWN]
        ref[at : at + half, :] = tile[ROWS - half : ROWS]
        ref[at + half : at + 2 * half, :] = tile[OWN : OWN + half]
    ref[STRIPS1[-1] : STRIPS1[-1] + ROWS, :] = packed_rims(tiles, WIDTH1)


def unpack1(ref, beyond_ref, rim_ref, first=0):
    for k in range(first, SEND1):
        half, at = WIDTH1[k] // 2, STRIPS1[k]
        beyond_ref[k, 8 - half : 8, :] = ref[at : at + half, :]
        beyond_ref[k, 0:half, :] = ref[at + half : at + 2 * half, :]

    def out(k, rim):
        if k >= first:
            rim_ref[k] = rim

    unpack_rims(ref[STRIPS1[-1] : STRIPS1[-1] + ROWS, :], WIDTH1, out)

    def tile(k, lane, row):
        if lane:
            return rim_ref[k, row : row + 8, :]
        return ref[OWN * k + row : OWN * k + row + 8, :] if row < OWN else beyond_ref[k]

    return tile


def pack2(ref, rim_ref, tiles):
    at = lax.broadcasted_iota(jnp.int32, (8, LANES), 0)
    joined = None
    for k, (main, _) in enumerate(tiles):
        tile = main()
        ref[2 * k], ref[2 * k + 1] = tile[0:8], tile[8:16]
        slot = 2 * (k % 4)
        piece = turn(tile[16:24], slot + 1, 0)
        joined = piece if slot == 0 else jnp.where(at >= slot, piece, joined)
        if slot == 6 or k == SEND2 - 1:
            ref[2 * SEND2 + k // 4] = joined
    rim_ref[0] = packed_rims(tiles, WIDTH2)
    for k in range(3):
        ref[ROWTILES2 + k] = rim_ref[0, 8 * k : 8 * k + 8, :]


def unpack2(ref, out_ref):
    for k in range(SEND2):
        out_ref[k, 0, 0:8, :] = ref[2 * k]
        out_ref[k, 0, 8:16, :] = ref[2 * k + 1]
        out_ref[k, 0, 16:24, :] = turn(ref[2 * SEND2 + k // 4], -(2 * (k % 4) + 1), 0)

    def out(k, rim):
        out_ref[k, 1] = rim

    unpack_rims(jnp.concatenate([ref[ROWTILES2 + k] for k in range(3)], axis=0), WIDTH2, out)


def call(kernel, outs, scratch=(), more=(), space=None, cost=1000):
    specs = {} if space is None else {"in_specs": [pl.BlockSpec(memory_space=s) for s in space]}
    return pl.pallas_call(
        kernel,
        out_shape=[jax.ShapeDtypeStruct(shape, jnp.float32) for shape in outs],
        scratch_shapes=[pltpu.VMEM(shape, jnp.float32) for shape in scratch] + list(more),
        compiler_params=None if INTERPRET else pltpu.CompilerParams(vmem_limit_bytes=40 * 2**20),
        cost_estimate=pl.CostEstimate(flops=cost * 2000, bytes_accessed=cost * 1000, transcendentals=0),
        interpret=INTERPRET,
        **specs,
    )


LEVEL_Y = [i for i in range(Q) if VEL[i][1] == 0]
YTILES = Q + 8


def rows_moves(up):
    inwards = 1 if up else -1
    first = lambda count: OWN - count if up else 0
    fourth, third = (OWN - 4, OWN - 3) if up else (3, 2)
    out = []
    for i in range(Q):
        for layer in range(2):
            out.append((0, i, layer, first(3), 3, i, 3 * layer))
            if i < 16:
                out.append((1, i, layer, first(2), 2, Q + i // 2, 4 * (i % 2) + 2 * layer))
            else:
                out.append((1, i, layer, first(2), 2, LEVEL_Y[3 + 2 * (i - 16) + layer], 6))
            if VEL[i][1] == inwards:
                out.append((0, i, layer, fourth, 1, i, 6 + layer))
            elif VEL[i][1] == -inwards:
                out.append((1, i, layer, third, 1, i, 6 + layer))
            elif i in LEVEL_Y[:3]:
                out.append((2, 0, layer, first(3) + LEVEL_Y.index(i), 1, i, 6 + layer))
    return out


def collided(f, blocking):
    even, odd = split(f)
    rho, u = moments(f[0], even, odd)
    return collide(f[0], even, odd, rho, u, blocking, range(Q))


def rows_kernel(
    f_hbm, por_hbm, solid_hbm, seed_hbm,
    up_ref, down_ref, f_ref, seed_ref, g_ref, b_ref, fluid_ref,
    por_ref, solid_ref, sems,
):
    copies = [
        pltpu.make_async_copy(src, dst, sems.at[k])
        for k, (src, dst) in enumerate(
            [(f_hbm, f_ref), (por_hbm, por_ref), (solid_hbm, solid_ref), (seed_hbm, seed_ref)]
        )
    ]
    for copy in copies:
        copy.start()
    for copy in copies[:3]:
        copy.wait()
    for layer in range(2):
        solid = solid_ref[layer] == 1
        b_ref[0, layer] = jnp.where(solid, 1.0, por_ref[layer])
        fluid_ref[layer] = jnp.where(solid, 0.0, 1.0)

        def body(row, layer=layer):
            rows = slice(row, row + 8)
            g = collided([f_ref[i, layer, rows, :] for i in range(Q)], b_ref[0, layer, rows, :])
            for i in range(Q):
                g_ref[i, layer, rows, :] = g[i]

        tiles_loop(2, body)
    copies[3].wait()
    arrays = (g_ref, seed_ref, b_ref)
    for ref, up in ((up_ref, True), (down_ref, False)):
        for which, i, layer, row, count, tile, at in rows_moves(up):
            ref[tile, at : at + count, :] = arrays[which][i, layer, row : row + count, :]


def columns_kernel(g_ref, seed_ref, b_ref, below_ref, above_ref, main_ref, up_ref, down_ref):
    for k in range(FIELDS):
        for layer in range(2):
            own = g_ref[k, layer] if k < Q else seed_ref[k - Q, layer] if k < 2 * Q else b_ref[0, layer]
            main_ref[k, layer, 0:OWN, :] = own
    for ref, up, shift in ((below_ref, True, ROWS - OWN), (above_ref, False, OWN)):
        for which, i, layer, row, count, tile, at in rows_moves(up):
            main_ref[which * Q + i, layer, row + shift : row + shift + count, :] = ref[tile, at : at + count, :]
    at = column((ROWS, LANES))
    high = low = None
    for k in range(FIELDS):
        for layer in range(2):
            tile = main_ref[k, layer]
            n = 2 * k + layer
            slot = n % 32
            piece = turn(tile, 4 * slot + 4, 1)
            high = piece if slot == 0 else jnp.where(at >= 4 * slot, piece, high)
            low = piece if slot == 0 else jnp.where((at >= 4 * slot + 4) if slot < 31 else (at < 4), piece, low)
            if slot == 31 or n == 2 * FIELDS - 1:
                up_ref[n // 32] = high
                down_ref[n // 32] = low


def tiles_loop(count, body):
    for n in range(count):
        body(8 * n)


def joined_columns(before_ref, beyond_ref, out_ref):
    odd = (column((ROWS, LANES)) // 4) % 2
    for tile in range(ZTILES):
        for part in range(2):
            out_ref[2 * tile + part] = jnp.where(odd == part, before_ref[tile], beyond_ref[tile])


def rim_of(columns_ref, k, layer):
    slot = (2 * k + layer) % 32
    return turn(columns_ref[2 * ((2 * k + layer) // 32) + slot % 2], -(4 * slot + 4), 1)


def turned(tile, i, sign):
    return turn(turn(tile, sign * VEL[i][1], 0), sign * VEL[i][2], 1)


def edged(main, rim, i, sign):
    z = sign * VEL[i][2]
    if z == 0:
        return main, rim
    edge = column(main.shape) == (0 if z == 1 else LANES - 1)
    return jnp.where(edge, rim, main), jnp.where(edge, main, rim)


def turn_kernel(main_ref, g_ref, seed_ref):
    for i in range(Q):
        for layer in range(2):
            g_ref[i, layer] = turned(main_ref[i, layer], i, 1)
    for layer, pops in ((1, XM), (0, XP)):
        for i in pops:
            seed_ref[i] = turned(main_ref[Q + i, layer], i, -1)


def first_kernel(
    main_ref, g_ref, turned_seed_ref, before_ref, beyond_ref,
    f1_ref, edge_ref, b_ref, up_ref, down_ref,
    level_ref, rim_ref, seed_ref, columns_ref,
):
    joined_columns(before_ref, beyond_ref, columns_ref)
    for i in range(Q):
        for layer in range(2):
            rim_ref[i, layer] = rim_of(columns_ref, i, layer)
    for layer, pops in ((1, XM), (0, XP)):
        for i in pops:
            seed_ref[i, 0] = rim_of(columns_ref, Q + i, layer)
    for layer in range(2):
        b_ref[layer, 0] = main_ref[2 * Q, layer]
        b_ref[layer, 1] = rim_of(columns_ref, 2 * Q, layer)
    for i in range(Q):
        for layer in range(2):
            to = layer + VEL[i][0]
            tiles = edged(g_ref[i, layer], turned(rim_ref[i, layer], i, 1), i, 1)
            for lane in range(2):
                if to in (0, 1):
                    f1_ref[i, to, lane] = tiles[lane]
                else:
                    edge_ref[i, lane] = tiles[lane]
    for layer in range(2):
        for lane in range(2):
            stay = {i: f1_ref[i, layer, lane] for i in X0}
            level_ref[0, layer, lane] = total(stay.values())
            for axis in (1, 2):
                level_ref[axis, layer, lane] = total(
                    stay[i] if VEL[i][axis] == 1 else -stay[i] for i in X0 if VEL[i][axis]
                )

    def tiles_of(forward, backward, layer):
        def pick(ref, *where):
            return (lambda: ref[where + (0,)]), (lambda: ref[where + (1,)])

        out = [pick(f1_ref, i, layer) for i in forward]
        out += [pick(level_ref, k, layer) for k in range(3)]
        out.append(pick(b_ref, layer))
        out += [pick(edge_ref, i) for i in forward]
        for i in backward:
            seed_ref[i, 0], seed_ref[i, 1] = edged(turned_seed_ref[i], turned(seed_ref[i, 0], i, -1), i, -1)
            out.append(pick(seed_ref, i))
        return out

    pack1(up_ref, tiles_of(XP, XM, 1))
    pack1(down_ref, tiles_of(XM, XP, 0))


def seed_kernel(main_ref, before_ref, beyond_ref, b2_ref, rim_ref, columns_ref):
    joined_columns(before_ref, beyond_ref, columns_ref)
    for i in range(Q):
        for layer in range(2):
            if layer - VEL[i][0] in (0, 1):
                rim_ref[i, layer] = rim_of(columns_ref, Q + i, layer)
    for i in range(Q):
        for layer in range(2):
            to = layer - VEL[i][0]
            if to in (0, 1):
                main, rim = moved(main_ref[Q + i, layer], rim_ref[i, layer], i, -1)
                b2_ref[i, to, 0] = main
                b2_ref[i, to, 1] = rim


def side_kernel(side, f1_ref, edge_ref, b_ref, got_ref, mom_ref, far_ref, bh_ref, g_ref, far_g_ref, beyond_scr, rim_scr):
    got = unpack1(got_ref, beyond_scr, rim_scr)
    theirs, ours = (XP, XM) if side == 0 else (XM, XP)
    for lane in range(2):
        def near(row, lane=lane):
            rows = slice(row, row + 8)
            f = [None if i in theirs else f1_ref[i, side, lane, rows, :] for i in range(Q)]
            for k, i in enumerate(theirs):
                f[i] = got(9 + k, lane, row)
            even, odd = split(f)
            rho, u = moments(f[0], even, odd)
            mom_ref[3, lane, rows, :] = rho
            for axis in range(3):
                mom_ref[axis, lane, rows, :] = u[axis]
            g = collide(f[0], even, odd, rho, u, b_ref[side, lane, rows, :], range(Q))
            for i in range(Q):
                g_ref[i, lane, rows, :] = g[i]

        def far(row, lane=lane):
            rows = slice(row, row + 8)
            f = [None] * Q
            for k, i in enumerate(theirs):
                f[i] = got(k, lane, row)
            for i in ours:
                f[i] = edge_ref[i, lane, rows, :]
            even, odd = split(f, XP)
            rho, u = moments_from([got(5 + k, lane, row) for k in range(3)], even, odd)
            for axis in range(3):
                far_ref[axis, lane, rows, :] = u[axis]
            blocking = got(8, lane, row)
            bh_ref[lane, rows, :] = blocking
            g = collide(None, even, odd, rho, u, blocking, theirs)
            for i in theirs:
                far_g_ref[i, lane, rows, :] = g[i]

        tiles_loop(3, near)
        tiles_loop(3, far)


def middle_kernel(
    b_ref, b2_ref, left_ref, right_ref, mom0_ref, mom1_ref, g0_ref, g1_ref, g_left_ref, g_right_ref,
    grad_ref, b1_ref, edge1_ref, sums_ref, up_ref, down_ref,
    l_beyond, l_scr, r_beyond, r_scr, f_scr, a_scr, rim_scr,
):
    got = (unpack1(left_ref, l_beyond, l_scr, 14), unpack1(right_ref, r_beyond, r_scr, 14))
    g_refs = (g_left_ref, g0_ref, g1_ref, g_right_ref)
    mom = (mom0_ref, mom1_ref)

    for i in range(Q):
        for layer in range(2):
            ref = g_refs[layer + 1 - VEL[i][0]]
            main, rim = moved(ref[i, 0], ref[i, 1], i, 1)
            f_scr[i, layer, 0] = main
            f_scr[i, layer, 1] = rim

    for layer in range(2):
        for lane in range(2):

            def body(row, layer=layer, lane=lane):
                rows = slice(row, row + 8)
                missing = XM if layer == 0 else XP
                f = [f_scr[i, layer, lane, rows, :] for i in range(Q)]
                b = {i: b2_ref[i, layer, lane, rows, :] for i in range(Q) if i not in missing}
                for k, i in enumerate(missing):
                    b[i] = got[layer](14 + k, lane, row)
                even, odd = split(f)
                rho, u = moments(f[0], even, odd)
                b_even, b_odd = split(b)
                sums = flow(b[0], b_even, b_odd, u)
                a = back(b[0], b_even, b_odd, sums, u, b_ref[layer, lane, rows, :], range(Q))
                for i in range(Q):
                    a_scr[i, layer, lane, rows, :] = a[i]
                if lane == 0 and row < OWN:
                    grad_ref[layer, rows, :] = gradient_of((b[0], b_even, b_odd), (f[0], even, odd), rho, sums[0])

            tiles_loop(3, body)

    for i in range(Q):
        for layer in range(2):
            to = layer - VEL[i][0]
            tiles = moved(a_scr[i, layer, 0], a_scr[i, layer, 1], i, -1)
            for lane in range(2):
                if to in (0, 1):
                    b1_ref[i, to, lane] = tiles[lane]
                else:
                    edge1_ref[i, lane] = tiles[lane]

    for layer in range(2):
        for lane in range(2):

            def body(row, layer=layer, lane=lane):
                rows = slice(row, row + 8)
                missing = XM if layer == 0 else XP
                b = {i: b1_ref[i, layer, lane, rows, :] for i in range(Q) if i not in missing}
                even, odd = split(b, [i for i in PAIRS if i in X0])
                for i in XP:
                    even[i], odd[i] = (b[i], b[i]) if layer == 0 else (b[i + 1], -b[i + 1])
                sums = flow(b[0], even, odd, [mom[layer][axis, lane, rows, :] for axis in range(3)])
                for k in range(4):
                    sums_ref[k, layer, lane, rows, :] = sums[k]

            tiles_loop(3, body)

    def tiles_of(theirs, layer):
        def pick(ref, *where):
            return (lambda: ref[where + (0,)]), (lambda: ref[where + (1,)])

        return (
            [pick(edge1_ref, i) for i in theirs]
            + [pick(b1_ref, i, layer) for i in theirs]
            + [pick(sums_ref, k, layer) for k in range(4)]
        )

    pack2(up_ref, rim_scr, tiles_of(XM, 1))
    pack2(down_ref, rim_scr, tiles_of(XP, 0))


def side_back_kernel(
    side, b1_ref, edge1_ref, sums_ref, mom_ref, far_ref, b_ref, bh_ref, f1_ref, got1_ref, grad_ref, got_ref,
    out_grad_ref, a_ref, far_a_ref,
    got,
):
    unpack2(got_ref, got)
    near_pops, far_pops = (XM, XP) if side == 0 else (XP, XM)

    def halves(b, plus):
        return {i: b[i] if plus else b[i + 1] for i in XP}, {i: b[i] if plus else -b[i + 1] for i in XP}

    for lane in range(2):

        def near(row, lane=lane):
            rows = slice(row, row + 8)
            b = {i: b1_ref[i, side, lane, rows, :] for i in range(Q) if i not in near_pops}
            for k, i in enumerate(near_pops):
                b[i] = got[k, lane, rows, :]
            even, odd = split(b)
            u = [mom_ref[axis, lane, rows, :] for axis in range(3)]
            parts = flow(None, *halves(b, side == 1), u)
            sums = [sums_ref[k, side, lane, rows, :] + part for k, part in enumerate(parts)]
            a = back(b[0], even, odd, sums, u, b_ref[side, lane, rows, :], range(Q))
            for i in range(Q):
                a_ref[i, lane, rows, :] = a[i]
            if lane == 0 and row < OWN:
                f = {i: f1_ref[i, side, lane, rows, :] for i in range(Q) if i not in far_pops}
                for k, i in enumerate(far_pops):
                    f[i] = got1_ref[OWN * (9 + k) + row : OWN * (9 + k) + row + 8, :]
                grad = gradient_of((b[0], even, odd), (f[0],) + split(f), mom_ref[3, lane, rows, :], sums[0])
                out_grad_ref[rows, :] = grad + grad_ref[side, rows, :]

        def far(row, lane=lane):
            rows = slice(row, row + 8)
            b = {i: edge1_ref[i, lane, rows, :] for i in far_pops}
            for k, i in enumerate(near_pops):
                b[i] = got[5 + k, lane, rows, :]
            even, odd = split(b, XP)
            u = [far_ref[axis, lane, rows, :] for axis in range(3)]
            parts = flow(None, *halves(b, side == 0), u)
            sums = [got[10 + k, lane, rows, :] + part for k, part in enumerate(parts)]
            a = back(None, even, odd, sums, u, bh_ref[lane, rows, :], near_pops)
            for i in near_pops:
                far_a_ref[i, lane, rows, :] = a[i]

        tiles_loop(3, near)
        tiles_loop(3, far)


def last_kernel(
    b_ref, grad0_ref, grad1_ref, a_left_ref, a0_ref, a1_ref, a_right_ref, f_ref, fluid_ref,
    out_grad_ref, out_ref,
    b_scr,
):
    a_refs = (a_left_ref, a0_ref, a1_ref, a_right_ref)
    grads = (grad0_ref, grad1_ref)
    for i in range(Q):
        for layer in range(2):
            ref = a_refs[layer + 1 + VEL[i][0]]
            main, _ = moved(ref[i, 0], ref[i, 1], i, -1)
            b_scr[i, layer] = main[0:OWN]

    for layer in range(2):

        def body(row, layer=layer):
            rows = slice(row, row + 8)
            f = [f_ref[i, layer, rows, :] for i in range(Q)]
            b = {i: b_scr[i, layer, rows, :] for i in range(Q)}
            even, odd = split(f)
            rho, u = moments(f[0], even, odd)
            b_even, b_odd = split(b)
            sums = flow(b[0], b_even, b_odd, u)
            a = back(b[0], b_even, b_odd, sums, u, b_ref[layer, 0, rows, :], range(Q))
            for i in range(Q):
                out_ref[i, layer, rows, :] = a[i]
            grad = gradient_of((b[0], b_even, b_odd), (f[0], even, odd), rho, sums[0]) + grads[layer][rows, :]
            out_grad_ref[layer, rows, :] = jnp.where(fluid_ref[layer, rows, :] == 0.0, 0.0, grad)

        tiles_loop(2, body)


def placed(x):
    return x if INTERPRET else pltpu.with_memory_space_constraint(x, pltpu.HBM)


def both_ways(up, down, axis):
    count = lax.axis_size(axis)
    ring = [(i, (i + 1) % count) for i in range(count)]
    return lax.ppermute(up, axis, ring), lax.ppermute(down, axis, [(j, i) for i, j in ring])


def body(populations, porosity, solid, seed_adjoint):
    half, tile = (2, 2, ROWS, LANES), (ROWS, LANES)
    inputs = [placed(x) for x in (populations, porosity, solid, seed_adjoint)]
    block = populations.shape
    cells = block[1:]
    up, down, f, seed, g, own_b, fluid = call(
        rows_kernel,
        [(YTILES, 8, LANES)] * 2 + [block, block, block, (1,) + cells, cells],
        [cells],
        [pltpu.VMEM(cells, jnp.int32), pltpu.SemaphoreType.DMA((4,))],
        space=[pltpu.HBM] * 4,
    )(*inputs)
    below, above = both_ways(up, down, "gy")
    main, up, down = call(columns_kernel, [(FIELDS, 2) + tile] + [(ZTILES,) + tile] * 2)(g, seed, own_b, below, above)
    before, beyond = both_ways(up, down, "gz")
    g_turned, seed_turned = call(turn_kernel, [(Q, 2) + tile, (Q,) + tile])(main)
    f1, edge, b, up, down = call(
        first_kernel,
        [(Q,) + half, (Q, 2) + tile, half] + [(STRIPS1[-1] + ROWS, LANES)] * 2,
        [(3,) + half, (Q, 2) + tile, (Q, 2) + tile, (2 * ZTILES,) + tile],
    )(main, g_turned, seed_turned, before, beyond)
    left1, right1 = both_ways(up, down, "gx")
    (b2,) = call(seed_kernel, [(Q,) + half], [(Q, 2) + tile, (2 * ZTILES,) + tile])(main, before, beyond)
    sides = []
    for side, got in enumerate((left1, right1)):
        sides.append(
            call(
                functools.partial(side_kernel, side),
                [(4, 2) + tile, (3, 2) + tile, (2,) + tile, (Q, 2) + tile, (Q, 2) + tile],
                [(SEND1, 8, LANES), (SEND1,) + tile],
            )(f1, edge, b, got)
        )
    (mom0, far0, bh0, g0, g_left), (mom1, far1, bh1, g1, g_right) = sides
    grad, b1, edge1, sums, up, down = call(
        middle_kernel,
        [(2, OWN, LANES), (Q,) + half, (Q, 2) + tile, (4,) + half] + [(ROWTILES2 + 3, 8, LANES)] * 2,
        [(SEND1, 8, LANES), (SEND1,) + tile] * 2 + [(Q,) + half, (Q,) + half, (1,) + tile],
    )(b, b2, left1, right1, mom0, mom1, g0, g1, g_left, g_right)
    left, right = both_ways(up, down, "gx")
    sides = []
    for side, (mom, far, bh, got1, got) in enumerate(((mom0, far0, bh0, left1, left), (mom1, far1, bh1, right1, right))):
        sides.append(
            call(
                functools.partial(side_back_kernel, side),
                [(OWN, LANES), (Q, 2) + tile, (Q, 2) + tile],
                [(SEND2, 2) + tile],
            )(b1, edge1, sums, mom, far, b, bh, f1, got1, grad, got)
        )
    (grad0, a0, a_left), (grad1, a1, a_right) = sides
    gradient, adjoint_out = call(last_kernel, [(2, OWN, LANES), (Q, 2, OWN, LANES)], [(Q, 2, OWN, LANES)])(
        b, grad0, grad1, a_left, a0, a1, a_right, f, fluid
    )
    return gradient, adjoint_out


def solution(mesh):
    field, cell = P(None, "gx", "gy", "gz"), P("gx", "gy", "gz")
    return jax.shard_map(
        body, mesh=mesh, in_specs=(field, cell, cell, field), out_specs=(cell, field), check_vma=False
    )
```

```python
import functools

import jax
import jax.numpy as jnp
from jax import lax
from jax.experimental import pallas as pl
from jax.experimental.pallas import tpu as pltpu
from jax.sharding import PartitionSpec as P

INTERPRET = False

VEL = [
    (0, 0, 0),
    (1, 0, 0), (-1, 0, 0), (0, 1, 0), (0, -1, 0), (0, 0, 1), (0, 0, -1),
    (1, 1, 0), (-1, -1, 0), (1, -1, 0), (-1, 1, 0),
    (1, 0, 1), (-1, 0, -1), (1, 0, -1), (-1, 0, 1),
    (0, 1, 1), (0, -1, -1), (0, 1, -1), (0, -1, 1),
]
OPP = [0, 2, 1, 4, 3, 6, 5, 8, 7, 10, 9, 12, 11, 14, 13, 16, 15, 18, 17]
WEIGHT = [1.0 / 3.0] + [1.0 / 18.0] * 6 + [1.0 / 36.0] * 12
OMEGA = 1.25
Q = 19
XP = [i for i in range(Q) if VEL[i][0] == 1]
X0 = [i for i in range(Q) if VEL[i][0] == 0]
XM = [i for i in range(Q) if VEL[i][0] == -1]
PAIRS = [i for i in range(1, Q, 2)]

ROWS, OWN, LANES, RIM = 24, 16, 128, 4
FIELDS = 2 * Q + 1
ZTILES = -(-2 * FIELDS // 32)


def total(terms):
    terms = list(terms)
    while len(terms) > 1:
        terms = [a + b for a, b in zip(terms[::2], terms[1::2])] + (terms[-1:] if len(terms) % 2 else [])
    return terms[0]


ROOT = 4.5**0.5
FACES = [i for i in PAIRS if i < 7]
EDGES = [i for i in PAIRS if i >= 7]


def project(vector, i):
    out = None
    for axis in range(3):
        c = VEL[i][axis]
        if c == 0:
            continue
        if out is None:
            out = vector[axis] if c == 1 else -vector[axis]
        else:
            out = out + vector[axis] if c == 1 else out - vector[axis]
    return out


def gathered(terms, axis):
    plus = [terms[i] for i in terms if VEL[i][axis] == 1]
    minus = [terms[i] for i in terms if VEL[i][axis] == -1]
    return total(plus) - total(minus) if minus else total(plus)


def split(f, pairs=PAIRS):
    return {i: f[i] + f[i + 1] for i in pairs}, {i: f[i] - f[i + 1] for i in pairs}


def moments(f0, even, odd):
    rho = f0 + total(even.values())
    inv = 1.0 / rho
    return rho, [gathered(odd, axis) * inv for axis in range(3)]


def moments_from(level, even, odd):
    rho = level[0] + total(even.values())
    inv = 1.0 / rho
    return rho, [gathered(odd, 0) * inv] + [(level[axis] + gathered(odd, axis)) * inv for axis in (1, 2)]


def weights(blocking):
    keep = 1.0 - blocking
    own = (1.0 - OMEGA) * keep
    return 0.5 * (own + blocking), 0.5 * (own - blocking), OMEGA * keep


def collide(f0, even, odd, rho, u, blocking, want):
    k_even, k_odd, mix = weights(blocking)
    scale = mix * rho
    v = [ROOT * part for part in u]
    squares = [part * part for part in v]
    base = 1.0 - (1.0 / 3.0) * (squares[0] + squares[1] + squares[2])
    out = {}
    if 0 in want:
        out[0] = (2.0 * k_even) * f0 + (WEIGHT[0] * scale) * base
    for group in (FACES, EDGES):
        s = WEIGHT[group[0]] * scale
        s_odd = (2.0**0.5) * s
        for i in group:
            if i not in want and i + 1 not in want:
                continue
            p = project(v, i)
            square = squares[VEL[i].index(1)] if i in FACES else p * p
            p_even = k_even * even[i] + s * (base + square)
            p_odd = k_odd * odd[i] + s_odd * p
            if i in want:
                out[i] = p_even + p_odd
            if i + 1 in want:
                out[i + 1] = p_even - p_odd
    return out


def flow(b0, even, odd, u):
    base = 1.0 - 1.5 * (u[0] * u[0] + u[1] * u[1] + u[2] * u[2])
    q = [1.5 * part for part in u]
    level = [] if b0 is None else [WEIGHT[0] * b0]
    value, slope = [], [[], [], []]
    for group in (FACES, EDGES):
        group = [i for i in group if i in even]
        w = WEIGHT[group[0]]
        level.append(w * total(even[i] for i in group))
        work, along = [], {}
        for i in group:
            p = project(q, i)
            t = p * even[i]
            h = odd[i] + t
            work.append(p * h)
            along[i] = h + t
        value.append((2.0 * w) * total(work))
        for axis in range(3):
            if any(VEL[i][axis] for i in group):
                slope[axis].append((3.0 * w) * gathered(along, axis))
    level = total(level)
    return [base * level + total(value)] + [total(slope[axis]) - 2.0 * (q[axis] * level) for axis in range(3)]


def back(b0, even, odd, sums, u, blocking, want):
    energy, *v = sums
    k_even, k_odd, mix = weights(blocking)
    common = mix * (energy - (v[0] * u[0] + v[1] * u[1] + v[2] * u[2]))
    mv = [mix * v[axis] for axis in range(3)]
    out = {}
    if 0 in want:
        out[0] = (2.0 * k_even) * b0 + common
    for i in PAIRS:
        if i not in want and i + 1 not in want:
            continue
        p_even = k_even * even[i] + common
        p_odd = k_odd * odd[i] + project(mv, i)
        if i in want:
            out[i] = p_even + p_odd
        if i + 1 in want:
            out[i + 1] = p_even - p_odd
    return out


def gradient_of(b, f, rho, energy):
    evens = total(b[1][i] * f[1][i] for i in PAIRS)
    odds = total(b[2][i] * f[2][i] for i in PAIRS)
    return OMEGA * (b[0] * f[0] - rho * energy) + (0.5 * OMEGA) * evens - (1.0 - 0.5 * OMEGA) * odds


def column(shape):
    return lax.broadcasted_iota(jnp.int32, shape, len(shape) - 1)


def turn(tile, shift, axis):
    shift = shift % tile.shape[axis]
    return tile if shift == 0 else pltpu.roll(tile, shift, axis)


def moved(main, rim, i, sign):
    y, z = sign * VEL[i][1], sign * VEL[i][2]
    if y:
        main, rim = turn(main, y, 0), turn(rim, y, 0)
    if z:
        at = column(main.shape)
        edge = at == (0 if z == 1 else LANES - 1)
        main, rim = turn(main, z, 1), turn(rim, z, 1)
        main, rim = jnp.where(edge, rim, main), jnp.where(edge, main, rim)
    return main, rim


def packed_rims(tiles, width):
    at = column((ROWS, LANES))
    joined, first = None, 0
    for k, (_, rim) in enumerate(tiles):
        piece = turn(rim(), first + width[k] // 2, 1)
        joined = piece if joined is None else jnp.where(at >= first, piece, joined)
        first += width[k]
    return joined


def unpack_rims(tile, width, out):
    first = 0
    for k in range(len(width)):
        out(k, turn(tile, -(first + width[k] // 2), 1))
        first += width[k]


SEND1, SEND2 = 19, 14
WIDTH1 = [6] * 14 + [4] * 5
WIDTH2 = [2] * SEND2
ROWTILES2 = 2 * SEND2 + -(-SEND2 // 4)


STRIPS1 = [sum(WIDTH1[:k]) + OWN * SEND1 for k in range(SEND1 + 1)]


def pack1(ref, tiles):
    for k, (main, _) in enumerate(tiles):
        tile, half, at = main(), WIDTH1[k] // 2, STRIPS1[k]
        ref[OWN * k : OWN * k + OWN, :] = tile[0:OWN]
        ref[at : at + half, :] = tile[ROWS - half : ROWS]
        ref[at + half : at + 2 * half, :] = tile[OWN : OWN + half]
    ref[STRIPS1[-1] : STRIPS1[-1] + ROWS, :] = packed_rims(tiles, WIDTH1)


def unpack1(ref, beyond_ref, rim_ref, first=0):
    for k in range(first, SEND1):
        half, at = WIDTH1[k] // 2, STRIPS1[k]
        beyond_ref[k, 8 - half : 8, :] = ref[at : at + half, :]
        beyond_ref[k, 0:half, :] = ref[at + half : at + 2 * half, :]

    def out(k, rim):
        if k >= first:
            rim_ref[k] = rim

    unpack_rims(ref[STRIPS1[-1] : STRIPS1[-1] + ROWS, :], WIDTH1, out)

    def tile(k, lane, row):
        if lane:
            return rim_ref[k, row : row + 8, :]
        return ref[OWN * k + row : OWN * k + row + 8, :] if row < OWN else beyond_ref[k]

    return tile


def pack2(ref, rim_ref, tiles):
    at = lax.broadcasted_iota(jnp.int32, (8, LANES), 0)
    joined = None
    for k, (main, _) in enumerate(tiles):
        tile = main()
        ref[2 * k], ref[2 * k + 1] = tile[0:8], tile[8:16]
        slot = 2 * (k % 4)
        piece = turn(tile[16:24], slot + 1, 0)
        joined = piece if slot == 0 else jnp.where(at >= slot, piece, joined)
        if slot == 6 or k == SEND2 - 1:
            ref[2 * SEND2 + k // 4] = joined
    rim_ref[0] = packed_rims(tiles, WIDTH2)
    for k in range(3):
        ref[ROWTILES2 + k] = rim_ref[0, 8 * k : 8 * k + 8, :]


def unpack2(ref, out_ref):
    for k in range(SEND2):
        out_ref[k, 0, 0:8, :] = ref[2 * k]
        out_ref[k, 0, 8:16, :] = ref[2 * k + 1]
        out_ref[k, 0, 16:24, :] = turn(ref[2 * SEND2 + k // 4], -(2 * (k % 4) + 1), 0)

    def out(k, rim):
        out_ref[k, 1] = rim

    unpack_rims(jnp.concatenate([ref[ROWTILES2 + k] for k in range(3)], axis=0), WIDTH2, out)


def call(kernel, outs, scratch=(), more=(), space=None, cost=1000):
    specs = {} if space is None else {"in_specs": [pl.BlockSpec(memory_space=s) for s in space]}
    return pl.pallas_call(
        kernel,
        out_shape=[jax.ShapeDtypeStruct(shape, jnp.float32) for shape in outs],
        scratch_shapes=[pltpu.VMEM(shape, jnp.float32) for shape in scratch] + list(more),
        compiler_params=None if INTERPRET else pltpu.CompilerParams(vmem_limit_bytes=40 * 2**20),
        cost_estimate=pl.CostEstimate(flops=cost * 2000, bytes_accessed=cost * 1000, transcendentals=0),
        interpret=INTERPRET,
        **specs,
    )


LEVEL_Y = [i for i in range(Q) if VEL[i][1] == 0]
YTILES = Q + 8


def rows_moves(up):
    inwards = 1 if up else -1
    first = lambda count: OWN - count if up else 0
    fourth, third = (OWN - 4, OWN - 3) if up else (3, 2)
    out = []
    for i in range(Q):
        for layer in range(2):
            out.append((0, i, layer, first(3), 3, i, 3 * layer))
            if i < 16:
                out.append((1, i, layer, first(2), 2, Q + i // 2, 4 * (i % 2) + 2 * layer))
            else:
                out.append((1, i, layer, first(2), 2, LEVEL_Y[3 + 2 * (i - 16) + layer], 6))
            if VEL[i][1] == inwards:
                out.append((0, i, layer, fourth, 1, i, 6 + layer))
            elif VEL[i][1] == -inwards:
                out.append((1, i, layer, third, 1, i, 6 + layer))
            elif i in LEVEL_Y[:3]:
                out.append((2, 0, layer, first(3) + LEVEL_Y.index(i), 1, i, 6 + layer))
    return out


def collided(f, blocking):
    even, odd = split(f)
    rho, u = moments(f[0], even, odd)
    return collide(f[0], even, odd, rho, u, blocking, range(Q))


def rows_kernel(
    f_hbm, por_hbm, solid_hbm, seed_hbm,
    up_ref, down_ref, f_ref, seed_ref, g_ref, b_ref, fluid_ref,
    por_ref, solid_ref, sems,
):
    copies = [
        pltpu.make_async_copy(src, dst, sems.at[k])
        for k, (src, dst) in enumerate(
            [(f_hbm, f_ref), (por_hbm, por_ref), (solid_hbm, solid_ref), (seed_hbm, seed_ref)]
        )
    ]
    for copy in copies:
        copy.start()
    for copy in copies[:3]:
        copy.wait()
    for layer in range(2):
        solid = solid_ref[layer] == 1
        b_ref[0, layer] = jnp.where(solid, 1.0, por_ref[layer])
        fluid_ref[layer] = jnp.where(solid, 0.0, 1.0)

        def body(row, layer=layer):
            rows = slice(row, row + 8)
            g = collided([f_ref[i, layer, rows, :] for i in range(Q)], b_ref[0, layer, rows, :])
            for i in range(Q):
                g_ref[i, layer, rows, :] = g[i]

        tiles_loop(2, body)
    copies[3].wait()
    arrays = (g_ref, seed_ref, b_ref)
    for ref, up in ((up_ref, True), (down_ref, False)):
        for which, i, layer, row, count, tile, at in rows_moves(up):
            ref[tile, at : at + count, :] = arrays[which][i, layer, row : row + count, :]


def columns_kernel(g_ref, seed_ref, b_ref, below_ref, above_ref, main_ref, up_ref, down_ref):
    for k in range(FIELDS):
        for layer in range(2):
            own = g_ref[k, layer] if k < Q else seed_ref[k - Q, layer] if k < 2 * Q else b_ref[0, layer]
            main_ref[k, layer, 0:OWN, :] = own
    for ref, up, shift in ((below_ref, True, ROWS - OWN), (above_ref, False, OWN)):
        for which, i, layer, row, count, tile, at in rows_moves(up):
            main_ref[which * Q + i, layer, row + shift : row + shift + count, :] = ref[tile, at : at + count, :]
    at = column((ROWS, LANES))
    high = low = None
    for k in range(FIELDS):
        for layer in range(2):
            tile = main_ref[k, layer]
            n = 2 * k + layer
            slot = n % 32
            piece = turn(tile, 4 * slot + 4, 1)
            high = piece if slot == 0 else jnp.where(at >= 4 * slot, piece, high)
            low = piece if slot == 0 else jnp.where((at >= 4 * slot + 4) if slot < 31 else (at < 4), piece, low)
            if slot == 31 or n == 2 * FIELDS - 1:
                up_ref[n // 32] = high
                down_ref[n // 32] = low


def tiles_loop(count, body):
    for n in range(count):
        body(8 * n)


def joined_columns(before_ref, beyond_ref, out_ref):
    odd = (column((ROWS, LANES)) // 4) % 2
    for tile in range(ZTILES):
        for part in range(2):
            out_ref[2 * tile + part] = jnp.where(odd == part, before_ref[tile], beyond_ref[tile])


def rim_of(columns_ref, k, layer):
    slot = (2 * k + layer) % 32
    return turn(columns_ref[2 * ((2 * k + layer) // 32) + slot % 2], -(4 * slot + 4), 1)


def turned(tile, i, sign):
    return turn(turn(tile, sign * VEL[i][1], 0), sign * VEL[i][2], 1)


def edged(main, rim, i, sign):
    z = sign * VEL[i][2]
    if z == 0:
        return main, rim
    edge = column(main.shape) == (0 if z == 1 else LANES - 1)
    return jnp.where(edge, rim, main), jnp.where(edge, main, rim)


def turn_kernel(main_ref, g_ref, seed_ref):
    for i in range(Q):
        for layer in range(2):
            g_ref[i, layer] = turned(main_ref[i, layer], i, 1)
    for layer, pops in ((1, XM), (0, XP)):
        for i in pops:
            seed_ref[i] = turned(main_ref[Q + i, layer], i, -1)


def first_kernel(
    main_ref, g_ref, turned_seed_ref, before_ref, beyond_ref,
    f1_ref, edge_ref, b_ref, up_ref, down_ref,
    level_ref, rim_ref, seed_ref, columns_ref,
):
    joined_columns(before_ref, beyond_ref, columns_ref)
    for i in range(Q):
        for layer in range(2):
            rim_ref[i, layer] = rim_of(columns_ref, i, layer)
    for layer, pops in ((1, XM), (0, XP)):
        for i in pops:
            seed_ref[i, 0] = rim_of(columns_ref, Q + i, layer)
    for layer in range(2):
        b_ref[layer, 0] = main_ref[2 * Q, layer]
        b_ref[layer, 1] = rim_of(columns_ref, 2 * Q, layer)
    for i in range(Q):
        for layer in range(2):
            to = layer + VEL[i][0]
            tiles = edged(g_ref[i, layer], turned(rim_ref[i, layer], i, 1), i, 1)
            for lane in range(2):
                if to in (0, 1):
                    f1_ref[i, to, lane] = tiles[lane]
                else:
                    edge_ref[i, lane] = tiles[lane]
    for layer in range(2):
        for lane in range(2):
            stay = {i: f1_ref[i, layer, lane] for i in X0}
            level_ref[0, layer, lane] = total(stay.values())
            for axis in (1, 2):
                level_ref[axis, layer, lane] = total(
                    stay[i] if VEL[i][axis] == 1 else -stay[i] for i in X0 if VEL[i][axis]
                )

    def tiles_of(forward, backward, layer):
        def pick(ref, *where):
            return (lambda: ref[where + (0,)]), (lambda: ref[where + (1,)])

        out = [pick(f1_ref, i, layer) for i in forward]
        out += [pick(level_ref, k, layer) for k in range(3)]
        out.append(pick(b_ref, layer))
        out += [pick(edge_ref, i) for i in forward]
        for i in backward:
            seed_ref[i, 0], seed_ref[i, 1] = edged(turned_seed_ref[i], turned(seed_ref[i, 0], i, -1), i, -1)
            out.append(pick(seed_ref, i))
        return out

    pack1(up_ref, tiles_of(XP, XM, 1))
    pack1(down_ref, tiles_of(XM, XP, 0))


def seed_kernel(main_ref, before_ref, beyond_ref, b2_ref, rim_ref, columns_ref):
    joined_columns(before_ref, beyond_ref, columns_ref)
    for i in range(Q):
        for layer in range(2):
            if layer - VEL[i][0] in (0, 1):
                rim_ref[i, layer] = rim_of(columns_ref, Q + i, layer)
    for i in range(Q):
        for layer in range(2):
            to = layer - VEL[i][0]
            if to in (0, 1):
                main, rim = moved(main_ref[Q + i, layer], rim_ref[i, layer], i, -1)
                b2_ref[i, to, 0] = main
                b2_ref[i, to, 1] = rim


def side_kernel(side, f1_ref, edge_ref, b_ref, got_ref, mom_ref, far_ref, bh_ref, g_ref, far_g_ref, beyond_scr, rim_scr):
    got = unpack1(got_ref, beyond_scr, rim_scr)
    theirs, ours = (XP, XM) if side == 0 else (XM, XP)
    for lane in range(2):
        def near(row, lane=lane):
            rows = slice(row, row + 8)
            f = [None if i in theirs else f1_ref[i, side, lane, rows, :] for i in range(Q)]
            for k, i in enumerate(theirs):
                f[i] = got(9 + k, lane, row)
            even, odd = split(f)
            rho, u = moments(f[0], even, odd)
            mom_ref[3, lane, rows, :] = rho
            for axis in range(3):
                mom_ref[axis, lane, rows, :] = u[axis]
            g = collide(f[0], even, odd, rho, u, b_ref[side, lane, rows, :], range(Q))
            for i in range(Q):
                g_ref[i, lane, rows, :] = g[i]

        def far(row, lane=lane):
            rows = slice(row, row + 8)
            f = [None] * Q
            for k, i in enumerate(theirs):
                f[i] = got(k, lane, row)
            for i in ours:
                f[i] = edge_ref[i, lane, rows, :]
            even, odd = split(f, XP)
            rho, u = moments_from([got(5 + k, lane, row) for k in range(3)], even, odd)
            for axis in range(3):
                far_ref[axis, lane, rows, :] = u[axis]
            blocking = got(8, lane, row)
            bh_ref[lane, rows, :] = blocking
            g = collide(None, even, odd, rho, u, blocking, theirs)
            for i in theirs:
                far_g_ref[i, lane, rows, :] = g[i]

        tiles_loop(3, near)
        tiles_loop(3, far)


def middle_kernel(
    b_ref, b2_ref, left_ref, right_ref, mom0_ref, mom1_ref, g0_ref, g1_ref, g_left_ref, g_right_ref,
    grad_ref, b1_ref, edge1_ref, sums_ref, up_ref, down_ref,
    l_beyond, l_scr, r_beyond, r_scr, f_scr, a_scr, rim_scr,
):
    got = (unpack1(left_ref, l_beyond, l_scr, 14), unpack1(right_ref, r_beyond, r_scr, 14))
    g_refs = (g_left_ref, g0_ref, g1_ref, g_right_ref)
    mom = (mom0_ref, mom1_ref)

    for i in range(Q):
        for layer in range(2):
            ref = g_refs[layer + 1 - VEL[i][0]]
            main, rim = moved(ref[i, 0], ref[i, 1], i, 1)
            f_scr[i, layer, 0] = main
            f_scr[i, layer, 1] = rim

    for layer in range(2):
        for lane in range(2):

            def body(row, layer=layer, lane=lane):
                rows = slice(row, row + 8)
                missing = XM if layer == 0 else XP
                f = [f_scr[i, layer, lane, rows, :] for i in range(Q)]
                b = {i: b2_ref[i, layer, lane, rows, :] for i in range(Q) if i not in missing}
                for k, i in enumerate(missing):
                    b[i] = got[layer](14 + k, lane, row)
                even, odd = split(f)
                rho, u = moments(f[0], even, odd)
                b_even, b_odd = split(b)
                sums = flow(b[0], b_even, b_odd, u)
                a = back(b[0], b_even, b_odd, sums, u, b_ref[layer, lane, rows, :], range(Q))
                for i in range(Q):
                    a_scr[i, layer, lane, rows, :] = a[i]
                if lane == 0 and row < OWN:
                    grad_ref[layer, rows, :] = gradient_of((b[0], b_even, b_odd), (f[0], even, odd), rho, sums[0])

            tiles_loop(3, body)

    for i in range(Q):
        for layer in range(2):
            to = layer - VEL[i][0]
            tiles = moved(a_scr[i, layer, 0], a_scr[i, layer, 1], i, -1)
            for lane in range(2):
                if to in (0, 1):
                    b1_ref[i, to, lane] = tiles[lane]
                else:
                    edge1_ref[i, lane] = tiles[lane]

    for layer in range(2):
        for lane in range(2):

            def body(row, layer=layer, lane=lane):
                rows = slice(row, row + 8)
                missing = XM if layer == 0 else XP
                b = {i: b1_ref[i, layer, lane, rows, :] for i in range(Q) if i not in missing}
                even, odd = split(b, [i for i in PAIRS if i in X0])
                for i in XP:
                    even[i], odd[i] = (b[i], b[i]) if layer == 0 else (b[i + 1], -b[i + 1])
                sums = flow(b[0], even, odd, [mom[layer][axis, lane, rows, :] for axis in range(3)])
                for k in range(4):
                    sums_ref[k, layer, lane, rows, :] = sums[k]

            tiles_loop(3, body)

    def tiles_of(theirs, layer):
        def pick(ref, *where):
            return (lambda: ref[where + (0,)]), (lambda: ref[where + (1,)])

        return (
            [pick(edge1_ref, i) for i in theirs]
            + [pick(b1_ref, i, layer) for i in theirs]
            + [pick(sums_ref, k, layer) for k in range(4)]
        )

    pack2(up_ref, rim_scr, tiles_of(XM, 1))
    pack2(down_ref, rim_scr, tiles_of(XP, 0))


def side_back_kernel(
    side, b1_ref, edge1_ref, sums_ref, mom_ref, far_ref, b_ref, bh_ref, f1_ref, got1_ref, grad_ref, got_ref,
    out_grad_ref, a_ref, far_a_ref,
    got,
):
    unpack2(got_ref, got)
    near_pops, far_pops = (XM, XP) if side == 0 else (XP, XM)

    def halves(b, plus):
        return {i: b[i] if plus else b[i + 1] for i in XP}, {i: b[i] if plus else -b[i + 1] for i in XP}

    for lane in range(2):

        def near(row, lane=lane):
            rows = slice(row, row + 8)
            b = {i: b1_ref[i, side, lane, rows, :] for i in range(Q) if i not in near_pops}
            for k, i in enumerate(near_pops):
                b[i] = got[k, lane, rows, :]
            even, odd = split(b)
            u = [mom_ref[axis, lane, rows, :] for axis in range(3)]
            parts = flow(None, *halves(b, side == 1), u)
            sums = [sums_ref[k, side, lane, rows, :] + part for k, part in enumerate(parts)]
            a = back(b[0], even, odd, sums, u, b_ref[side, lane, rows, :], range(Q))
            for i in range(Q):
                a_ref[i, lane, rows, :] = a[i]
            if lane == 0 and row < OWN:
                f = {i: f1_ref[i, side, lane, rows, :] for i in range(Q) if i not in far_pops}
                for k, i in enumerate(far_pops):
                    f[i] = got1_ref[OWN * (9 + k) + row : OWN * (9 + k) + row + 8, :]
                grad = gradient_of((b[0], even, odd), (f[0],) + split(f), mom_ref[3, lane, rows, :], sums[0])
                out_grad_ref[rows, :] = grad + grad_ref[side, rows, :]

        def far(row, lane=lane):
            rows = slice(row, row + 8)
            b = {i: edge1_ref[i, lane, rows, :] for i in far_pops}
            for k, i in enumerate(near_pops):
                b[i] = got[5 + k, lane, rows, :]
            even, odd = split(b, XP)
            u = [far_ref[axis, lane, rows, :] for axis in range(3)]
            parts = flow(None, *halves(b, side == 0), u)
            sums = [got[10 + k, lane, rows, :] + part for k, part in enumerate(parts)]
            a = back(None, even, odd, sums, u, bh_ref[lane, rows, :], near_pops)
            for i in near_pops:
                far_a_ref[i, lane, rows, :] = a[i]

        tiles_loop(3, near)
        tiles_loop(3, far)


def last_kernel(
    b_ref, grad0_ref, grad1_ref, a_left_ref, a0_ref, a1_ref, a_right_ref, f_ref, fluid_ref,
    out_grad_ref, out_ref,
    b_scr,
):
    a_refs = (a_left_ref, a0_ref, a1_ref, a_right_ref)
    grads = (grad0_ref, grad1_ref)
    for i in range(Q):
        for layer in range(2):
            ref = a_refs[layer + 1 + VEL[i][0]]
            main, _ = moved(ref[i, 0], ref[i, 1], i, -1)
            b_scr[i, layer] = main[0:OWN]

    for layer in range(2):

        def body(row, layer=layer):
            rows = slice(row, row + 8)
            f = [f_ref[i, layer, rows, :] for i in range(Q)]
            b = {i: b_scr[i, layer, rows, :] for i in range(Q)}
            even, odd = split(f)
            rho, u = moments(f[0], even, odd)
            b_even, b_odd = split(b)
            sums = flow(b[0], b_even, b_odd, u)
            a = back(b[0], b_even, b_odd, sums, u, b_ref[layer, 0, rows, :], range(Q))
            for i in range(Q):
                out_ref[i, layer, rows, :] = a[i]
            grad = gradient_of((b[0], b_even, b_odd), (f[0], even, odd), rho, sums[0]) + grads[layer][rows, :]
            out_grad_ref[layer, rows, :] = jnp.where(fluid_ref[layer, rows, :] == 0.0, 0.0, grad)

        tiles_loop(2, body)


def left_middle_kernel(
    f1_ref, edge_ref, b_ref, b2_ref, left_ref, right_ref, mom1_ref, g1_ref, g_right_ref,
    mom0_ref, far0_ref, bh0_ref, grad_ref, b1_ref, edge1_ref, sums_ref, up_ref, down_ref,
    g0_ref, g_left_ref, l_beyond, l_scr, r_beyond, r_scr, f_scr, a_scr, rim_scr,
):
    side_kernel(0, f1_ref, edge_ref, b_ref, left_ref, mom0_ref, far0_ref, bh0_ref, g0_ref, g_left_ref, l_beyond, l_scr)
    middle_kernel(
        b_ref, b2_ref, left_ref, right_ref, mom0_ref, mom1_ref, g0_ref, g1_ref, g_left_ref, g_right_ref,
        grad_ref, b1_ref, edge1_ref, sums_ref, up_ref, down_ref,
        l_beyond, l_scr, r_beyond, r_scr, f_scr, a_scr, rim_scr,
    )


def left_last_kernel(
    b1_ref, edge1_ref, sums_ref, mom_ref, far_ref, b_ref, bh_ref, f1_ref, got1_ref, grad_ref, got_ref,
    grad1_ref, a1_ref, a_right_ref, f_ref, fluid_ref,
    out_grad_ref, out_ref,
    grad0_ref, a0_ref, a_left_ref, got, b_scr,
):
    side_back_kernel(
        0, b1_ref, edge1_ref, sums_ref, mom_ref, far_ref, b_ref, bh_ref, f1_ref, got1_ref, grad_ref, got_ref,
        grad0_ref, a0_ref, a_left_ref, got,
    )
    last_kernel(b_ref, grad0_ref, grad1_ref, a_left_ref, a0_ref, a1_ref, a_right_ref, f_ref, fluid_ref, out_grad_ref, out_ref, b_scr)


def placed(x):
    return x if INTERPRET else pltpu.with_memory_space_constraint(x, pltpu.HBM)


def both_ways(up, down, axis):
    count = lax.axis_size(axis)
    ring = [(i, (i + 1) % count) for i in range(count)]
    return lax.ppermute(up, axis, ring), lax.ppermute(down, axis, [(j, i) for i, j in ring])


def body(populations, porosity, solid, seed_adjoint):
    half, tile = (2, 2, ROWS, LANES), (ROWS, LANES)
    inputs = [placed(x) for x in (populations, porosity, solid, seed_adjoint)]
    block = populations.shape
    cells = block[1:]
    up, down, f, seed, g, own_b, fluid = call(
        rows_kernel,
        [(YTILES, 8, LANES)] * 2 + [block, block, block, (1,) + cells, cells],
        [cells],
        [pltpu.VMEM(cells, jnp.int32), pltpu.SemaphoreType.DMA((4,))],
        space=[pltpu.HBM] * 4,
    )(*inputs)
    below, above = both_ways(up, down, "gy")
    main, up, down = call(columns_kernel, [(FIELDS, 2) + tile] + [(ZTILES,) + tile] * 2)(g, seed, own_b, below, above)
    before, beyond = both_ways(up, down, "gz")
    g_turned, seed_turned = call(turn_kernel, [(Q, 2) + tile, (Q,) + tile])(main)
    f1, edge, b, up, down = call(
        first_kernel,
        [(Q,) + half, (Q, 2) + tile, half] + [(STRIPS1[-1] + ROWS, LANES)] * 2,
        [(3,) + half, (Q, 2) + tile, (Q, 2) + tile, (2 * ZTILES,) + tile],
    )(main, g_turned, seed_turned, before, beyond)
    left1, right1 = both_ways(up, down, "gx")
    (b2,) = call(seed_kernel, [(Q,) + half], [(Q, 2) + tile, (2 * ZTILES,) + tile])(main, before, beyond)
    field = (Q, 2) + tile
    moments_out = [(4, 2) + tile, (3, 2) + tile, (2,) + tile]
    mom1, far1, bh1, g1, g_right = call(
        functools.partial(side_kernel, 1), moments_out + [field, field], [(SEND1, 8, LANES), (SEND1,) + tile]
    )(f1, edge, b, right1)
    mom0, far0, bh0, grad, b1, edge1, sums, up, down = call(
        left_middle_kernel,
        moments_out + [(2, OWN, LANES), (Q,) + half, field, (4,) + half] + [(ROWTILES2 + 3, 8, LANES)] * 2,
        [field, field] + [(SEND1, 8, LANES), (SEND1,) + tile] * 2 + [(Q,) + half, (Q,) + half, (1,) + tile],
    )(f1, edge, b, b2, left1, right1, mom1, g1, g_right)
    left, right = both_ways(up, down, "gx")
    grad1, a1, a_right = call(
        functools.partial(side_back_kernel, 1), [(OWN, LANES), field, field], [(SEND2, 2) + tile]
    )(b1, edge1, sums, mom1, far1, b, bh1, f1, right1, grad, right)
    gradient, adjoint_out = call(
        left_last_kernel,
        [cells, block],
        [(OWN, LANES), field, field, (SEND2, 2) + tile, block],
    )(b1, edge1, sums, mom0, far0, b, bh0, f1, left1, grad, left, grad1, a1, a_right, f, fluid)
    return gradient, adjoint_out


def solution(mesh):
    field, cell = P(None, "gx", "gy", "gz"), P("gx", "gy", "gz")
    return jax.shard_map(
        body, mesh=mesh, in_specs=(field, cell, cell, field), out_specs=(cell, field), check_vma=False
    )
```
